256 devices in a mesh: rows: 8 (over z), cols: 32 (over y, x, core).
Axes of the slice: x: 4, y: 4, z: 8, core: 2. Of those that a mesh axis runs over, the one named last changes fastest.
Arguments:
- guidance: float32 [2, 3, 512, 4096], P(None, None, 'rows', 'cols'), may hold values from -6 to 6
- seam_weight: int32 [512, 4096], P('rows', 'cols'), may hold values from 1 to 64
- source_label: int32 [512, 4096], P('rows', 'cols'), may hold values from 0 to 3
Outputs:
- solution: float32 [3, 512, 4096], P(None, 'rows', 'cols')
- residual: float32 [3, 512, 4096], P(None, 'rows', 'cols')
The draws below stay inside these ranges and needn't reach their ends.
All inputs are finite; a program needn't handle non-finite values.
Results may differ from the reference program's by a relative error of at most 0.0003.
Values sent between devices are 32-bit elements; how exact they have to be, the bound alone decides.
No kernel may reach another device: no remote copies, remote signals or barrier semaphores. Data moves between devices by JAX's collectives and lax.ppermute only.
A program may use at most 192 MiB of HBM per device.

```python
import math
import jax
import jax.numpy as jnp
from jax import lax

CHANNELS = 3
LABELS = 4
LEVELS = 7
SWEEPS = 2
COARSE_SWEEPS = 48
CYCLES = 2
NX = 512
NY = 4096


def draw_guidance(key, part):
    key = jax.random.fold_in(key, 7)
    rows_index = lax.broadcasted_iota(jnp.float32, (NX, NY), 0)
    cols_index = lax.broadcasted_iota(jnp.float32, (NX, NY), 1)
    height = float(NX)
    breadth = float(NY)
    amp_first = 0.5 * height
    amp_second = breadth / 32.0
    step_rows = -2.0 * amp_first * jnp.sin(math.pi * (rows_index + 0.5) / height) * math.sin(math.pi / (2.0 * height)) * jnp.cos(2.0 * math.pi * cols_index / breadth)
    step_cols = -2.0 * amp_first * jnp.cos(math.pi * rows_index / height) * jnp.sin(2.0 * math.pi * (cols_index + 0.5) / breadth) * math.sin(math.pi / breadth)
    step_cols = step_cols + 2.0 * amp_second * jnp.cos(6.0 * math.pi * (cols_index + 0.5) / breadth) * math.sin(3.0 * math.pi / breadth)
    smooth = jnp.stack([step_rows, step_cols])[:, None, :, :]
    channel_gain = 1.0 - 0.2 * jnp.arange(CHANNELS).astype(jnp.float32)
    smooth = smooth * channel_gain[None, :, None, None]
    shape = (2, CHANNELS, NX, NY)
    noise = jax.random.normal(key, shape, jnp.float32)
    return jnp.clip(smooth + noise, -6.0, 6.0)


def with_ends(result, key, least, high):
    longest = result.shape.index(max(result.shape))
    spots = []
    for shift in (0, 1):
        where = [jax.random.randint(jax.random.fold_in(key, axis), (), 0, length) for axis, length in enumerate(result.shape)]
        where[longest] = (where[longest] + shift) % result.shape[longest]
        spots.append(tuple(where))
    return result.at[spots[0]].set(least).at[spots[1]].set(high)


def setup_inputs(seed: int = 0) -> dict:
    key_of = jax.random.split(jax.random.key(seed), 4)
    guidance = draw_guidance(jax.random.fold_in(key_of[3], 71), 0)
    seam_weight = with_ends(jax.random.randint(key_of[1], (NX, NY), 1, 65), jax.random.fold_in(key_of[1], 1), 1, 64).astype(jnp.int32)
    source_label = with_ends(jax.random.randint(key_of[2], (NX, NY), 0, LABELS), jax.random.fold_in(key_of[2], 1), 0, LABELS - 1).astype(jnp.int32)
    return {"guidance": guidance, "seam_weight": seam_weight, "source_label": source_label}


RELAX_WEIGHT = 0.8
SEAM_FACTOR = 0.25


def conductance(weight_here, weight_near, label_here, label_near):
    matching = jnp.where(label_near == label_here, 1.0, SEAM_FACTOR)
    return (weight_here + weight_near) / 64.0 * matching


def edge_maps(padded_weight, padded_label):
    weight_here = padded_weight[1:-1, 1:-1]
    label_here = padded_label[1:-1, 1:-1]
    upward = conductance(weight_here, padded_weight[:-2, 1:-1], label_here, padded_label[:-2, 1:-1])
    downward = conductance(weight_here, padded_weight[2:, 1:-1], label_here, padded_label[2:, 1:-1])
    leftward = conductance(weight_here, padded_weight[1:-1, :-2], label_here, padded_label[1:-1, :-2])
    rightward = conductance(weight_here, padded_weight[1:-1, 2:], label_here, padded_label[1:-1, 2:])
    return (upward, downward, leftward, rightward)


def fold_rows(values, offset):
    blocks = values.reshape(values.shape[0] // 2, 2, values.shape[1] // 2, 2)
    return 0.5 * (blocks[:, offset, :, 0] + blocks[:, offset, :, 1])


def fold_columns(values, offset):
    blocks = values.reshape(values.shape[0] // 2, 2, values.shape[1] // 2, 2)
    return 0.5 * (blocks[:, 0, :, offset] + blocks[:, 1, :, offset])


def coarsen(conductances):
    upward, downward, leftward, rightward = conductances
    return (fold_rows(upward, 0), fold_rows(downward, 1), fold_columns(leftward, 0), fold_columns(rightward, 1))


def level_entry(conductances, level_index):
    factor = 0.5 ** level_index
    upward, downward, leftward, rightward = conductances
    return (conductances, factor * (upward + downward + leftward + rightward), factor)


def restrict(values):
    blocks = values.reshape(values.shape[0], values.shape[1] // 2, 2, values.shape[2] // 2, 2)
    return 0.25 * (blocks[:, :, 0, :, 0] + blocks[:, :, 0, :, 1] + blocks[:, :, 1, :, 0] + blocks[:, :, 1, :, 1])


def prolong(values):
    channels, height, breadth = values.shape
    spread = jnp.broadcast_to(values[:, :, None, :, None], (channels, height, 2, breadth, 2))
    return spread.reshape(channels, 2 * height, 2 * breadth)


def stencil(centre, padded, conductances, factor):
    upward, downward, leftward, rightward = conductances
    flux_sum = upward * (centre - padded[:, :-2, 1:-1]) + downward * (centre - padded[:, 2:, 1:-1])
    flux_sum = flux_sum + leftward * (centre - padded[:, 1:-1, :-2]) + rightward * (centre - padded[:, 1:-1, 2:])
    return factor * flux_sum


def whole_apply(values, conductances, factor):
    padded = jnp.pad(values, ((0, 0), (1, 1), (1, 1)))
    return stencil(values, padded, conductances, factor)


def relax(source_term, iterate, entry):
    conductances, diagonal, factor = entry
    return iterate + RELAX_WEIGHT * (source_term - whole_apply(iterate, conductances, factor)) / diagonal


def cycle(source_term, hierarchy, level_index):
    entry = hierarchy[level_index]
    iterate = RELAX_WEIGHT * source_term / entry[1]
    if level_index == len(hierarchy) - 1:
        def coarse_step(number, current):
            return relax(source_term, current, entry)
        return lax.fori_loop(0, COARSE_SWEEPS - 1, coarse_step, iterate)
    for number in range(SWEEPS - 1):
        iterate = relax(source_term, iterate, entry)
    residual_now = source_term - whole_apply(iterate, entry[0], entry[2])
    iterate = iterate + prolong(cycle(restrict(residual_now), hierarchy, level_index + 1))
    for number in range(SWEEPS):
        iterate = relax(source_term, iterate, entry)
    return iterate


def reference(guidance, seam_weight, source_label):
    padded_weight = jnp.pad(seam_weight.astype(jnp.float32), 1)
    padded_label = jnp.pad(source_label, 1)
    conductances = edge_maps(padded_weight, padded_label)
    hierarchy = []
    for level_index in range(LEVELS):
        if level_index > 0:
            conductances = coarsen(conductances)
        hierarchy.append(level_entry(conductances, level_index))
    upward, downward, leftward, rightward = hierarchy[0][0]
    down_guide = guidance[0]
    side_guide = guidance[1]
    above_rows = jnp.pad(down_guide, ((0, 0), (1, 0), (0, 0)))[:, :-1, :]
    beside = jnp.pad(side_guide, ((0, 0), (0, 0), (1, 0)))[:, :, :-1]
    source_term = upward * above_rows - downward * down_guide + leftward * beside - rightward * side_guide
    solution = jnp.zeros_like(source_term)
    for number in range(CYCLES):
        residual_now = source_term - whole_apply(solution, hierarchy[0][0], 1.0)
        solution = solution + cycle(residual_now, hierarchy, 0)
    residual = source_term - whole_apply(solution, hierarchy[0][0], 1.0)
    return solution, residual
```

```python
import jax
import jax.numpy as jnp
from jax import lax
from jax.experimental import pallas as pl
from jax.experimental.pallas import tpu as pltpu
from jax.sharding import Mesh, PartitionSpec as P

F32 = jnp.float32
CHANNELS = 3
COARSE_SWEEPS = 48
RELAX_WEIGHT = 0.8
SEAM_FACTOR = 0.25
PAD = 8
LANES = 128
REACH = 56
SIDES = ("y", "x", "core")
CHIPS = ("z", "y", "x")
LOCAL_ROWS = (192, 96, 48)
UP, DOWN, LEFT, RIGHT, SCALE, INVERSE = range(6)


def lane_ids(rows):
    return lax.broadcasted_iota(jnp.int32, (rows, LANES), 1)


def beside(halves, width):
    count = len(halves)
    lane = lane_ids(halves[0].shape[0])
    ahead = [pltpu.roll(x, width, 1) for x in halves]
    behind = [pltpu.roll(x, LANES - width, 1) for x in halves]
    if count == 1:
        return ahead, behind
    left = [jnp.where(lane < width, ahead[h - 1], ahead[h]) for h in range(count)]
    right = [
        jnp.where(lane >= LANES - width, behind[(h + 1) % count], behind[h]) for h in range(count)
    ]
    return left, right


def pair_sum(x, width):
    low = (lane_ids(x.shape[0]) & width) == 0
    return x + jnp.where(low, pltpu.roll(x, LANES - width, 1), pltpu.roll(x, width, 1))


def low_of_pair(x, width):
    low = (lane_ids(x.shape[0]) & width) == 0
    return jnp.where(low, x, pltpu.roll(x, width, 1))


def high_of_pair(x, width):
    low = (lane_ids(x.shape[0]) & width) == 0
    return jnp.where(low, pltpu.roll(x, LANES - width, 1), x)


def exact_dot(x, chosen):
    return lax.dot_general(
        x,
        chosen,
        (((1,), (0,)), ((), ())),
        precision=lax.Precision.HIGHEST,
        preferred_element_type=F32,
    )


def chunks(low, high, size, body):
    count = (high - low) // size
    assert count * size == high - low

    def step(i, carry):
        body(pl.multiple_of(PAD + low + i * size, 8))
        return carry

    if count == 1:
        body(PAD + low)
    else:
        lax.fori_loop(0, count, step, 0)


def stencil(mode, target, field, base, maps, low, high, size, width=1, halves=2, first=0, extra=None):
    def body(start):
        at = pl.ds(start, size)
        span = range(first, first + halves)
        coef = [[maps[m, h, at, :] for h in span] for m in range(4)]
        for c in range(CHANNELS):
            here = [field[c, h, at, :] for h in span]
            above = [field[c, h, pl.ds(start - 1, size), :] for h in span]
            below = [field[c, h, pl.ds(start + 1, size), :] for h in span]
            left, right = beside(here, width)
            for i, h in enumerate(span):
                near = (above[i], below[i], left[i], right[i])
                if mode in ("difference", "scaled_difference", "final"):
                    near = [n - here[i] for n in near]
                total = coef[0][i] * near[0] + coef[1][i] * near[1]
                total = total + (coef[2][i] * near[2] + coef[3][i] * near[3])
                if mode == "first":
                    result = (2.0 - RELAX_WEIGHT) * here[i] + total
                elif mode == "relax":
                    result = (1.0 - RELAX_WEIGHT) * here[i] + base[c, h, at, :] + total
                elif mode == "relax_add":
                    result = (1.0 - RELAX_WEIGHT) * here[i] + base[c, h, at, :] + total
                    result = extra[c, h, at, :] + result
                elif mode == "residual":
                    result = base[c, h, at, :] - RELAX_WEIGHT * here[i] + total
                    result = maps[SCALE, h, at, :] * result
                elif mode == "difference":
                    result = base[c, h, at, :] + total
                else:
                    result = maps[SCALE, h, at, :] * (base[c, h, at, :] + total)
                target[c, h, at, :] = result

    chunks(low, high, size, body)


def scaled_maps(raw, factor):
    whole = raw[0] + raw[1] + raw[2] + raw[3]
    inside = whole > 0.0
    share = jnp.where(inside, RELAX_WEIGHT / jnp.where(inside, whole, 1.0), 0.0)
    return [r * share for r in raw], whole * (factor / RELAX_WEIGHT), share * (1.0 / factor)


def even_odd(ref, lead, start, count):
    return (
        ref[lead + (pl.ds(start, count, stride=2), slice(None))],
        ref[lead + (pl.ds(start + 1, count, stride=2), slice(None))],
    )


def stack_kernel(guidance, weight, label, whole, upper, lower):
    def put(a, x):
        whole[a] = x
        upper[a] = x[:REACH]
        lower[a] = x[64 - REACH :]

    for c in range(CHANNELS):
        put(c, guidance[0, c])
        put(CHANNELS + c, guidance[1, c])
    put(6, weight[...].astype(F32))
    put(7, label[...].astype(F32))


def pack_kernel(own, above, below, to_left, to_right):
    for a in range(8):
        top = jnp.concatenate([above[a], own[a, :32]], axis=0)
        bottom = jnp.concatenate([own[a, 32:], below[a]], axis=0)
        bottom = pltpu.roll(bottom, 64, 1)
        low = lane_ids(88) < 64
        to_left[a] = jnp.where(low, top, bottom)
        to_right[a] = jnp.where(low, bottom, top)


def local_down(level, field, base, work, maps, next_base, next_maps, first_rows, rest_rows, next_rows):
    width = 2**level
    low, high, size = first_rows
    stencil("first", field, base, base, maps, low, high, size, width)
    low, high, size = rest_rows
    stencil("scaled_difference", work, field, base, maps, low, high, size, width)
    if next_base is None:
        return

    low, high, size = next_rows

    def body(start):
        at = pl.ds(start, size)
        for h in range(2):
            inverse = 0.25 * next_maps[INVERSE, h, at, :]
            for c in range(CHANNELS):
                even, odd = even_odd(work, (c, h), 2 * start - PAD, size)
                next_base[c, h, at, :] = pair_sum(even + odd, width) * inverse

    chunks(low, high, size, body)


def own_row(x):
    lane = lax.broadcasted_iota(jnp.int32, (LANES, LANES), 0)
    place = lax.broadcasted_iota(jnp.int32, (LANES, LANES), 1)
    chosen = jnp.where(lane == 8 * (place & 15), 1.0, 0.0).astype(F32)
    count = x.shape[0] // 8
    spread = exact_dot(x, chosen)
    rows = []
    keep = (lane_ids(8) >> 4) == lax.broadcasted_iota(jnp.int32, (8, LANES), 0)
    for i in range(count):
        part = jnp.where(keep, spread[8 * i : 8 * i + 8], 0.0)
        rows.append(jnp.sum(part, axis=0, keepdims=True))
    return rows


def down_levels(fields, bases, work, maps, ranges):
    for level in range(3):
        local_down(
            level,
            fields[level],
            bases[level],
            work[level],
            maps[level],
            bases[level + 1] if level < 2 else None,
            maps[level + 1] if level < 2 else None,
            *ranges[level],
        )
    tiles = []
    for c in range(CHANNELS):
        even, odd = even_odd(work[2], (c, 0), PAD + 16, 8)
        tiles.append(0.25 * pair_sum(even + odd, 4))
    return tiles


FIRST_DOWN = (
    ((8, 184, 16), (8, 184, 16), (0, 96, 32)),
    ((0, 96, 32), (0, 96, 32), (0, 48, 24)),
    ((0, 48, 24), (0, 48, 24), None),
)
LATER_DOWN = (
    ((32, 160, 32), (32, 160, 32), (16, 80, 32)),
    ((16, 80, 32), (16, 80, 32), (8, 40, 32)),
    ((8, 40, 32), (8, 40, 32), None),
)
FIRST_UP = ((32, 160, 32), (8, 88, 16), (0, 48, 24))
LATER_UP = ((56, 136, 16), (24, 72, 24), (8, 40, 32))


def clear(ref, *bounds):
    for index in range(ref.shape[0]):
        for h in range(ref.shape[1]):
            for low, high in bounds:
                ref[index, h, low:high, :] = jnp.zeros((high - low, LANES), F32)


def setup_kernel(
    place, own, above, below, from_right, from_left,
    m0, m1, m2, source, f0, g1, f1, g2, f2, message,
    cells, raw0, raw1, raw2, w0, w1, w2,
):
    row_at, col_at = place[0], place[1]
    rows_of = lambda n, low: low + lax.broadcasted_iota(jnp.int32, (n, LANES), 0)
    edge = jnp.zeros((16, LANES), F32)
    not_top, not_bottom = row_at > 0, row_at < 7
    for a in range(8):
        for h in range(2):
            cells[a, h, 0:16, :] = edge
            cells[a, h, 192:208, :] = edge
        cells[a, 0, 16:72, :] = jnp.where(not_top, above[a], 0.0)
        cells[a, 0, 72:136, :] = own[a]
        cells[a, 0, 136:192, :] = jnp.where(not_bottom, below[a], 0.0)
        low = lane_ids(88) < 64
        inside = (low & (col_at < 31)) | (~low & (col_at > 0))
        top = jnp.where(low, from_right[a], from_left[a])
        bottom = pltpu.roll(jnp.where(low, from_left[a], from_right[a]), 64, 1)
        cells[a, 1, 16:104, :] = jnp.where(inside & (not_top | (rows_of(88, 8) >= 64)), top, 0.0)
        cells[a, 1, 104:192, :] = jnp.where(
            inside & (not_bottom | (rows_of(88, 96) < 128)), bottom, 0.0
        )
    for ref in (m0, raw0, source, f0, w0):
        clear(ref, (0, 16), (192, 208))
    for ref, rows in ((m1, 96), (raw1, 96), (g1, 96), (f1, 96), (w1, 96)):
        clear(ref, (0, 8), (rows + 8, rows + 16))
    for ref, rows in ((m2, 48), (raw2, 48), (g2, 48), (f2, 48), (w2, 48)):
        clear(ref, (0, 8), (rows + 8, rows + 16))

    def fine(start):
        size = 16
        at = pl.ds(start, size)
        up_at, down_at = pl.ds(start - 1, size), pl.ds(start + 1, size)
        weights = [cells[6, h, at, :] for h in range(2)]
        labels = [cells[7, h, at, :] for h in range(2)]
        weight_sides = beside(weights, 1)
        label_sides = beside(labels, 1)
        coef = []
        for h in range(2):
            near_weights = (
                cells[6, h, up_at, :], cells[6, h, down_at, :], weight_sides[0][h], weight_sides[1][h],
            )
            near_labels = (
                cells[7, h, up_at, :], cells[7, h, down_at, :], label_sides[0][h], label_sides[1][h],
            )
            raw = []
            for m in range(4):
                matching = jnp.where(near_labels[m] == labels[h], 1.0 / 64.0, SEAM_FACTOR / 64.0)
                value = (weights[h] + near_weights[m]) * matching
                value = jnp.where(weights[h] > 0.0, value, 0.0)
                raw.append(value)
                raw0[m, h, at, :] = value
            scaled, scale, _ = scaled_maps(raw, 1.0)
            for m in range(4):
                m0[m, h, at, :] = scaled[m]
            m0[SCALE, h, at, :] = scale
            coef.append(scaled)
        for c in range(CHANNELS):
            second = [cells[CHANNELS + c, h, at, :] for h in range(2)]
            left = beside(second, 1)[0]
            for h in range(2):
                flux = coef[h][UP] * cells[c, h, up_at, :] - coef[h][DOWN] * cells[c, h, at, :]
                flux = flux + coef[h][LEFT] * left[h] - coef[h][RIGHT] * second[h]
                source[c, h, at, :] = flux

    chunks(8, 184, 16, fine)

    def coarser(raw, width, start, size, h):
        parts = []
        for m in range(4):
            even, odd = even_odd(raw, (m, h), start, size)
            if m == UP:
                parts.append(0.5 * pair_sum(even, width))
            elif m == DOWN:
                parts.append(0.5 * pair_sum(odd, width))
            elif m == LEFT:
                parts.append(0.5 * low_of_pair(even + odd, width))
            else:
                parts.append(0.5 * high_of_pair(even + odd, width))
        return parts

    for level, fine_raw, raw, maps, rows in ((1, raw0, raw1, m1, 96), (2, raw1, raw2, m2, 48)):

        def coarse(start, level=level, fine_raw=fine_raw, raw=raw, maps=maps):
            size = 16
            at = pl.ds(start, size)
            for h in range(2):
                parts = coarser(fine_raw, 2 ** (level - 1), 2 * start - PAD, size, h)
                scaled, scale, inverse = scaled_maps(parts, 0.5**level)
                for m in range(4):
                    raw[m, h, at, :] = parts[m]
                    maps[m, h, at, :] = scaled[m]
                maps[SCALE, h, at, :] = scale
                maps[INVERSE, h, at, :] = inverse

        chunks(0, rows, 16, coarse)
    tiles = down_levels((f0, f1, f2), (source, g1, g2), (w0, w1, w2), (m0, m1, m2), FIRST_DOWN)
    tiles = tiles + coarser(raw2, 4, PAD + 16, 8, 0)
    rows = own_row(jnp.concatenate(tiles, axis=0))
    for i in range(7):
        message[i : i + 1, :] = rows[i]
    message[7:8, :] = jnp.zeros((1, LANES), F32)


def unpack(place, mine, other, count, stride, ordered, put):
    core = place[2]
    for f in range(count):
        own = mine[pl.ds(f, 128, stride=stride), :]
        theirs = other[pl.ds(f, 128, stride=stride), :]
        ordered[f, pl.ds(0, 128, stride=2), :] = jnp.where(core == 0, own, theirs)
        ordered[f, pl.ds(1, 128, stride=2), :] = jnp.where(core == 0, theirs, own)
    sub = lax.broadcasted_iota(jnp.int32, (8, LANES), 0)
    part = lane_ids(8) >> 4

    def body(z, carry):
        for f in range(count):
            for group in range(4):
                x = ordered[f, pl.ds(pl.multiple_of(z * 32 + 8 * group, 8), 8), :]
                for k in (4, 2, 1):
                    same = (sub & k) == (part & k)
                    ahead = pltpu.roll(pltpu.roll(x, 8 - k, 0), 16 * k, 1)
                    if k == 4:
                        moved = ahead
                    else:
                        behind = pltpu.roll(pltpu.roll(x, k, 0), LANES - 16 * k, 1)
                        moved = jnp.where((sub & k) == 0, ahead, behind)
                    x = jnp.where(same, x, moved)
                put(f, pl.multiple_of(PAD + 8 * z, 8), group, x)
        return carry

    lax.fori_loop(0, 8, body, 0)


def halving(kind):
    lane = lax.broadcasted_iota(jnp.int32, (2 * LANES, LANES), 0)
    place = lax.broadcasted_iota(jnp.int32, (2 * LANES, LANES), 1)
    if kind == "sum":
        hit = (lane >> 1) == place
    elif kind == "low":
        hit = lane == 2 * place
    else:
        hit = lane == 2 * place + 1
    return jnp.where(hit, 1.0, 0.0).astype(F32)


def doubling():
    place = lax.broadcasted_iota(jnp.int32, (LANES, 2 * LANES), 0)
    lane = lax.broadcasted_iota(jnp.int32, (LANES, 2 * LANES), 1)
    return jnp.where((lane >> 1) == place, 1.0, 0.0).astype(F32)


def folded(halves, matrix):
    if len(halves) == 1:
        return [exact_dot(halves[0], matrix[:LANES])]
    return [
        exact_dot(jnp.concatenate(halves[i : i + 2], axis=1), matrix)
        for i in range(0, len(halves), 2)
    ]


WHOLE = {3: (4, 64, 1), 4: (2, 32, 0), 5: (1, 16, 0), 6: (1, 8, 0)}


def whole_maps(level, raw, maps):
    halves, rows, first = WHOLE[level]
    size = min(rows, 16)

    def body(start):
        at = pl.ds(start, size)
        lane = lane_ids(size)
        for i in range(halves):
            scaled, scale, inverse = scaled_maps(
                [raw[m, first + i, at, :] for m in range(4)], 0.5**level
            )
            if i == 0:
                scaled[LEFT] = jnp.where(lane == 0, 0.0, scaled[LEFT])
            if i == halves - 1:
                last = 63 if level == 6 else LANES - 1
                scaled[RIGHT] = jnp.where(lane == last, 0.0, scaled[RIGHT])
            for m in range(4):
                maps[m, first + i, at, :] = scaled[m]
            maps[SCALE, first + i, at, :] = scale
            maps[INVERSE, first + i, at, :] = inverse

    chunks(0, rows, size, body)


def coarsen_whole(level, raw, next_raw):
    halves, rows, first = WHOLE[level]
    next_halves, next_rows, next_first = WHOLE[level + 1]
    for m in range(4):
        parts = []
        for h in range(halves):
            even, odd = even_odd(raw, (m, first + h), PAD, next_rows)
            parts.append(even if m == UP else odd if m == DOWN else even + odd)
        kind = "sum" if m in (UP, DOWN) else "low" if m == LEFT else "high"
        for h, x in enumerate(folded(parts, halving(kind))):
            next_raw[m, next_first + h, PAD : PAD + next_rows, :] = 0.5 * x


def coarse_solve(base, maps):
    coef = [maps[m, 0, PAD : PAD + 8, :] for m in range(4)]
    row = lax.broadcasted_iota(jnp.int32, (8, LANES), 0)
    coef[UP] = jnp.where(row == 0, 0.0, coef[UP])
    coef[DOWN] = jnp.where(row == 7, 0.0, coef[DOWN])
    right_side = [base[c, 0, PAD : PAD + 8, :] for c in range(CHANNELS)]

    def step(number, values):
        out = []
        for c in range(CHANNELS):
            v = values[c]
            near = coef[UP] * pltpu.roll(v, 1, 0) + coef[DOWN] * pltpu.roll(v, 7, 0)
            side = coef[LEFT] * pltpu.roll(v, 1, 1) + coef[RIGHT] * pltpu.roll(v, LANES - 1, 1)
            out.append(((1.0 - RELAX_WEIGHT) * v + right_side[c]) + (near + side))
        return tuple(out)

    return lax.fori_loop(0, COARSE_SWEEPS - 1, step, tuple(right_side), unroll=True)


def whole_cycle(level, bases, fields, others, maps):
    halves, rows, first = WHOLE[level]
    base, field, other, level_maps = bases[level], fields[level], others[level], maps[level]
    size = {3: 16, 4: 32, 5: 16}[level]
    stencil("first", field, base, base, level_maps, 0, rows, size, 1, halves, first)
    stencil("residual", other, field, base, level_maps, 0, rows, size, 1, halves, first)
    next_halves, next_rows, next_first = WHOLE[level + 1]
    summed = []
    for h in range(halves):
        parts = []
        for c in range(CHANNELS):
            even, odd = even_odd(other, (c, first + h), PAD, next_rows)
            parts.append(even + odd)
        summed.append(jnp.concatenate(parts, axis=0))
    for h, x in enumerate(folded(summed, halving("sum"))):
        inverse = 0.25 * maps[level + 1][INVERSE, next_first + h, PAD : PAD + next_rows, :]
        for c in range(CHANNELS):
            part = x[c * next_rows : (c + 1) * next_rows]
            bases[level + 1][c, next_first + h, PAD : PAD + next_rows, :] = part * inverse
    if level == 5:
        coarse = coarse_solve(bases[6], maps[6])
        coarse = [jnp.concatenate(coarse, axis=0)]
    else:
        whole_cycle(level + 1, bases, fields, others, maps)
        coarse = [
            jnp.concatenate(
                [
                    fields[level + 1][c, next_first + h, PAD : PAD + next_rows, :]
                    for c in range(CHANNELS)
                ],
                axis=0,
            )
            for h in range(next_halves)
        ]
    for m, x in enumerate(coarse):
        wide = exact_dot(x, doubling())
        for i in range(min(halves, 2)):
            h = first + 2 * m + i
            for c in range(CHANNELS):
                part = wide[c * next_rows : (c + 1) * next_rows, LANES * i : LANES * (i + 1)]
                for offset in range(2):
                    at = pl.ds(PAD + offset, next_rows, stride=2)
                    field[c, h, at, :] = field[c, h, at, :] + part
    if level > 3:
        stencil("relax", other, field, base, level_maps, 0, rows, size, 1, halves, first)
        stencil("relax", field, other, base, level_maps, 0, rows, size, 1, halves, first)


def window(ref, index, place):
    group = lax.shift_right_logical(place[1], 3)
    offset = 16 * (place[1] & 7)
    at = pl.ds(pl.multiple_of(8 * place[0], 8), 24)
    lane = lane_ids(24)
    turn = lax.rem(LANES - offset, LANES)
    before, here, after = [pltpu.roll(ref[index, group + i, at, :], turn, 1) for i in range(3)]
    low = lane < 64
    fits = lane + offset < LANES
    return jnp.where(low, jnp.where(fits, here, after), jnp.where(fits, before, here))


def spread_matrix():
    place = lax.broadcasted_iota(jnp.int32, (LANES, 2 * LANES), 0)
    lane = lax.broadcasted_iota(jnp.int32, (LANES, 2 * LANES), 1)
    source = lane >> 3
    source = jnp.where(lane >= 192, source + 96, source)
    return jnp.where(place == source, 1.0, 0.0).astype(F32)


def correct_level_two(place, bases, fields, maps, f2, near_maps, near_base, near_a, near_b):
    for m in range(4):
        near_maps[m, 0, PAD : PAD + 24, :] = window(maps[3], m, place)
    edge = jnp.zeros((PAD, LANES), F32)
    for c in range(CHANNELS):
        near_base[c, 0, PAD : PAD + 24, :] = window(bases[3], c, place)
        near_a[c, 0, PAD : PAD + 24, :] = window(fields[3], c, place)
        for ref in (near_a, near_b):
            ref[c, 0, 0:PAD, :] = edge
            ref[c, 0, PAD + 24 : PAD + 32, :] = edge
    stencil("relax", near_b, near_a, near_base, near_maps, 0, 24, 24, 1, 1)
    stencil("relax", near_a, near_b, near_base, near_maps, 0, 24, 24, 1, 1)
    flat = jnp.concatenate([near_a[c, 0, PAD : PAD + 24, :] for c in range(CHANNELS)], axis=0)
    wide = exact_dot(flat, spread_matrix())
    for c in range(CHANNELS):
        for h in range(2):
            part = wide[24 * c : 24 * c + 24, LANES * h : LANES * h + LANES]
            for offset in range(2):
                at = pl.ds(PAD + offset, 24, stride=2)
                f2[c, h, at, :] = f2[c, h, at, :] + part


def add_rows(field, coarse, low, high, size):
    def body(start):
        for c in range(CHANNELS):
            for h in range(2):
                part = coarse[c, h, pl.ds(start, size), :]
                for offset in range(2):
                    at = pl.ds(2 * start - PAD + offset, size, stride=2)
                    field[c, h, at, :] = field[c, h, at, :] + part

    chunks(low, high, size, body)


def up_levels(ranges, fields, bases, works, maps, extra):
    low, high, size = ranges[2]
    stencil("relax", works[2], fields[2], bases[2], maps[2], low, high, size, 4)
    stencil("relax", fields[2], works[2], bases[2], maps[2], low, high, size, 4)
    add_rows(fields[1], fields[2], 0, 48, 24)
    low, high, size = ranges[1]
    stencil("relax", works[1], fields[1], bases[1], maps[1], low, high, size, 2)
    stencil("relax", fields[1], works[1], bases[1], maps[1], low, high, size, 2)
    add_rows(fields[0], fields[1], 0, 96, 24)
    low, high, size = ranges[0]
    stencil("relax", works[0], fields[0], bases[0], maps[0], low, high, size, 1)
    if extra is None:
        stencil("relax", fields[0], works[0], bases[0], maps[0], low, high, size, 1)
    else:
        stencil(
            "relax_add", fields[0], works[0], bases[0], maps[0], low, high, size, 1, extra=extra
        )


def copy_field(source, target):
    count, halves, rows, _ = source.shape
    for c in range(count):
        for h in range(halves):
            target[c, h] = source[c, h]


def middle_kernel(
    place, mine, other, m0, m1, m2, source, f0, g1, f1, g2, f2,
    m3, m4, m5, m6, solution, n0, h0, k1, h1, k2, h2, message,
    ordered, raw3, raw4, raw5, raw6, b3, v3, o3, b4, v4, o4, b5, v5, o5, b6,
    w0, w1, w2, near_maps, near_base, near_a, near_b,
):
    for ref in (m3, raw3, b3, v3, o3):
        rows = ref.shape[2]
        clear(ref, (0, PAD), (rows - PAD, rows))
        for index in range(ref.shape[0]):
            for h in (0, 5):
                ref[index, h] = jnp.zeros((rows, LANES), F32)
    for ref in (b4, v4, o4, b5, v5, o5):
        rows = ref.shape[2]
        clear(ref, (0, PAD), (rows - PAD, rows))
    for ref in (w0, w1, w2, n0):
        rows = ref.shape[2]
        clear(ref, (0, rows))

    def put(f, start, group, tile):
        if f < CHANNELS:
            b3[f, 1 + group, pl.ds(start, 8), :] = tile
        else:
            raw3[f - CHANNELS, 1 + group, pl.ds(start, 8), :] = tile

    unpack(place, mine, other, 7, 8, ordered, put)
    raws = {3: raw3, 4: raw4, 5: raw5, 6: raw6}
    maps = {3: m3, 4: m4, 5: m5, 6: m6}
    whole_maps(3, raw3, m3)
    for level in (3, 4, 5):
        coarsen_whole(level, raws[level], raws[level + 1])
        whole_maps(level + 1, raws[level + 1], maps[level + 1])
    scale_base(b3, m3)
    whole_cycle(
        3, {3: b3, 4: b4, 5: b5, 6: b6}, {3: v3, 4: v4, 5: v5}, {3: o3, 4: o4, 5: o5}, maps
    )
    copy_field(f0, solution)
    copy_field(f1, h1)
    copy_field(f2, h2)
    correct_level_two(
        place, {3: b3}, {3: v3}, maps, h2, near_maps, near_base, near_a, near_b
    )
    local_maps = (m0, m1, m2)
    up_levels(FIRST_UP, (solution, h1, h2), (source, g1, g2), (w0, w1, w2), local_maps, None)
    stencil("difference", n0, solution, source, m0, 32, 160, 32, 1)
    for ref in (h0, k1, k2):
        rows = ref.shape[2]
        clear(ref, (0, rows))
    tiles = down_levels((h0, h1, h2), (n0, k1, k2), (w0, w1, w2), local_maps, LATER_DOWN)
    rows = own_row(jnp.concatenate(tiles, axis=0))
    for i in range(CHANNELS):
        message[i : i + 1, :] = rows[i]


def scale_base(base, maps):
    halves, rows, first = WHOLE[3]

    def body(start):
        at = pl.ds(start, 16)
        for i in range(halves):
            inverse = maps[INVERSE, first + i, at, :]
            for c in range(CHANNELS):
                base[c, first + i, at, :] = base[c, first + i, at, :] * inverse

    chunks(0, rows, 16, body)


def last_kernel(
    place, mine, other, m0, m1, m2, source, m3, m4, m5, m6, before, n0, f0, k1, f1, k2, f2,
    solution, residual,
    ordered, b3, v3, o3, b4, v4, o4, b5, v5, o5, b6,
    h0, h1, h2, w0, w1, w2, near_maps, near_base, near_a, near_b,
):
    for ref in (b3, v3, o3):
        rows = ref.shape[2]
        clear(ref, (0, PAD), (rows - PAD, rows))
        for index in range(ref.shape[0]):
            for h in (0, 5):
                ref[index, h] = jnp.zeros((rows, LANES), F32)
    for ref in (b4, v4, o4, b5, v5, o5):
        rows = ref.shape[2]
        clear(ref, (0, PAD), (rows - PAD, rows))
    for ref in (w0, w1, w2):
        rows = ref.shape[2]
        clear(ref, (0, rows))

    def put(f, start, group, tile):
        b3[f, 1 + group, pl.ds(start, 8), :] = tile

    unpack(place, mine, other, CHANNELS, CHANNELS, ordered, put)
    maps = {3: m3, 4: m4, 5: m5, 6: m6}
    scale_base(b3, m3)
    whole_cycle(
        3, {3: b3, 4: b4, 5: b5, 6: b6}, {3: v3, 4: v4, 5: v5}, {3: o3, 4: o4, 5: o5}, maps
    )
    copy_field(f0, h0)
    copy_field(f1, h1)
    copy_field(f2, h2)
    correct_level_two(
        place, {3: b3}, {3: v3}, maps, h2, near_maps, near_base, near_a, near_b
    )
    local_maps = (m0, m1, m2)
    up_levels(LATER_UP, (h0, h1, h2), (n0, k1, k2), (w0, w1, w2), local_maps, before)
    stencil("final", w0, h0, source, m0, 64, 128, 32, 1)
    for c in range(CHANNELS):
        solution[c] = h0[c, 0, PAD + 64 : PAD + 128, :]
        residual[c] = w0[c, 0, PAD + 64 : PAD + 128, :]


def shape(*dims):
    return jax.ShapeDtypeStruct(dims, F32)


def field_shape(level, count):
    return (count, 2, LOCAL_ROWS[level] + 2 * PAD, LANES)


def whole_shape(level, count):
    halves, rows, first = WHOLE[level]
    return (count, halves + 2 * first, rows + 2 * PAD, LANES)


def call(kernel, outs, scratch, *args):
    in_specs = [pl.BlockSpec(memory_space=pltpu.VMEM) for _ in args]
    if args[0].dtype == jnp.int32 and args[0].ndim == 1:
        in_specs[0] = pl.BlockSpec(memory_space=pltpu.SMEM)
    return pl.pallas_call(
        kernel,
        out_shape=[shape(*o) for o in outs],
        in_specs=in_specs,
        out_specs=[pl.BlockSpec(memory_space=pltpu.VMEM) for _ in outs],
        scratch_shapes=[pltpu.VMEM(s, F32) for s in scratch],
        compiler_params=pltpu.CompilerParams(vmem_limit_bytes=48 * 1024 * 1024),
    )(*args)


def ring(count, step):
    return [(i, (i + step) % count) for i in range(count)]


def gathered(message):
    rows = message.shape[0]
    sent = jnp.broadcast_to(message[None], (128, rows, LANES))
    mine = lax.all_to_all(sent, CHIPS, 0, 0, tiled=True)
    mine = mine.reshape(128 * rows, LANES)
    return mine, lax.ppermute(mine, "core", ring(2, 1))


def local(guidance, seam_weight, source_label):
    place = jnp.stack(
        [lax.axis_index("z"), lax.axis_index(SIDES), lax.axis_index("core")]
    ).astype(jnp.int32)
    own, upper, lower = call(
        stack_kernel,
        [(8, 64, LANES), (8, REACH, LANES), (8, REACH, LANES)],
        [],
        guidance,
        seam_weight,
        source_label,
    )
    above = lax.ppermute(lower, "z", ring(8, 1))
    below = lax.ppermute(upper, "z", ring(8, -1))
    to_left, to_right = call(
        pack_kernel, [(8, 88, LANES)] * 2, [], own, above, below
    )
    from_right = lax.ppermute(to_left, SIDES, ring(32, -1))
    from_left = lax.ppermute(to_right, SIDES, ring(32, 1))
    fields = [field_shape(level, CHANNELS) for level in range(3)]
    maps = [field_shape(0, 5), field_shape(1, 6), field_shape(2, 6)]
    raws = [field_shape(level, 4) for level in range(3)]
    m0, m1, m2, source, f0, g1, f1, g2, f2, message = call(
        setup_kernel,
        maps + [fields[0], fields[0], fields[1], fields[1], fields[2], fields[2], (8, LANES)],
        [field_shape(0, 8)] + raws + fields,
        place, own, above, below, from_right, from_left,
    )
    mine, other = gathered(message)
    wholes = [whole_shape(level, CHANNELS) for level in (3, 4, 5) for _ in range(3)]
    wholes = wholes + [whole_shape(6, CHANNELS)]
    near = [(4, 1, 40, LANES)] + [(CHANNELS, 1, 40, LANES)] * 3
    m3, m4, m5, m6, solution, n0, h0, k1, h1, k2, h2, message = call(
        middle_kernel,
        [whole_shape(level, 6) for level in (3, 4, 5, 6)]
        + [fields[0]] * 3 + [fields[1]] * 2 + [fields[2]] * 2 + [(CHANNELS, LANES)],
        [(7, 256, LANES)] + [whole_shape(level, 4) for level in (3, 4, 5, 6)]
        + wholes + fields + near,
        place, mine, other, m0, m1, m2, source, f0, g1, f1, g2, f2,
    )
    mine, other = gathered(message)
    outs = call(
        last_kernel,
        [(CHANNELS, 64, LANES)] * 2,
        [(CHANNELS, 256, LANES)] + wholes + fields + fields + near,
        place, mine, other, m0, m1, m2, source, m3, m4, m5, m6,
        solution, n0, h0, k1, h1, k2, h2,
    )
    return tuple(outs)


def solution(mesh):
    fine = Mesh(mesh.devices.reshape(8, 4, 4, 2), ("z", "y", "x", "core"))
    return jax.shard_map(
        local,
        mesh=fine,
        in_specs=(P(None, None, "z", SIDES), P("z", SIDES), P("z", SIDES)),
        out_specs=(P(None, "z", SIDES), P(None, "z", SIDES)),
        check_vma=False,
    )
```

```python
import jax
import jax.numpy as jnp
from jax import lax
from jax.experimental import pallas as pl
from jax.experimental.pallas import tpu as pltpu
from jax.sharding import Mesh, PartitionSpec as P

F32 = jnp.float32
CHANNELS = 3
COARSE_SWEEPS = 48
RELAX_WEIGHT = 0.8
SEAM_FACTOR = 0.25
PAD = 8
LANES = 128
REACH = 56
SIDES = ("y", "x", "core")
CHIPS = ("z", "y", "x")
LOCAL_ROWS = (192, 96, 48)
UP, DOWN, LEFT, RIGHT, SCALE, INVERSE = range(6)


def lane_ids(rows):
    return lax.broadcasted_iota(jnp.int32, (rows, LANES), 1)


def beside(halves, width):
    count = len(halves)
    lane = lane_ids(halves[0].shape[0])
    ahead = [pltpu.roll(x, width, 1) for x in halves]
    behind = [pltpu.roll(x, LANES - width, 1) for x in halves]
    if count == 1:
        return ahead, behind
    left = [jnp.where(lane < width, ahead[h - 1], ahead[h]) for h in range(count)]
    right = [
        jnp.where(lane >= LANES - width, behind[(h + 1) % count], behind[h]) for h in range(count)
    ]
    return left, right


def pair_sum(x, width):
    low = (lane_ids(x.shape[0]) & width) == 0
    return x + jnp.where(low, pltpu.roll(x, LANES - width, 1), pltpu.roll(x, width, 1))


def low_of_pair(x, width):
    low = (lane_ids(x.shape[0]) & width) == 0
    return jnp.where(low, x, pltpu.roll(x, width, 1))


def high_of_pair(x, width):
    low = (lane_ids(x.shape[0]) & width) == 0
    return jnp.where(low, pltpu.roll(x, LANES - width, 1), x)


def exact_dot(x, chosen):
    return lax.dot_general(
        x,
        chosen,
        (((1,), (0,)), ((), ())),
        precision=lax.Precision.HIGHEST,
        preferred_element_type=F32,
    )


def chunks(low, high, size, body):
    count = (high - low) // size
    assert count * size == high - low

    def step(i, carry):
        body(pl.multiple_of(PAD + low + i * size, 8))
        return carry

    if count == 1:
        body(PAD + low)
    else:
        lax.fori_loop(0, count, step, 0)


def stencil(mode, target, field, base, maps, low, high, size, width=1, halves=2, first=0, extra=None):
    def body(start):
        at = pl.ds(start, size)
        span = range(first, first + halves)
        coef = [[maps[m, h, at, :] for h in span] for m in range(4)]
        for c in range(CHANNELS):
            here = [field[c, h, at, :] for h in span]
            above = [field[c, h, pl.ds(start - 1, size), :] for h in span]
            below = [field[c, h, pl.ds(start + 1, size), :] for h in span]
            left, right = beside(here, width)
            for i, h in enumerate(span):
                near = (above[i], below[i], left[i], right[i])
                if mode in ("difference", "scaled_difference", "final"):
                    near = [n - here[i] for n in near]
                total = coef[0][i] * near[0] + coef[1][i] * near[1]
                total = total + (coef[2][i] * near[2] + coef[3][i] * near[3])
                if mode == "first":
                    result = (2.0 - RELAX_WEIGHT) * here[i] + total
                elif mode == "relax":
                    result = (1.0 - RELAX_WEIGHT) * here[i] + base[c, h, at, :] + total
                elif mode == "relax_add":
                    result = (1.0 - RELAX_WEIGHT) * here[i] + base[c, h, at, :] + total
                    result = extra[c, h, at, :] + result
                elif mode == "residual":
                    result = base[c, h, at, :] - RELAX_WEIGHT * here[i] + total
                    result = maps[SCALE, h, at, :] * result
                elif mode == "difference":
                    result = base[c, h, at, :] + total
                else:
                    result = maps[SCALE, h, at, :] * (base[c, h, at, :] + total)
                target[c, h, at, :] = result

    chunks(low, high, size, body)


def scaled_maps(raw, factor):
    whole = raw[0] + raw[1] + raw[2] + raw[3]
    inside = whole > 0.0
    share = jnp.where(inside, RELAX_WEIGHT / jnp.where(inside, whole, 1.0), 0.0)
    return [r * share for r in raw], whole * (factor / RELAX_WEIGHT), share * (1.0 / factor)


def even_odd(ref, lead, start, count):
    return (
        ref[lead + (pl.ds(start, count, stride=2), slice(None))],
        ref[lead + (pl.ds(start + 1, count, stride=2), slice(None))],
    )


def stack_kernel(
    guidance_in, weight_in, label_in, whole, upper, lower, guidance, weight, label, arrived
):
    copies = [
        pltpu.make_async_copy(source, target, arrived.at[i])
        for i, (source, target) in enumerate(
            ((guidance_in, guidance), (weight_in, weight), (label_in, label))
        )
    ]
    for copy in copies:
        copy.start()
    for copy in copies:
        copy.wait()

    def put(a, x):
        whole[a] = x
        upper[a] = x[:REACH]
        lower[a] = x[64 - REACH :]

    for c in range(CHANNELS):
        put(c, guidance[0, c])
        put(CHANNELS + c, guidance[1, c])
    put(6, weight[...].astype(F32))
    put(7, label[...].astype(F32))


def pack_kernel(own, above, below, to_left, to_right):
    for a in range(8):
        top = jnp.concatenate([above[a], own[a, :32]], axis=0)
        bottom = jnp.concatenate([own[a, 32:], below[a]], axis=0)
        bottom = pltpu.roll(bottom, 64, 1)
        low = lane_ids(88) < 64
        to_left[a] = jnp.where(low, top, bottom)
        to_right[a] = jnp.where(low, bottom, top)


def local_down(level, field, base, work, maps, next_base, next_maps, first_rows, rest_rows, next_rows):
    width = 2**level
    low, high, size = first_rows
    stencil("first", field, base, base, maps, low, high, size, width)
    low, high, size = rest_rows
    stencil("scaled_difference", work, field, base, maps, low, high, size, width)
    if next_base is None:
        return

    low, high, size = next_rows

    def body(start):
        at = pl.ds(start, size)
        for h in range(2):
            inverse = 0.25 * next_maps[INVERSE, h, at, :]
            for c in range(CHANNELS):
                even, odd = even_odd(work, (c, h), 2 * start - PAD, size)
                next_base[c, h, at, :] = pair_sum(even + odd, width) * inverse

    chunks(low, high, size, body)


def own_row(x):
    lane = lax.broadcasted_iota(jnp.int32, (LANES, LANES), 0)
    place = lax.broadcasted_iota(jnp.int32, (LANES, LANES), 1)
    chosen = jnp.where(lane == 8 * (place & 15), 1.0, 0.0).astype(F32)
    count = x.shape[0] // 8
    spread = exact_dot(x, chosen)
    rows = []
    keep = (lane_ids(8) >> 4) == lax.broadcasted_iota(jnp.int32, (8, LANES), 0)
    for i in range(count):
        part = jnp.where(keep, spread[8 * i : 8 * i + 8], 0.0)
        rows.append(jnp.sum(part, axis=0, keepdims=True))
    return rows


def down_levels(fields, bases, work, maps, ranges):
    for level in range(3):
        local_down(
            level,
            fields[level],
            bases[level],
            work[level],
            maps[level],
            bases[level + 1] if level < 2 else None,
            maps[level + 1] if level < 2 else None,
            *ranges[level],
        )
    tiles = []
    for c in range(CHANNELS):
        even, odd = even_odd(work[2], (c, 0), PAD + 16, 8)
        tiles.append(0.25 * pair_sum(even + odd, 4))
    return tiles


FIRST_DOWN = (
    ((8, 184, 176), (8, 184, 176), (0, 96, 96)),
    ((0, 96, 96), (0, 96, 96), (0, 48, 48)),
    ((0, 48, 48), (0, 48, 48), None),
)
LATER_DOWN = (
    ((32, 160, 128), (32, 160, 128), (16, 80, 64)),
    ((16, 80, 64), (16, 80, 64), (8, 40, 32)),
    ((8, 40, 32), (8, 40, 32), None),
)
FIRST_UP = ((32, 160, 128), (8, 88, 80), (0, 48, 48))
LATER_UP = ((56, 136, 80), (24, 72, 48), (8, 40, 32))


def clear(ref, *bounds):
    for index in range(ref.shape[0]):
        for h in range(ref.shape[1]):
            for low, high in bounds:
                ref[index, h, low:high, :] = jnp.zeros((high - low, LANES), F32)


def setup_kernel(
    place, own, above, below, from_right, from_left,
    m0, m1, m2, source, f0, g1, f1, g2, f2, message,
    cells, raw0, raw1, raw2, w0, w1, w2,
):
    row_at, col_at = place[0], place[1]
    rows_of = lambda n, low: low + lax.broadcasted_iota(jnp.int32, (n, LANES), 0)
    edge = jnp.zeros((16, LANES), F32)
    not_top, not_bottom = row_at > 0, row_at < 7
    for a in range(8):
        for h in range(2):
            cells[a, h, 0:16, :] = edge
            cells[a, h, 192:208, :] = edge
        cells[a, 0, 16:72, :] = jnp.where(not_top, above[a], 0.0)
        cells[a, 0, 72:136, :] = own[a]
        cells[a, 0, 136:192, :] = jnp.where(not_bottom, below[a], 0.0)
        low = lane_ids(88) < 64
        inside = (low & (col_at < 31)) | (~low & (col_at > 0))
        top = jnp.where(low, from_right[a], from_left[a])
        bottom = pltpu.roll(jnp.where(low, from_left[a], from_right[a]), 64, 1)
        cells[a, 1, 16:104, :] = jnp.where(inside & (not_top | (rows_of(88, 8) >= 64)), top, 0.0)
        cells[a, 1, 104:192, :] = jnp.where(
            inside & (not_bottom | (rows_of(88, 96) < 128)), bottom, 0.0
        )
    for ref in (m0, raw0, source, f0, w0):
        clear(ref, (0, 16), (192, 208))
    for ref, rows in ((m1, 96), (raw1, 96), (g1, 96), (f1, 96), (w1, 96)):
        clear(ref, (0, 8), (rows + 8, rows + 16))
    for ref, rows in ((m2, 48), (raw2, 48), (g2, 48), (f2, 48), (w2, 48)):
        clear(ref, (0, 8), (rows + 8, rows + 16))

    def fine(start):
        size = 176
        at = pl.ds(start, size)
        up_at, down_at = pl.ds(start - 1, size), pl.ds(start + 1, size)
        weights = [cells[6, h, at, :] for h in range(2)]
        labels = [cells[7, h, at, :] for h in range(2)]
        weight_sides = beside(weights, 1)
        label_sides = beside(labels, 1)
        coef = []
        for h in range(2):
            near_weights = (
                cells[6, h, up_at, :], cells[6, h, down_at, :], weight_sides[0][h], weight_sides[1][h],
            )
            near_labels = (
                cells[7, h, up_at, :], cells[7, h, down_at, :], label_sides[0][h], label_sides[1][h],
            )
            raw = []
            for m in range(4):
                matching = jnp.where(near_labels[m] == labels[h], 1.0 / 64.0, SEAM_FACTOR / 64.0)
                value = (weights[h] + near_weights[m]) * matching
                value = jnp.where(weights[h] > 0.0, value, 0.0)
                raw.append(value)
                raw0[m, h, at, :] = value
            scaled, scale, _ = scaled_maps(raw, 1.0)
            for m in range(4):
                m0[m, h, at, :] = scaled[m]
            m0[SCALE, h, at, :] = scale
            coef.append(scaled)
        for c in range(CHANNELS):
            second = [cells[CHANNELS + c, h, at, :] for h in range(2)]
            left = beside(second, 1)[0]
            for h in range(2):
                flux = coef[h][UP] * cells[c, h, up_at, :] - coef[h][DOWN] * cells[c, h, at, :]
                flux = flux + coef[h][LEFT] * left[h] - coef[h][RIGHT] * second[h]
                source[c, h, at, :] = flux

    chunks(8, 184, 176, fine)

    def coarser(raw, width, start, size, h):
        parts = []
        for m in range(4):
            even, odd = even_odd(raw, (m, h), start, size)
            if m == UP:
                parts.append(0.5 * pair_sum(even, width))
            elif m == DOWN:
                parts.append(0.5 * pair_sum(odd, width))
            elif m == LEFT:
                parts.append(0.5 * low_of_pair(even + odd, width))
            else:
                parts.append(0.5 * high_of_pair(even + odd, width))
        return parts

    for level, fine_raw, raw, maps, rows in ((1, raw0, raw1, m1, 96), (2, raw1, raw2, m2, 48)):

        def coarse(start, level=level, fine_raw=fine_raw, raw=raw, maps=maps, rows=rows):
            size = rows
            at = pl.ds(start, size)
            for h in range(2):
                parts = coarser(fine_raw, 2 ** (level - 1), 2 * start - PAD, size, h)
                scaled, scale, inverse = scaled_maps(parts, 0.5**level)
                for m in range(4):
                    raw[m, h, at, :] = parts[m]
                    maps[m, h, at, :] = scaled[m]
                maps[SCALE, h, at, :] = scale
                maps[INVERSE, h, at, :] = inverse

        chunks(0, rows, rows, coarse)
    tiles = down_levels((f0, f1, f2), (source, g1, g2), (w0, w1, w2), (m0, m1, m2), FIRST_DOWN)
    upward, downward, leftward, rightward = coarser(raw2, 4, PAD + 16, 8, 0)
    row = lax.broadcasted_iota(jnp.int32, (8, LANES), 0)
    cell = lane_ids(8) >> 3
    turned = pltpu.roll(pltpu.roll(rightward, LANES - 8, 1), 7, 0)
    ends = jnp.where(row == 7, downward, jnp.where(cell == 15, rightward, turned))
    rows = own_row(jnp.concatenate(tiles + [upward, leftward, ends], axis=0))
    for i in range(6):
        message[i : i + 1, :] = rows[i]


def unpack(place, mine, other, count, stride, ordered, put):
    core = place[2]
    for f in range(count):
        own = mine[pl.ds(f, 128, stride=stride), :]
        theirs = other[pl.ds(f, 128, stride=stride), :]
        ordered[f, pl.ds(0, 128, stride=2), :] = jnp.where(core == 0, own, theirs)
        ordered[f, pl.ds(1, 128, stride=2), :] = jnp.where(core == 0, theirs, own)
    sub = lax.broadcasted_iota(jnp.int32, (8, LANES), 0)
    part = lane_ids(8) >> 4

    for z in range(8):
        for f in range(count):
            for group in range(4):
                x = ordered[f, pl.ds(z * 32 + 8 * group, 8), :]
                for k in (4, 2, 1):
                    same = (sub & k) == (part & k)
                    ahead = pltpu.roll(pltpu.roll(x, 8 - k, 0), 16 * k, 1)
                    if k == 4:
                        moved = ahead
                    else:
                        behind = pltpu.roll(pltpu.roll(x, k, 0), LANES - 16 * k, 1)
                        moved = jnp.where((sub & k) == 0, ahead, behind)
                    x = jnp.where(same, x, moved)
                put(f, PAD + 8 * z, group, x)


def halving(kind):
    lane = lax.broadcasted_iota(jnp.int32, (2 * LANES, LANES), 0)
    place = lax.broadcasted_iota(jnp.int32, (2 * LANES, LANES), 1)
    if kind == "sum":
        hit = (lane >> 1) == place
    elif kind == "low":
        hit = lane == 2 * place
    else:
        hit = lane == 2 * place + 1
    return jnp.where(hit, 1.0, 0.0).astype(F32)


def doubling():
    place = lax.broadcasted_iota(jnp.int32, (LANES, 2 * LANES), 0)
    lane = lax.broadcasted_iota(jnp.int32, (LANES, 2 * LANES), 1)
    return jnp.where((lane >> 1) == place, 1.0, 0.0).astype(F32)


def folded(halves, matrix):
    if len(halves) == 1:
        return [exact_dot(halves[0], matrix[:LANES])]
    return [
        exact_dot(jnp.concatenate(halves[i : i + 2], axis=1), matrix)
        for i in range(0, len(halves), 2)
    ]


WHOLE = {3: (4, 64, 1), 4: (2, 32, 0), 5: (1, 16, 0), 6: (1, 8, 0)}


def whole_maps(level, raw, maps):
    halves, rows, first = WHOLE[level]
    size = rows

    def body(start):
        at = pl.ds(start, size)
        lane = lane_ids(size)
        for i in range(halves):
            scaled, scale, inverse = scaled_maps(
                [raw[m, first + i, at, :] for m in range(4)], 0.5**level
            )
            if i == 0:
                scaled[LEFT] = jnp.where(lane == 0, 0.0, scaled[LEFT])
            if i == halves - 1:
                last = 63 if level == 6 else LANES - 1
                scaled[RIGHT] = jnp.where(lane == last, 0.0, scaled[RIGHT])
            for m in range(4):
                maps[m, first + i, at, :] = scaled[m]
            maps[SCALE, first + i, at, :] = scale
            maps[INVERSE, first + i, at, :] = inverse

    chunks(0, rows, size, body)


def coarsen_whole(level, raw, next_raw):
    halves, rows, first = WHOLE[level]
    next_halves, next_rows, next_first = WHOLE[level + 1]
    for m in range(4):
        parts = []
        for h in range(halves):
            even, odd = even_odd(raw, (m, first + h), PAD, next_rows)
            parts.append(even if m == UP else odd if m == DOWN else even + odd)
        kind = "sum" if m in (UP, DOWN) else "low" if m == LEFT else "high"
        for h, x in enumerate(folded(parts, halving(kind))):
            next_raw[m, next_first + h, PAD : PAD + next_rows, :] = 0.5 * x


def one_sweep(maps):
    coef = [maps[m, 0, PAD : PAD + 8, :] for m in range(4)]
    row = lax.broadcasted_iota(jnp.int32, (8, LANES), 0)
    coef[UP] = jnp.where(row == 0, 0.0, coef[UP])
    coef[DOWN] = jnp.where(row == 7, 0.0, coef[DOWN])
    steps = ((-1, 0), (1, 0), (0, -1), (0, 1))
    return dict(zip(steps, coef))


def moved(x, rows, columns):
    if rows:
        x = pltpu.roll(x, (-rows) % 8, 0)
    if columns:
        x = pltpu.roll(x, (-columns) % LANES, 1)
    return x


DIAMOND = [(a, b) for a in range(-4, 5) for b in range(-4, 5) if abs(a) + abs(b) <= 4]


def four_sweeps(maps, product):
    sweep = one_sweep(maps)
    whole = dict(sweep)
    whole[0, 0] = jnp.full((8, LANES), 1.0 - RELAX_WEIGHT, F32)
    for _ in range(3):
        grown = {at: (1.0 - RELAX_WEIGHT) * x for at, x in whole.items()}
        for step, coef in sweep.items():
            for at, x in whole.items():
                place = (at[0] + step[0], at[1] + step[1])
                term = coef * moved(x, *step)
                grown[place] = grown[place] + term if place in grown else term
        whole = grown
    for i, at in enumerate(DIAMOND):
        product[i] = moved(whole[at], -at[0], 0)


def coarse_solve(base, maps, product):
    sweep = one_sweep(maps)
    right_side = [base[c, 0, PAD : PAD + 8, :] for c in range(CHANNELS)]
    first = right_side
    for _ in range(3):
        first = [
            (1.0 - RELAX_WEIGHT) * v + g + sum(coef * moved(v, *at) for at, coef in sweep.items())
            for v, g in zip(first, right_side)
        ]
    values = first
    for _ in range(COARSE_SWEEPS // 4 - 1):
        lanes = [[moved(v, 0, b) for b in range(-4, 5)] for v in values]
        totals = [list() for _ in range(CHANNELS)]
        for a in range(-4, 5):
            sums = [None] * CHANNELS
            for i, at in enumerate(DIAMOND):
                if at[0] == a:
                    coef = product[i]
                    for c in range(CHANNELS):
                        term = coef * lanes[c][at[1] + 4]
                        sums[c] = term if sums[c] is None else sums[c] + term
            for c in range(CHANNELS):
                totals[c].append(moved(sums[c], a, 0))
        values = []
        for c in range(CHANNELS):
            t = totals[c]
            even = (t[0] + t[1]) + (t[2] + t[3])
            odd = (t[5] + t[6]) + (t[7] + t[8])
            values.append((first[c] + t[4]) + (even + odd))
    return values


def whole_cycle(level, bases, fields, others, maps, product):
    halves, rows, first = WHOLE[level]
    base, field, other, level_maps = bases[level], fields[level], others[level], maps[level]
    size = rows
    stencil("first", field, base, base, level_maps, 0, rows, size, 1, halves, first)
    stencil("residual", other, field, base, level_maps, 0, rows, size, 1, halves, first)
    next_halves, next_rows, next_first = WHOLE[level + 1]
    summed = []
    for h in range(halves):
        parts = []
        for c in range(CHANNELS):
            even, odd = even_odd(other, (c, first + h), PAD, next_rows)
            parts.append(even + odd)
        summed.append(jnp.concatenate(parts, axis=0))
    for h, x in enumerate(folded(summed, halving("sum"))):
        inverse = 0.25 * maps[level + 1][INVERSE, next_first + h, PAD : PAD + next_rows, :]
        for c in range(CHANNELS):
            part = x[c * next_rows : (c + 1) * next_rows]
            bases[level + 1][c, next_first + h, PAD : PAD + next_rows, :] = part * inverse
    if level == 5:
        coarse = coarse_solve(bases[6], maps[6], product)
        coarse = [jnp.concatenate(coarse, axis=0)]
    else:
        whole_cycle(level + 1, bases, fields, others, maps, product)
        coarse = [
            jnp.concatenate(
                [
                    fields[level + 1][c, next_first + h, PAD : PAD + next_rows, :]
                    for c in range(CHANNELS)
                ],
                axis=0,
            )
            for h in range(next_halves)
        ]
    for m, x in enumerate(coarse):
        wide = exact_dot(x, doubling())
        for i in range(min(halves, 2)):
            h = first + 2 * m + i
            for c in range(CHANNELS):
                part = wide[c * next_rows : (c + 1) * next_rows, LANES * i : LANES * (i + 1)]
                for offset in range(2):
                    at = pl.ds(PAD + offset, next_rows, stride=2)
                    field[c, h, at, :] = field[c, h, at, :] + part
    if level > 3:
        stencil("relax", other, field, base, level_maps, 0, rows, size, 1, halves, first)
        stencil("relax", field, other, base, level_maps, 0, rows, size, 1, halves, first)


def window(ref, index, place):
    group = lax.shift_right_logical(place[1], 3)
    offset = 16 * (place[1] & 7)
    at = pl.ds(pl.multiple_of(8 * place[0], 8), 24)
    lane = lane_ids(24)
    turn = lax.rem(LANES - offset, LANES)
    before, here, after = [pltpu.roll(ref[index, group + i, at, :], turn, 1) for i in range(3)]
    low = lane < 64
    fits = lane + offset < LANES
    return jnp.where(low, jnp.where(fits, here, after), jnp.where(fits, before, here))


def spread_matrix():
    place = lax.broadcasted_iota(jnp.int32, (LANES, 2 * LANES), 0)
    lane = lax.broadcasted_iota(jnp.int32, (LANES, 2 * LANES), 1)
    source = lane >> 3
    source = jnp.where(lane >= 192, source + 96, source)
    return jnp.where(place == source, 1.0, 0.0).astype(F32)


def correct_level_two(place, bases, fields, maps, f2, near_maps, near_base, near_a, near_b):
    for m in range(4):
        near_maps[m, 0, PAD : PAD + 24, :] = window(maps[3], m, place)
    edge = jnp.zeros((PAD, LANES), F32)
    for c in range(CHANNELS):
        near_base[c, 0, PAD : PAD + 24, :] = window(bases[3], c, place)
        near_a[c, 0, PAD : PAD + 24, :] = window(fields[3], c, place)
        for ref in (near_a, near_b):
            ref[c, 0, 0:PAD, :] = edge
            ref[c, 0, PAD + 24 : PAD + 32, :] = edge
    stencil("relax", near_b, near_a, near_base, near_maps, 0, 24, 24, 1, 1)
    stencil("relax", near_a, near_b, near_base, near_maps, 0, 24, 24, 1, 1)
    flat = jnp.concatenate([near_a[c, 0, PAD : PAD + 24, :] for c in range(CHANNELS)], axis=0)
    wide = exact_dot(flat, spread_matrix())
    for c in range(CHANNELS):
        for h in range(2):
            part = wide[24 * c : 24 * c + 24, LANES * h : LANES * h + LANES]
            for offset in range(2):
                at = pl.ds(PAD + offset, 24, stride=2)
                f2[c, h, at, :] = f2[c, h, at, :] + part


def add_rows(field, coarse, low, high, size):
    def body(start):
        for c in range(CHANNELS):
            for h in range(2):
                part = coarse[c, h, pl.ds(start, size), :]
                for offset in range(2):
                    at = pl.ds(2 * start - PAD + offset, size, stride=2)
                    field[c, h, at, :] = field[c, h, at, :] + part

    chunks(low, high, size, body)


def up_levels(ranges, fields, bases, works, maps, extra):
    low, high, size = ranges[2]
    stencil("relax", works[2], fields[2], bases[2], maps[2], low, high, size, 4)
    stencil("relax", fields[2], works[2], bases[2], maps[2], low, high, size, 4)
    add_rows(fields[1], fields[2], 0, 48, 48)
    low, high, size = ranges[1]
    stencil("relax", works[1], fields[1], bases[1], maps[1], low, high, size, 2)
    stencil("relax", fields[1], works[1], bases[1], maps[1], low, high, size, 2)
    add_rows(fields[0], fields[1], 0, 96, 96)
    low, high, size = ranges[0]
    stencil("relax", works[0], fields[0], bases[0], maps[0], low, high, size, 1)
    if extra is None:
        stencil("relax", fields[0], works[0], bases[0], maps[0], low, high, size, 1)
    else:
        stencil(
            "relax_add", fields[0], works[0], bases[0], maps[0], low, high, size, 1, extra=extra
        )


def copy_field(source, target):
    count, halves, rows, _ = source.shape
    for c in range(count):
        for h in range(halves):
            target[c, h] = source[c, h]


def complete_maps(raw):
    size = 64
    at = pl.ds(PAD, size)
    lane = lane_ids(size)
    row = lax.broadcasted_iota(jnp.int32, (size, LANES), 0)
    ends = [raw[RIGHT, h, at, :] for h in range(1, 5)]
    shifted = beside([raw[LEFT, h, at, :] for h in range(1, 5)], 1)[1]
    last = ends[3]
    last = jnp.where((row & 7) == 7, pltpu.roll(pltpu.roll(last, 1, 1), 1, 0), last)
    shifted[3] = jnp.where(lane == LANES - 1, last, shifted[3])
    for i in range(4):
        below = raw[UP, 1 + i, pl.ds(PAD + 1, size), :]
        raw[DOWN, 1 + i, at, :] = jnp.where(row == size - 1, ends[i], below)
        raw[RIGHT, 1 + i, at, :] = shifted[i]


def middle_kernel(
    place, mine, other, m0, m1, m2, source, f0, g1, f1, g2, f2,
    m3, m4, m5, m6, product, solution, n0, h0, k1, h1, k2, h2, message,
    ordered, raw3, raw4, raw5, raw6, b3, v3, o3, b4, v4, o4, b5, v5, o5, b6,
    w0, w1, w2, near_maps, near_base, near_a, near_b,
):
    for ref in (m3, raw3, b3, v3, o3):
        rows = ref.shape[2]
        clear(ref, (0, PAD), (rows - PAD, rows))
        for index in range(ref.shape[0]):
            for h in (0, 5):
                ref[index, h] = jnp.zeros((rows, LANES), F32)
    for ref in (b4, v4, o4, b5, v5, o5):
        rows = ref.shape[2]
        clear(ref, (0, PAD), (rows - PAD, rows))
    for ref in (w0, w1, w2, n0):
        rows = ref.shape[2]
        clear(ref, (0, rows))

    def put(f, start, group, tile):
        if f < CHANNELS:
            b3[f, 1 + group, pl.ds(start, 8), :] = tile
        else:
            slot = (UP, LEFT, RIGHT)[f - CHANNELS]
            raw3[slot, 1 + group, pl.ds(start, 8), :] = tile

    unpack(place, mine, other, 6, 6, ordered, put)
    complete_maps(raw3)
    raws = {3: raw3, 4: raw4, 5: raw5, 6: raw6}
    maps = {3: m3, 4: m4, 5: m5, 6: m6}
    whole_maps(3, raw3, m3)
    for level in (3, 4, 5):
        coarsen_whole(level, raws[level], raws[level + 1])
        whole_maps(level + 1, raws[level + 1], maps[level + 1])
    four_sweeps(m6, product)
    scale_base(b3, m3)
    whole_cycle(
        3, {3: b3, 4: b4, 5: b5, 6: b6}, {3: v3, 4: v4, 5: v5}, {3: o3, 4: o4, 5: o5}, maps,
        product,
    )
    copy_field(f0, solution)
    copy_field(f1, h1)
    copy_field(f2, h2)
    correct_level_two(
        place, {3: b3}, {3: v3}, maps, h2, near_maps, near_base, near_a, near_b
    )
    local_maps = (m0, m1, m2)
    up_levels(FIRST_UP, (solution, h1, h2), (source, g1, g2), (w0, w1, w2), local_maps, None)
    stencil("difference", n0, solution, source, m0, 32, 160, 128, 1)
    for ref in (h0, k1, k2):
        rows = ref.shape[2]
        clear(ref, (0, rows))
    tiles = down_levels((h0, h1, h2), (n0, k1, k2), (w0, w1, w2), local_maps, LATER_DOWN)
    rows = own_row(jnp.concatenate(tiles, axis=0))
    for i in range(CHANNELS):
        message[i : i + 1, :] = rows[i]


def scale_base(base, maps):
    halves, rows, first = WHOLE[3]

    def body(start):
        at = pl.ds(start, rows)
        for i in range(halves):
            inverse = maps[INVERSE, first + i, at, :]
            for c in range(CHANNELS):
                base[c, first + i, at, :] = base[c, first + i, at, :] * inverse

    chunks(0, rows, rows, body)


def last_kernel(
    place, mine, other, m0, m1, m2, source, m3, m4, m5, m6, product, before, n0, f0, k1, f1, k2, f2,
    solution, residual,
    ordered, b3, v3, o3, b4, v4, o4, b5, v5, o5, b6,
    h0, h1, h2, w0, w1, w2, near_maps, near_base, near_a, near_b,
):
    for ref in (b3, v3, o3):
        rows = ref.shape[2]
        clear(ref, (0, PAD), (rows - PAD, rows))
        for index in range(ref.shape[0]):
            for h in (0, 5):
                ref[index, h] = jnp.zeros((rows, LANES), F32)
    for ref in (b4, v4, o4, b5, v5, o5):
        rows = ref.shape[2]
        clear(ref, (0, PAD), (rows - PAD, rows))
    for ref in (w0, w1, w2):
        rows = ref.shape[2]
        clear(ref, (0, rows))

    def put(f, start, group, tile):
        b3[f, 1 + group, pl.ds(start, 8), :] = tile

    unpack(place, mine, other, CHANNELS, CHANNELS, ordered, put)
    maps = {3: m3, 4: m4, 5: m5, 6: m6}
    scale_base(b3, m3)
    whole_cycle(
        3, {3: b3, 4: b4, 5: b5, 6: b6}, {3: v3, 4: v4, 5: v5}, {3: o3, 4: o4, 5: o5}, maps,
        product,
    )
    copy_field(f0, h0)
    copy_field(f1, h1)
    copy_field(f2, h2)
    correct_level_two(
        place, {3: b3}, {3: v3}, maps, h2, near_maps, near_base, near_a, near_b
    )
    local_maps = (m0, m1, m2)
    up_levels(LATER_UP, (h0, h1, h2), (n0, k1, k2), (w0, w1, w2), local_maps, before)
    stencil("final", w0, h0, source, m0, 64, 128, 64, 1)
    for c in range(CHANNELS):
        solution[c] = h0[c, 0, PAD + 64 : PAD + 128, :]
        residual[c] = w0[c, 0, PAD + 64 : PAD + 128, :]


def shape(*dims):
    return jax.ShapeDtypeStruct(dims, F32)


def field_shape(level, count):
    return (count, 2, LOCAL_ROWS[level] + 2 * PAD, LANES)


def whole_shape(level, count):
    halves, rows, first = WHOLE[level]
    return (count, halves + 2 * first, rows + 2 * PAD, LANES)


def call(kernel, outs, scratch, *args):
    in_specs = [pl.BlockSpec(memory_space=pltpu.VMEM) for _ in args]
    if args[0].dtype == jnp.int32 and args[0].ndim == 1:
        in_specs[0] = pl.BlockSpec(memory_space=pltpu.SMEM)
    return pl.pallas_call(
        kernel,
        out_shape=[shape(*o) for o in outs],
        in_specs=in_specs,
        out_specs=[pl.BlockSpec(memory_space=pltpu.VMEM) for _ in outs],
        scratch_shapes=[pltpu.VMEM(s, F32) for s in scratch],
        compiler_params=pltpu.CompilerParams(vmem_limit_bytes=14 * 1024 * 1024),
    )(*args)


def ring(count, step):
    return [(i, (i + step) % count) for i in range(count)]


def gathered(message):
    rows = message.shape[0]
    sent = jnp.broadcast_to(message.reshape(1, 1, rows * LANES), (128, 1, rows * LANES))
    mine = lax.all_to_all(sent, CHIPS, 0, 0, tiled=True)
    mine = mine.reshape(128 * rows, LANES)
    return mine, lax.ppermute(mine, "core", ring(2, 1))


def local(guidance, seam_weight, source_label):
    place = jnp.stack(
        [lax.axis_index("z"), lax.axis_index(SIDES), lax.axis_index("core")]
    ).astype(jnp.int32)
    own, upper, lower = pl.pallas_call(
        stack_kernel,
        out_shape=[shape(8, 64, LANES), shape(8, REACH, LANES), shape(8, REACH, LANES)],
        in_specs=[pl.BlockSpec(memory_space=pltpu.HBM)] * 3,
        out_specs=[pl.BlockSpec(memory_space=pltpu.VMEM)] * 3,
        scratch_shapes=[
            pltpu.VMEM((2, CHANNELS, 64, LANES), F32),
            pltpu.VMEM((64, LANES), jnp.int32),
            pltpu.VMEM((64, LANES), jnp.int32),
            pltpu.SemaphoreType.DMA((3,)),
        ],
        compiler_params=pltpu.CompilerParams(vmem_limit_bytes=58 * 1024 * 1024),
    )(guidance, seam_weight, source_label)
    above = lax.ppermute(lower, "z", ring(8, 1))
    below = lax.ppermute(upper, "z", ring(8, -1))
    to_left, to_right = call(
        pack_kernel, [(8, 88, LANES)] * 2, [], own, above, below
    )
    from_right = lax.ppermute(to_left, SIDES, ring(32, -1))
    from_left = lax.ppermute(to_right, SIDES, ring(32, 1))
    fields = [field_shape(level, CHANNELS) for level in range(3)]
    maps = [field_shape(0, 5), field_shape(1, 6), field_shape(2, 6)]
    raws = [field_shape(level, 4) for level in range(3)]
    m0, m1, m2, source, f0, g1, f1, g2, f2, message = call(
        setup_kernel,
        maps + [fields[0], fields[0], fields[1], fields[1], fields[2], fields[2], (6, LANES)],
        [field_shape(0, 8)] + raws + fields,
        place, own, above, below, from_right, from_left,
    )
    mine, other = gathered(message)
    wholes = [whole_shape(level, CHANNELS) for level in (3, 4, 5) for _ in range(3)]
    wholes = wholes + [whole_shape(6, CHANNELS)]
    near = [(4, 1, 40, LANES)] + [(CHANNELS, 1, 40, LANES)] * 3
    m3, m4, m5, m6, product, solution, n0, h0, k1, h1, k2, h2, message = call(
        middle_kernel,
        [whole_shape(level, 6) for level in (3, 4, 5, 6)]
        + [(len(DIAMOND), 8, LANES)] + [fields[0]] * 3 + [fields[1]] * 2 + [fields[2]] * 2 + [(CHANNELS, LANES)],
        [(6, 256, LANES)] + [whole_shape(level, 4) for level in (3, 4, 5, 6)]
        + wholes + fields + near,
        place, mine, other, m0, m1, m2, source, f0, g1, f1, g2, f2,
    )
    mine, other = gathered(message)
    outs = call(
        last_kernel,
        [(CHANNELS, 64, LANES)] * 2,
        [(CHANNELS, 256, LANES)] + wholes + fields + fields + near,
        place, mine, other, m0, m1, m2, source, m3, m4, m5, m6, product,
        solution, n0, h0, k1, h1, k2, h2,
    )
    return tuple(outs)


def solution(mesh):
    fine = Mesh(mesh.devices.reshape(8, 4, 4, 2), ("z", "y", "x", "core"))
    return jax.shard_map(
        local,
        mesh=fine,
        in_specs=(P(None, None, "z", SIDES), P("z", SIDES), P("z", SIDES)),
        out_specs=(P(None, "z", SIDES), P(None, "z", SIDES)),
        check_vma=False,
    )
```

```python
import jax
import jax.numpy as jnp
from jax import lax
from jax.experimental import pallas as pl
from jax.experimental.pallas import tpu as pltpu
from jax.sharding import Mesh, PartitionSpec as P

F32 = jnp.float32
CHANNELS = 3
COARSE_SWEEPS = 48
RELAX_WEIGHT = 0.8
SEAM_FACTOR = 0.25
PAD = 8
LANES = 128
REACH = 56
SIDES = ("y", "x", "core")
CHIPS = ("z", "y", "x")
LOCAL_ROWS = (192, 96, 48)
UP, DOWN, LEFT, RIGHT, SCALE, INVERSE = range(6)


def lane_ids(rows):
    return lax.broadcasted_iota(jnp.int32, (rows, LANES), 1)


def beside(halves, width):
    count = len(halves)
    lane = lane_ids(halves[0].shape[0])
    ahead = [pltpu.roll(x, width, 1) for x in halves]
    behind = [pltpu.roll(x, LANES - width, 1) for x in halves]
    if count == 1:
        return ahead, behind
    left = [jnp.where(lane < width, ahead[h - 1], ahead[h]) for h in range(count)]
    right = [
        jnp.where(lane >= LANES - width, behind[(h + 1) % count], behind[h]) for h in range(count)
    ]
    return left, right


def pair_sum(x, width):
    low = (lane_ids(x.shape[0]) & width) == 0
    return x + jnp.where(low, pltpu.roll(x, LANES - width, 1), pltpu.roll(x, width, 1))


def low_of_pair(x, width):
    low = (lane_ids(x.shape[0]) & width) == 0
    return jnp.where(low, x, pltpu.roll(x, width, 1))


def high_of_pair(x, width):
    low = (lane_ids(x.shape[0]) & width) == 0
    return jnp.where(low, pltpu.roll(x, LANES - width, 1), x)


def picked(x, lanes):
    return jnp.take_along_axis(x, lanes, axis=1, mode="promise_in_bounds")


def chunks(low, high, size, body):
    count = (high - low) // size
    assert count * size == high - low

    def step(i, carry):
        body(pl.multiple_of(PAD + low + i * size, 8))
        return carry

    if count == 1:
        body(PAD + low)
    else:
        lax.fori_loop(0, count, step, 0)


def stencil(mode, target, field, base, maps, low, high, size, width=1, halves=2, first=0, extra=None):
    def body(start):
        at = pl.ds(start, size)
        span = range(first, first + halves)
        coef = [[maps[m, h, at, :] for h in span] for m in range(4)]
        for c in range(CHANNELS):
            here = [field[c, h, at, :] for h in span]
            above = [field[c, h, pl.ds(start - 1, size), :] for h in span]
            below = [field[c, h, pl.ds(start + 1, size), :] for h in span]
            left, right = beside(here, width)
            for i, h in enumerate(span):
                near = (above[i], below[i], left[i], right[i])
                if mode in ("difference", "scaled_difference", "final"):
                    near = [n - here[i] for n in near]
                total = coef[0][i] * near[0] + coef[1][i] * near[1]
                total = total + (coef[2][i] * near[2] + coef[3][i] * near[3])
                if mode == "first":
                    result = (2.0 - RELAX_WEIGHT) * here[i] + total
                elif mode == "relax":
                    result = (1.0 - RELAX_WEIGHT) * here[i] + base[c, h, at, :] + total
                elif mode == "relax_add":
                    result = (1.0 - RELAX_WEIGHT) * here[i] + base[c, h, at, :] + total
                    result = extra[c, h, at, :] + result
                elif mode == "residual":
                    result = base[c, h, at, :] - RELAX_WEIGHT * here[i] + total
                    result = maps[SCALE, h, at, :] * result
                elif mode == "difference":
                    result = base[c, h, at, :] + total
                else:
                    result = maps[SCALE, h, at, :] * (base[c, h, at, :] + total)
                target[c, h, at, :] = result

    chunks(low, high, size, body)


def scaled_maps(raw, factor):
    whole = raw[0] + raw[1] + raw[2] + raw[3]
    inside = whole > 0.0
    share = jnp.where(inside, RELAX_WEIGHT / jnp.where(inside, whole, 1.0), 0.0)
    return [r * share for r in raw], whole * (factor / RELAX_WEIGHT), share * (1.0 / factor)


def even_odd(ref, lead, start, count):
    return (
        ref[lead + (pl.ds(start, count, stride=2), slice(None))],
        ref[lead + (pl.ds(start + 1, count, stride=2), slice(None))],
    )


FIELDS = 5
WEIGHT, LABEL = 3, 4
UPDOWN_ROWS = FIELDS * REACH + 8
SIDE_ROWS = FIELDS * 88 + 16


def stack_kernel(guidance_in, weight_in, label_in, down, up, guidance, weight_at, label_at, arrived):
    copies = [
        pltpu.make_async_copy(source, target, arrived.at[i])
        for i, (source, target) in enumerate(
            ((guidance_in, guidance), (weight_in, weight_at), (label_in, label_at))
        )
    ]
    for copy in copies:
        copy.start()
    for copy in copies:
        copy.wait()
    weight, label = weight_at[...].astype(F32), label_at[...].astype(F32)
    row = lax.broadcasted_iota(jnp.int32, (64, LANES), 0)
    lane = lane_ids(64)

    def edge(turn, axis, inside):
        matching = jnp.where(pltpu.roll(label, turn, axis) == label, 1.0 / 64.0, SEAM_FACTOR / 64.0)
        return jnp.where(inside, (weight + pltpu.roll(weight, turn, axis)) * matching, 0.0)

    below, right = edge(63, 0, row < 63), edge(LANES - 1, 1, lane < LANES - 1)

    def put(a, x):
        down[REACH * a : REACH * (a + 1), :] = x[64 - REACH :]
        up[REACH * a : REACH * (a + 1), :] = x[:REACH]

    ends = [guidance[0, c, 63:64, :] for c in range(CHANNELS)]
    for c in range(CHANNELS):
        first, second = below * guidance[0, c], right * guidance[1, c]
        put(c, (pltpu.roll(first, 1, 0) - first) + (pltpu.roll(second, 1, 1) - second))
        last = jnp.broadcast_to(guidance[1, c, :, LANES - 1 :], (64, LANES))
        ends.append(jnp.sum(jnp.where(row == lane, last, 0.0), axis=0, keepdims=True))
    put(WEIGHT, weight)
    put(LABEL, label)
    ends = jnp.concatenate(ends + [jnp.zeros((2, LANES), F32)], axis=0)
    down[FIELDS * REACH :, :] = ends
    up[FIELDS * REACH :, :] = ends


def own_kernel(down, up, own, ends):
    for a in range(FIELDS):
        own[a, :REACH, :] = up[REACH * a : REACH * (a + 1), :]
        own[a, REACH:, :] = down[REACH * (a + 1) - (64 - REACH) : REACH * (a + 1), :]
    ends[...] = up[FIELDS * REACH :, :]


def upright(row, first, count):
    hit = lane_ids(count) == first + lax.broadcasted_iota(jnp.int32, (count, LANES), 0)
    return jnp.sum(jnp.where(hit, jnp.broadcast_to(row, (count, LANES)), 0.0), axis=1, keepdims=True)


def pack_kernel(place, own, ends, above, below, swap, side, edge):
    first_core = place[2] == 0
    low = lane_ids(88) < 64
    base = FIELDS * REACH

    def halves(x):
        return x[:88], pltpu.roll(x[88:], 64, 1)

    for a in range(FIELDS):
        at = slice(REACH * a, REACH * (a + 1))
        whole = jnp.concatenate([above[at, :], own[a], below[at, :]], axis=0)
        top, bottom = halves(whole)
        to_left = jnp.where(low, top, bottom)
        if a < CHANNELS:
            column = jnp.concatenate(
                [
                    upright(above[base + 3 + a : base + 4 + a, :], 64 - REACH, REACH),
                    upright(ends[3 + a : 4 + a, :], 0, 64),
                    upright(below[base + 3 + a : base + 4 + a, :], 0, REACH),
                ],
                axis=0,
            )
            column = jnp.broadcast_to(column, (176, LANES))
            edge[a] = column
            top, bottom = halves(jnp.where(lane_ids(176) == 64, column, whole))
        to_right = jnp.where(low, bottom, top)
        at = slice(88 * a, 88 * (a + 1))
        swap[at, :] = jnp.where(first_core, to_right, to_left)
        side[at, :] = jnp.where(first_core, to_left, to_right)
    for ref in (swap, side):
        ref[88 * FIELDS : 88 * FIELDS + 8, :] = above[base:, :]
        ref[88 * FIELDS + 8 :, :] = ends[...]


def local_down(level, field, base, work, maps, next_base, next_maps, first_rows, rest_rows, next_rows):
    width = 2**level
    low, high, size = first_rows
    stencil("first", field, base, base, maps, low, high, size, width)
    low, high, size = rest_rows
    stencil("scaled_difference", work, field, base, maps, low, high, size, width)
    if next_base is None:
        return

    low, high, size = next_rows

    def body(start):
        at = pl.ds(start, size)
        for h in range(2):
            inverse = 0.25 * next_maps[INVERSE, h, at, :]
            for c in range(CHANNELS):
                even, odd = even_odd(work, (c, h), 2 * start - PAD, size)
                next_base[c, h, at, :] = pair_sum(even + odd, width) * inverse

    chunks(low, high, size, body)


def own_row(x):
    count = x.shape[0] // 8
    spread = picked(x, 8 * (lane_ids(x.shape[0]) & 15))
    rows = []
    keep = (lane_ids(8) >> 4) == lax.broadcasted_iota(jnp.int32, (8, LANES), 0)
    for i in range(count):
        part = jnp.where(keep, spread[8 * i : 8 * i + 8], 0.0)
        rows.append(jnp.sum(part, axis=0, keepdims=True))
    return rows


def down_levels(fields, bases, work, maps, ranges):
    for level in range(3):
        local_down(
            level,
            fields[level],
            bases[level],
            work[level],
            maps[level],
            bases[level + 1] if level < 2 else None,
            maps[level + 1] if level < 2 else None,
            *ranges[level],
        )
    tiles = []
    for c in range(CHANNELS):
        even, odd = even_odd(work[2], (c, 0), PAD + 16, 8)
        tiles.append(0.25 * pair_sum(even + odd, 4))
    return tiles


FIRST_DOWN = (
    ((8, 184, 176), (8, 184, 176), (0, 96, 96)),
    ((0, 96, 96), (0, 96, 96), (0, 48, 48)),
    ((0, 48, 48), (0, 48, 48), None),
)
LATER_DOWN = (
    ((32, 160, 128), (32, 160, 128), (16, 80, 64)),
    ((16, 80, 64), (16, 80, 64), (8, 40, 32)),
    ((8, 40, 32), (8, 40, 32), None),
)
FIRST_UP = ((32, 160, 128), (8, 88, 80), (0, 48, 48))
LATER_UP = ((56, 136, 80), (24, 72, 48), (8, 40, 32))


def clear(ref, *bounds):
    for index in range(ref.shape[0]):
        for h in range(ref.shape[1]):
            for low, high in bounds:
                ref[index, h, low:high, :] = jnp.zeros((high - low, LANES), F32)


def setup_kernel(
    place, own, ends, above, below, swapped, sided, border,
    m0, m1, m2, source, f0, g1, f1, g2, f2, message,
    cells, raw0, raw1, raw2, w0, w1, w2,
):
    row_at, col_at, first_core = place[0], place[1], place[2] == 0
    rows_of = lambda n, low: low + lax.broadcasted_iota(jnp.int32, (n, LANES), 0)
    edge = jnp.zeros((16, LANES), F32)
    not_top, not_bottom = row_at > 0, row_at < 7
    low = lane_ids(88) < 64
    inside = (low & (col_at < 31)) | (~low & (col_at > 0))

    def sides(start, size):
        one, two = swapped[start : start + size, :], sided[start : start + size, :]
        return jnp.where(first_core, one, two), jnp.where(first_core, two, one)

    for a in range(FIELDS):
        at = slice(REACH * a, REACH * (a + 1))
        for h in range(2):
            cells[a, h, 0:16, :] = edge
            cells[a, h, 192:208, :] = edge
        cells[a, 0, 16:72, :] = jnp.where(not_top, above[at, :], 0.0)
        cells[a, 0, 72:136, :] = own[a]
        cells[a, 0, 136:192, :] = jnp.where(not_bottom, below[at, :], 0.0)
        from_right, from_left = sides(88 * a, 88)
        top = jnp.where(low, from_right, from_left)
        bottom = pltpu.roll(jnp.where(low, from_left, from_right), 64, 1)
        cells[a, 1, 16:104, :] = jnp.where(inside & (not_top | (rows_of(88, 8) >= 64)), top, 0.0)
        cells[a, 1, 104:192, :] = jnp.where(
            inside & (not_bottom | (rows_of(88, 96) < 128)), bottom, 0.0
        )
    for ref in (m0, raw0, source, f0, w0):
        clear(ref, (0, 16), (192, 208))
    for ref, rows in ((m1, 96), (raw1, 96), (g1, 96), (f1, 96), (w1, 96)):
        clear(ref, (0, 8), (rows + 8, rows + 16))
    for ref, rows in ((m2, 48), (raw2, 48), (g2, 48), (f2, 48), (w2, 48)):
        clear(ref, (0, 8), (rows + 8, rows + 16))

    def fine(start):
        size = 176
        at = pl.ds(start, size)
        up_at, down_at = pl.ds(start - 1, size), pl.ds(start + 1, size)
        weights = [cells[WEIGHT, h, at, :] for h in range(2)]
        labels = [cells[LABEL, h, at, :] for h in range(2)]
        weight_sides = beside(weights, 1)
        label_sides = beside(labels, 1)
        coef, shares = [], []
        for h in range(2):
            near_weights = (
                cells[WEIGHT, h, up_at, :], cells[WEIGHT, h, down_at, :], weight_sides[0][h], weight_sides[1][h],
            )
            near_labels = (
                cells[LABEL, h, up_at, :], cells[LABEL, h, down_at, :], label_sides[0][h], label_sides[1][h],
            )
            raw = []
            for m in range(4):
                matching = jnp.where(near_labels[m] == labels[h], 1.0 / 64.0, SEAM_FACTOR / 64.0)
                value = (weights[h] + near_weights[m]) * matching
                value = jnp.where(weights[h] > 0.0, value, 0.0)
                raw.append(value)
                raw0[m, h, at, :] = value
            scaled, scale, share = scaled_maps(raw, 1.0)
            shares.append(share)
            for m in range(4):
                m0[m, h, at, :] = scaled[m]
            m0[SCALE, h, at, :] = scale
            coef.append(scaled)
        for c in range(CHANNELS):
            part = [cells[c, h, at, :] for h in range(2)]
            own_end = border[c]
            left_end = pltpu.roll(part[1], 64, 1), pltpu.roll(part[1], 63, 1)
            first, last = lane_ids(size) == 0, lane_ids(size) == LANES - 1
            flux = jnp.where(first, coef[0][LEFT] * left_end[0], 0.0)
            flux = flux - jnp.where(last, coef[0][RIGHT] * own_end, 0.0)
            source[c, 0, at, :] = shares[0] * part[0] + flux
            flux = jnp.where(first, coef[1][LEFT] * own_end, 0.0)
            flux = flux - jnp.where(last, coef[1][RIGHT] * left_end[1], 0.0)
            source[c, 1, at, :] = shares[1] * part[1] + flux

    chunks(8, 184, 176, fine)
    from_right, from_left = sides(88 * FIELDS, 16)
    beside_own = jnp.where(lane_ids(16) < 64, from_right, from_left)
    for first, upper in ((0, 71), (8, 135)):
        for c in range(CHANNELS):
            if first == 0:
                straight = above[FIELDS * REACH + c : FIELDS * REACH + c + 1, :]
            else:
                straight = ends[c : c + 1, :]
            for h, flow in ((0, straight), (1, beside_own[first + c : first + c + 1])):
                if first == 0:
                    flow = jnp.where(not_top, flow, 0.0)
                one, two = pl.ds(upper, 1), pl.ds(upper + 1, 1)
                source[c, h, one, :] = source[c, h, one, :] - m0[DOWN, h, one, :] * flow
                source[c, h, two, :] = source[c, h, two, :] + m0[UP, h, two, :] * flow

    def coarser(raw, width, start, size, h):
        parts = []
        for m in range(4):
            even, odd = even_odd(raw, (m, h), start, size)
            if m == UP:
                parts.append(0.5 * pair_sum(even, width))
            elif m == DOWN:
                parts.append(0.5 * pair_sum(odd, width))
            elif m == LEFT:
                parts.append(0.5 * low_of_pair(even + odd, width))
            else:
                parts.append(0.5 * high_of_pair(even + odd, width))
        return parts

    for level, fine_raw, raw, maps, rows in ((1, raw0, raw1, m1, 96), (2, raw1, raw2, m2, 48)):

        def coarse(start, level=level, fine_raw=fine_raw, raw=raw, maps=maps, rows=rows):
            size = rows
            at = pl.ds(start, size)
            for h in range(2):
                parts = coarser(fine_raw, 2 ** (level - 1), 2 * start - PAD, size, h)
                scaled, scale, inverse = scaled_maps(parts, 0.5**level)
                for m in range(4):
                    raw[m, h, at, :] = parts[m]
                    maps[m, h, at, :] = scaled[m]
                maps[SCALE, h, at, :] = scale
                maps[INVERSE, h, at, :] = inverse

        chunks(0, rows, rows, coarse)
    tiles = down_levels((f0, f1, f2), (source, g1, g2), (w0, w1, w2), (m0, m1, m2), FIRST_DOWN)
    upward, downward, leftward, rightward = coarser(raw2, 4, PAD + 16, 8, 0)
    row = lax.broadcasted_iota(jnp.int32, (8, LANES), 0)
    cell = lane_ids(8) >> 3
    turned = pltpu.roll(pltpu.roll(rightward, LANES - 8, 1), 7, 0)
    ends = jnp.where(row == 7, downward, jnp.where(cell == 15, rightward, turned))
    rows = own_row(jnp.concatenate(tiles + [upward, leftward, ends], axis=0))
    for i in range(6):
        message[i : i + 1, :] = rows[i]


def unpack(place, mine, other, count, stride, ordered, put):
    core = place[2]
    for f in range(count):
        own = mine[pl.ds(f, 128, stride=stride), :]
        theirs = other[pl.ds(f, 128, stride=stride), :]
        ordered[f, pl.ds(0, 128, stride=2), :] = jnp.where(core == 0, own, theirs)
        ordered[f, pl.ds(1, 128, stride=2), :] = jnp.where(core == 0, theirs, own)
    sub = lax.broadcasted_iota(jnp.int32, (8, LANES), 0)
    part = lane_ids(8) >> 4

    for z in range(8):
        for f in range(count):
            for group in range(4):
                x = ordered[f, pl.ds(z * 32 + 8 * group, 8), :]
                for k in (4, 2, 1):
                    same = (sub & k) == (part & k)
                    ahead = pltpu.roll(pltpu.roll(x, 8 - k, 0), 16 * k, 1)
                    if k == 4:
                        moved = ahead
                    else:
                        behind = pltpu.roll(pltpu.roll(x, k, 0), LANES - 16 * k, 1)
                        moved = jnp.where((sub & k) == 0, ahead, behind)
                    x = jnp.where(same, x, moved)
                put(f, PAD + 8 * z, group, x)


def folded(halves, kind):
    lane = lane_ids(halves[0].shape[0])
    even = (2 * lane) & (LANES - 1)

    def one(x):
        if kind == "low":
            return picked(x, even)
        if kind == "high":
            return picked(x, even + 1)
        return picked(x, even) + picked(x, even + 1)

    parts = [one(x) for x in halves]
    if len(parts) == 1:
        parts.append(jnp.zeros_like(parts[0]))
    return [jnp.where(lane < 64, parts[i], parts[i + 1]) for i in range(0, len(parts), 2)]


def doubled(x):
    lane = lane_ids(x.shape[0])
    return [picked(x, lane >> 1), picked(x, 64 + (lane >> 1))]


WHOLE = {3: (4, 64, 1), 4: (2, 32, 0), 5: (1, 16, 0), 6: (1, 8, 0)}


def whole_maps(level, raw, maps):
    halves, rows, first = WHOLE[level]
    size = rows

    def body(start):
        at = pl.ds(start, size)
        lane = lane_ids(size)
        for i in range(halves):
            scaled, scale, inverse = scaled_maps(
                [raw[m, first + i, at, :] for m in range(4)], 0.5**level
            )
            if i == 0:
                scaled[LEFT] = jnp.where(lane == 0, 0.0, scaled[LEFT])
            if i == halves - 1:
                last = 63 if level == 6 else LANES - 1
                scaled[RIGHT] = jnp.where(lane == last, 0.0, scaled[RIGHT])
            for m in range(4):
                maps[m, first + i, at, :] = scaled[m]
            maps[SCALE, first + i, at, :] = scale
            maps[INVERSE, first + i, at, :] = inverse

    chunks(0, rows, size, body)


def coarsen_whole(level, raw, next_raw):
    halves, rows, first = WHOLE[level]
    next_halves, next_rows, next_first = WHOLE[level + 1]
    for m in range(4):
        parts = []
        for h in range(halves):
            even, odd = even_odd(raw, (m, first + h), PAD, next_rows)
            parts.append(even if m == UP else odd if m == DOWN else even + odd)
        kind = "sum" if m in (UP, DOWN) else "low" if m == LEFT else "high"
        for h, x in enumerate(folded(parts, kind)):
            next_raw[m, next_first + h, PAD : PAD + next_rows, :] = 0.5 * x


def one_sweep(maps):
    coef = [maps[m, 0, PAD : PAD + 8, :] for m in range(4)]
    row = lax.broadcasted_iota(jnp.int32, (8, LANES), 0)
    coef[UP] = jnp.where(row == 0, 0.0, coef[UP])
    coef[DOWN] = jnp.where(row == 7, 0.0, coef[DOWN])
    steps = ((-1, 0), (1, 0), (0, -1), (0, 1))
    return dict(zip(steps, coef))


def moved(x, rows, columns):
    if rows:
        x = pltpu.roll(x, (-rows) % 8, 0)
    if columns:
        x = pltpu.roll(x, (-columns) % LANES, 1)
    return x


DIAMOND = [(a, b) for a in range(-4, 5) for b in range(-4, 5) if abs(a) + abs(b) <= 4]


def four_sweeps(maps, product):
    sweep = one_sweep(maps)
    whole = dict(sweep)
    whole[0, 0] = jnp.full((8, LANES), 1.0 - RELAX_WEIGHT, F32)
    for _ in range(3):
        grown = {at: (1.0 - RELAX_WEIGHT) * x for at, x in whole.items()}
        for step, coef in sweep.items():
            for at, x in whole.items():
                place = (at[0] + step[0], at[1] + step[1])
                term = coef * moved(x, *step)
                grown[place] = grown[place] + term if place in grown else term
        whole = grown
    for i, at in enumerate(DIAMOND):
        product[i] = moved(whole[at], -at[0], 0)


def coarse_solve(base, maps, product):
    sweep = one_sweep(maps)
    right_side = [base[c, 0, PAD : PAD + 8, :] for c in range(CHANNELS)]
    first = right_side
    for _ in range(3):
        first = [
            (1.0 - RELAX_WEIGHT) * v + g + sum(coef * moved(v, *at) for at, coef in sweep.items())
            for v, g in zip(first, right_side)
        ]
    values = first
    for _ in range(COARSE_SWEEPS // 4 - 1):
        lanes = [[moved(v, 0, b) for b in range(-4, 5)] for v in values]
        totals = [list() for _ in range(CHANNELS)]
        for a in range(-4, 5):
            sums = [None] * CHANNELS
            for i, at in enumerate(DIAMOND):
                if at[0] == a:
                    coef = product[i]
                    for c in range(CHANNELS):
                        term = coef * lanes[c][at[1] + 4]
                        sums[c] = term if sums[c] is None else sums[c] + term
            for c in range(CHANNELS):
                totals[c].append(moved(sums[c], a, 0))
        values = []
        for c in range(CHANNELS):
            t = totals[c]
            even = (t[0] + t[1]) + (t[2] + t[3])
            odd = (t[5] + t[6]) + (t[7] + t[8])
            values.append((first[c] + t[4]) + (even + odd))
    return values


def whole_cycle(level, bases, fields, others, maps, product):
    halves, rows, first = WHOLE[level]
    base, field, other, level_maps = bases[level], fields[level], others[level], maps[level]
    size = rows
    stencil("first", field, base, base, level_maps, 0, rows, size, 1, halves, first)
    stencil("residual", other, field, base, level_maps, 0, rows, size, 1, halves, first)
    next_halves, next_rows, next_first = WHOLE[level + 1]
    summed = []
    for h in range(halves):
        parts = []
        for c in range(CHANNELS):
            even, odd = even_odd(other, (c, first + h), PAD, next_rows)
            parts.append(even + odd)
        summed.append(jnp.concatenate(parts, axis=0))
    for h, x in enumerate(folded(summed, "sum")):
        inverse = 0.25 * maps[level + 1][INVERSE, next_first + h, PAD : PAD + next_rows, :]
        for c in range(CHANNELS):
            part = x[c * next_rows : (c + 1) * next_rows]
            bases[level + 1][c, next_first + h, PAD : PAD + next_rows, :] = part * inverse
    if level == 5:
        coarse = coarse_solve(bases[6], maps[6], product)
        coarse = [jnp.concatenate(coarse, axis=0)]
    else:
        whole_cycle(level + 1, bases, fields, others, maps, product)
        coarse = [
            jnp.concatenate(
                [
                    fields[level + 1][c, next_first + h, PAD : PAD + next_rows, :]
                    for c in range(CHANNELS)
                ],
                axis=0,
            )
            for h in range(next_halves)
        ]
    for m, x in enumerate(coarse):
        wide = doubled(x)
        for i in range(min(halves, 2)):
            h = first + 2 * m + i
            for c in range(CHANNELS):
                part = wide[i][c * next_rows : (c + 1) * next_rows]
                for offset in range(2):
                    at = pl.ds(PAD + offset, next_rows, stride=2)
                    field[c, h, at, :] = field[c, h, at, :] + part
    if level > 3:
        stencil("relax", other, field, base, level_maps, 0, rows, size, 1, halves, first)
        stencil("relax", field, other, base, level_maps, 0, rows, size, 1, halves, first)


def window(ref, index, place):
    group = lax.shift_right_logical(place[1], 3)
    offset = 16 * (place[1] & 7)
    at = pl.ds(pl.multiple_of(8 * place[0], 8), 24)
    lane = lane_ids(24)
    turn = lax.rem(LANES - offset, LANES)
    before, here, after = [pltpu.roll(ref[index, group + i, at, :], turn, 1) for i in range(3)]
    low = lane < 64
    fits = lane + offset < LANES
    return jnp.where(low, jnp.where(fits, here, after), jnp.where(fits, before, here))


def correct_level_two(place, bases, fields, maps, f2, near_maps, near_base, near_a, near_b):
    for m in range(4):
        near_maps[m, 0, PAD : PAD + 24, :] = window(maps[3], m, place)
    edge = jnp.zeros((PAD, LANES), F32)
    for c in range(CHANNELS):
        near_base[c, 0, PAD : PAD + 24, :] = window(bases[3], c, place)
        near_a[c, 0, PAD : PAD + 24, :] = window(fields[3], c, place)
        for ref in (near_a, near_b):
            ref[c, 0, 0:PAD, :] = edge
            ref[c, 0, PAD + 24 : PAD + 32, :] = edge
    stencil("relax", near_b, near_a, near_base, near_maps, 0, 24, 24, 1, 1)
    stencil("relax", near_a, near_b, near_base, near_maps, 0, 24, 24, 1, 1)
    flat = jnp.concatenate([near_a[c, 0, PAD : PAD + 24, :] for c in range(CHANNELS)], axis=0)
    lane = lane_ids(flat.shape[0])
    wide = [picked(flat, lane >> 3), picked(flat, jnp.where(lane < 64, 16, 112) + (lane >> 3))]
    for c in range(CHANNELS):
        for h in range(2):
            part = wide[h][24 * c : 24 * c + 24]
            for offset in range(2):
                at = pl.ds(PAD + offset, 24, stride=2)
                f2[c, h, at, :] = f2[c, h, at, :] + part


def add_rows(field, coarse, low, high, size):
    def body(start):
        for c in range(CHANNELS):
            for h in range(2):
                part = coarse[c, h, pl.ds(start, size), :]
                for offset in range(2):
                    at = pl.ds(2 * start - PAD + offset, size, stride=2)
                    field[c, h, at, :] = field[c, h, at, :] + part

    chunks(low, high, size, body)


def up_levels(ranges, fields, bases, works, maps, extra):
    low, high, size = ranges[2]
    stencil("relax", works[2], fields[2], bases[2], maps[2], low, high, size, 4)
    stencil("relax", fields[2], works[2], bases[2], maps[2], low, high, size, 4)
    add_rows(fields[1], fields[2], 0, 48, 48)
    low, high, size = ranges[1]
    stencil("relax", works[1], fields[1], bases[1], maps[1], low, high, size, 2)
    stencil("relax", fields[1], works[1], bases[1], maps[1], low, high, size, 2)
    add_rows(fields[0], fields[1], 0, 96, 96)
    low, high, size = ranges[0]
    stencil("relax", works[0], fields[0], bases[0], maps[0], low, high, size, 1)
    if extra is None:
        stencil("relax", fields[0], works[0], bases[0], maps[0], low, high, size, 1)
    else:
        stencil(
            "relax_add", fields[0], works[0], bases[0], maps[0], low, high, size, 1, extra=extra
        )


def copy_field(source, target):
    count, halves, rows, _ = source.shape
    for c in range(count):
        for h in range(halves):
            target[c, h] = source[c, h]


def complete_maps(raw):
    size = 64
    at = pl.ds(PAD, size)
    lane = lane_ids(size)
    row = lax.broadcasted_iota(jnp.int32, (size, LANES), 0)
    ends = [raw[RIGHT, h, at, :] for h in range(1, 5)]
    shifted = beside([raw[LEFT, h, at, :] for h in range(1, 5)], 1)[1]
    last = ends[3]
    last = jnp.where((row & 7) == 7, pltpu.roll(pltpu.roll(last, 1, 1), 1, 0), last)
    shifted[3] = jnp.where(lane == LANES - 1, last, shifted[3])
    for i in range(4):
        below = raw[UP, 1 + i, pl.ds(PAD + 1, size), :]
        raw[DOWN, 1 + i, at, :] = jnp.where(row == size - 1, ends[i], below)
        raw[RIGHT, 1 + i, at, :] = shifted[i]


def middle_kernel(
    place, mine, other, m0, m1, m2, source, f0, g1, f1, g2, f2,
    m3, m4, m5, m6, product, solution, n0, h0, k1, h1, k2, h2, message,
    ordered, raw3, raw4, raw5, raw6, b3, v3, o3, b4, v4, o4, b5, v5, o5, b6,
    w0, w1, w2, near_maps, near_base, near_a, near_b,
):
    for ref in (m3, raw3, b3, v3, o3):
        rows = ref.shape[2]
        clear(ref, (0, PAD), (rows - PAD, rows))
        for index in range(ref.shape[0]):
            for h in (0, 5):
                ref[index, h] = jnp.zeros((rows, LANES), F32)
    for ref in (b4, v4, o4, b5, v5, o5):
        rows = ref.shape[2]
        clear(ref, (0, PAD), (rows - PAD, rows))
    for ref in (w0, w1, w2, n0):
        rows = ref.shape[2]
        clear(ref, (0, rows))

    def put(f, start, group, tile):
        if f < CHANNELS:
            b3[f, 1 + group, pl.ds(start, 8), :] = tile
        else:
            slot = (UP, LEFT, RIGHT)[f - CHANNELS]
            raw3[slot, 1 + group, pl.ds(start, 8), :] = tile

    unpack(place, mine, other, 6, 6, ordered, put)
    complete_maps(raw3)
    raws = {3: raw3, 4: raw4, 5: raw5, 6: raw6}
    maps = {3: m3, 4: m4, 5: m5, 6: m6}
    whole_maps(3, raw3, m3)
    for level in (3, 4, 5):
        coarsen_whole(level, raws[level], raws[level + 1])
        whole_maps(level + 1, raws[level + 1], maps[level + 1])
    four_sweeps(m6, product)
    scale_base(b3, m3)
    whole_cycle(
        3, {3: b3, 4: b4, 5: b5, 6: b6}, {3: v3, 4: v4, 5: v5}, {3: o3, 4: o4, 5: o5}, maps,
        product,
    )
    copy_field(f0, solution)
    copy_field(f1, h1)
    copy_field(f2, h2)
    correct_level_two(
        place, {3: b3}, {3: v3}, maps, h2, near_maps, near_base, near_a, near_b
    )
    local_maps = (m0, m1, m2)
    up_levels(FIRST_UP, (solution, h1, h2), (source, g1, g2), (w0, w1, w2), local_maps, None)
    stencil("difference", n0, solution, source, m0, 32, 160, 128, 1)
    for ref in (h0, k1, k2):
        rows = ref.shape[2]
        clear(ref, (0, rows))
    tiles = down_levels((h0, h1, h2), (n0, k1, k2), (w0, w1, w2), local_maps, LATER_DOWN)
    rows = own_row(jnp.concatenate(tiles, axis=0))
    for i in range(CHANNELS):
        message[i : i + 1, :] = rows[i]


def scale_base(base, maps):
    halves, rows, first = WHOLE[3]

    def body(start):
        at = pl.ds(start, rows)
        for i in range(halves):
            inverse = maps[INVERSE, first + i, at, :]
            for c in range(CHANNELS):
                base[c, first + i, at, :] = base[c, first + i, at, :] * inverse

    chunks(0, rows, rows, body)


def last_kernel(
    place, mine, other, m0, m1, m2, source, m3, m4, m5, m6, product, before, n0, f0, k1, f1, k2, f2,
    solution, residual,
    ordered, b3, v3, o3, b4, v4, o4, b5, v5, o5, b6,
    h0, h1, h2, w0, w1, w2, near_maps, near_base, near_a, near_b,
):
    for ref in (b3, v3, o3):
        rows = ref.shape[2]
        clear(ref, (0, PAD), (rows - PAD, rows))
        for index in range(ref.shape[0]):
            for h in (0, 5):
                ref[index, h] = jnp.zeros((rows, LANES), F32)
    for ref in (b4, v4, o4, b5, v5, o5):
        rows = ref.shape[2]
        clear(ref, (0, PAD), (rows - PAD, rows))
    for ref in (w0, w1, w2):
        rows = ref.shape[2]
        clear(ref, (0, rows))

    def put(f, start, group, tile):
        b3[f, 1 + group, pl.ds(start, 8), :] = tile

    unpack(place, mine, other, CHANNELS, CHANNELS, ordered, put)
    maps = {3: m3, 4: m4, 5: m5, 6: m6}
    scale_base(b3, m3)
    whole_cycle(
        3, {3: b3, 4: b4, 5: b5, 6: b6}, {3: v3, 4: v4, 5: v5}, {3: o3, 4: o4, 5: o5}, maps,
        product,
    )
    copy_field(f0, h0)
    copy_field(f1, h1)
    copy_field(f2, h2)
    correct_level_two(
        place, {3: b3}, {3: v3}, maps, h2, near_maps, near_base, near_a, near_b
    )
    local_maps = (m0, m1, m2)
    up_levels(LATER_UP, (h0, h1, h2), (n0, k1, k2), (w0, w1, w2), local_maps, before)
    stencil("final", w0, h0, source, m0, 64, 128, 64, 1)
    for c in range(CHANNELS):
        solution[c] = h0[c, 0, PAD + 64 : PAD + 128, :]
        residual[c] = w0[c, 0, PAD + 64 : PAD + 128, :]


def shape(*dims):
    return jax.ShapeDtypeStruct(dims, F32)


def field_shape(level, count):
    return (count, 2, LOCAL_ROWS[level] + 2 * PAD, LANES)


def whole_shape(level, count):
    halves, rows, first = WHOLE[level]
    return (count, halves + 2 * first, rows + 2 * PAD, LANES)


def call(kernel, outs, scratch, *args):
    in_specs = [pl.BlockSpec(memory_space=pltpu.VMEM) for _ in args]
    if args[0].dtype == jnp.int32 and args[0].ndim == 1:
        in_specs[0] = pl.BlockSpec(memory_space=pltpu.SMEM)
    return pl.pallas_call(
        kernel,
        out_shape=[shape(*o) for o in outs],
        in_specs=in_specs,
        out_specs=[pl.BlockSpec(memory_space=pltpu.VMEM) for _ in outs],
        scratch_shapes=[pltpu.VMEM(s, F32) for s in scratch],
        compiler_params=pltpu.CompilerParams(vmem_limit_bytes=14 * 1024 * 1024),
        cost_estimate=pl.CostEstimate(flops=0, bytes_accessed=8_000_000, transcendentals=0),
    )(*args)


def ring(count, step):
    return [(i, (i + step) % count) for i in range(count)]


def gathered(message):
    rows = message.shape[0]
    sent = jnp.broadcast_to(message.reshape(1, 1, rows * LANES), (128, 1, rows * LANES))
    mine = lax.all_to_all(sent, CHIPS, 0, 0, tiled=True)
    mine = mine.reshape(128 * rows, LANES)
    return mine, lax.ppermute(mine, "core", ring(2, 1))


def local(guidance, seam_weight, source_label):
    place = jnp.stack(
        [lax.axis_index("z"), lax.axis_index(SIDES), lax.axis_index("core")]
    ).astype(jnp.int32)
    down, up = pl.pallas_call(
        stack_kernel,
        out_shape=[shape(UPDOWN_ROWS, LANES)] * 2,
        in_specs=[pl.BlockSpec(memory_space=pltpu.HBM)] * 3,
        out_specs=[pl.BlockSpec(memory_space=pltpu.VMEM)] * 2,
        scratch_shapes=[
            pltpu.VMEM((2, CHANNELS, 64, LANES), F32),
            pltpu.VMEM((64, LANES), jnp.int32),
            pltpu.VMEM((64, LANES), jnp.int32),
            pltpu.SemaphoreType.DMA((3,)),
        ],
        compiler_params=pltpu.CompilerParams(vmem_limit_bytes=58 * 1024 * 1024),
    )(guidance, seam_weight, source_label)
    above = lax.ppermute(down, "z", ring(8, 1))
    below = lax.ppermute(up, "z", ring(8, -1))
    own, ends = call(own_kernel, [(FIELDS, 64, LANES), (8, LANES)], [], down, up)
    swap, side, border = call(
        pack_kernel,
        [(SIDE_ROWS, LANES)] * 2 + [(CHANNELS, 176, LANES)],
        [],
        place, own, ends, above, below,
    )
    swapped = lax.ppermute(swap, "core", ring(2, 1))
    pairs = [(i, min(max(i + 2 * (i % 2) - 1, 0), 31)) for i in range(32)]
    sided = lax.ppermute(side, SIDES, pairs)
    fields = [field_shape(level, CHANNELS) for level in range(3)]
    maps = [field_shape(0, 5), field_shape(1, 6), field_shape(2, 6)]
    raws = [field_shape(level, 4) for level in range(3)]
    m0, m1, m2, source, f0, g1, f1, g2, f2, message = call(
        setup_kernel,
        maps + [fields[0], fields[0], fields[1], fields[1], fields[2], fields[2], (6, LANES)],
        [field_shape(0, FIELDS)] + raws + fields,
        place, own, ends, above, below, swapped, sided, border,
    )
    mine, other = gathered(message)
    wholes = [whole_shape(level, CHANNELS) for level in (3, 4, 5) for _ in range(3)]
    wholes = wholes + [whole_shape(6, CHANNELS)]
    near = [(4, 1, 40, LANES)] + [(CHANNELS, 1, 40, LANES)] * 3
    m3, m4, m5, m6, product, solution, n0, h0, k1, h1, k2, h2, message = call(
        middle_kernel,
        [whole_shape(level, 6) for level in (3, 4, 5, 6)]
        + [(len(DIAMOND), 8, LANES)] + [fields[0]] * 3 + [fields[1]] * 2 + [fields[2]] * 2 + [(CHANNELS, LANES)],
        [(6, 256, LANES)] + [whole_shape(level, 4) for level in (3, 4, 5, 6)]
        + wholes + fields + near,
        place, mine, other, m0, m1, m2, source, f0, g1, f1, g2, f2,
    )
    mine, other = gathered(message)
    outs = call(
        last_kernel,
        [(CHANNELS, 64, LANES)] * 2,
        [(CHANNELS, 256, LANES)] + wholes + fields + fields + near,
        place, mine, other, m0, m1, m2, source, m3, m4, m5, m6, product,
        solution, n0, h0, k1, h1, k2, h2,
    )
    return tuple(outs)


def solution(mesh):
    fine = Mesh(mesh.devices.reshape(8, 4, 4, 2), ("z", "y", "x", "core"))
    return jax.shard_map(
        local,
        mesh=fine,
        in_specs=(P(None, None, "z", SIDES), P("z", SIDES), P("z", SIDES)),
        out_specs=(P(None, "z", SIDES), P(None, "z", SIDES)),
        check_vma=False,
    )
```

```python
import jax
import jax.numpy as jnp
from jax import lax
from jax.experimental import pallas as pl
from jax.experimental.pallas import tpu as pltpu
from jax.sharding import Mesh, PartitionSpec as P

F32 = jnp.float32
CHANNELS = 3
COARSE_SWEEPS = 48
RELAX_WEIGHT = 0.8
SEAM_FACTOR = 0.25
PAD = 8
LANES = 128
REACH = 56
SIDES = ("y", "x", "core")
CHIPS = ("z", "y", "x")
LOCAL_ROWS = (192, 96, 48)
UP, DOWN, LEFT, RIGHT, SCALE, INVERSE = range(6)


def lane_ids(rows):
    return lax.broadcasted_iota(jnp.int32, (rows, LANES), 1)


def beside(halves, width):
    count = len(halves)
    lane = lane_ids(halves[0].shape[0])
    ahead = [pltpu.roll(x, width, 1) for x in halves]
    behind = [pltpu.roll(x, LANES - width, 1) for x in halves]
    if count == 1:
        return ahead, behind
    left = [jnp.where(lane < width, ahead[h - 1], ahead[h]) for h in range(count)]
    right = [
        jnp.where(lane >= LANES - width, behind[(h + 1) % count], behind[h]) for h in range(count)
    ]
    return left, right


def pair_sum(x, width):
    low = (lane_ids(x.shape[0]) & width) == 0
    return x + jnp.where(low, pltpu.roll(x, LANES - width, 1), pltpu.roll(x, width, 1))


def low_of_pair(x, width):
    low = (lane_ids(x.shape[0]) & width) == 0
    return jnp.where(low, x, pltpu.roll(x, width, 1))


def high_of_pair(x, width):
    low = (lane_ids(x.shape[0]) & width) == 0
    return jnp.where(low, pltpu.roll(x, LANES - width, 1), x)


def picked(x, lanes):
    return jnp.take_along_axis(x, lanes, axis=1, mode="promise_in_bounds")


def chunks(low, high, size, body):
    count = (high - low) // size
    assert count * size == high - low

    def step(i, carry):
        body(pl.multiple_of(PAD + low + i * size, 8))
        return carry

    if count == 1:
        body(PAD + low)
    else:
        lax.fori_loop(0, count, step, 0)


def stencil(mode, target, field, base, maps, low, high, size, width=1, halves=2, first=0, extra=None):
    def body(start):
        at = pl.ds(start, size)
        span = range(first, first + halves)
        coef = [[maps[m, h, at, :] for h in span] for m in range(4)]
        for c in range(CHANNELS):
            here = [field[c, h, at, :] for h in span]
            above = [field[c, h, pl.ds(start - 1, size), :] for h in span]
            below = [field[c, h, pl.ds(start + 1, size), :] for h in span]
            left, right = beside(here, width)
            for i, h in enumerate(span):
                near = (above[i], below[i], left[i], right[i])
                if mode in ("difference", "scaled_difference", "final"):
                    near = [n - here[i] for n in near]
                total = coef[0][i] * near[0] + coef[1][i] * near[1]
                total = total + (coef[2][i] * near[2] + coef[3][i] * near[3])
                if mode == "first":
                    result = (2.0 - RELAX_WEIGHT) * here[i] + total
                elif mode == "relax":
                    result = (1.0 - RELAX_WEIGHT) * here[i] + base[c, h, at, :] + total
                elif mode == "relax_add":
                    result = (1.0 - RELAX_WEIGHT) * here[i] + base[c, h, at, :] + total
                    result = extra[c, h, at, :] + result
                elif mode == "residual":
                    result = base[c, h, at, :] - RELAX_WEIGHT * here[i] + total
                    result = maps[SCALE, h, at, :] * result
                elif mode == "difference":
                    result = base[c, h, at, :] + total
                else:
                    result = maps[SCALE, h, at, :] * (base[c, h, at, :] + total)
                target[c, h, at, :] = result

    chunks(low, high, size, body)


def scaled_maps(raw, factor):
    whole = raw[0] + raw[1] + raw[2] + raw[3]
    inside = whole > 0.0
    share = jnp.where(inside, RELAX_WEIGHT / jnp.where(inside, whole, 1.0), 0.0)
    return [r * share for r in raw], whole * (factor / RELAX_WEIGHT), share * (1.0 / factor)


def even_odd(ref, lead, start, count):
    return (
        ref[lead + (pl.ds(start, count, stride=2), slice(None))],
        ref[lead + (pl.ds(start + 1, count, stride=2), slice(None))],
    )


FIELDS = 5
WEIGHT, LABEL = 3, 4
UPDOWN_ROWS = FIELDS * REACH + 8
SIDE_ROWS = FIELDS * 88 + 16


def stack_kernel(guidance_in, weight_in, label_in, down, up, guidance, weight_at, label_at, arrived):
    copies = [
        pltpu.make_async_copy(source, target, arrived.at[i])
        for i, (source, target) in enumerate(
            ((guidance_in, guidance), (weight_in, weight_at), (label_in, label_at))
        )
    ]
    for copy in copies:
        copy.start()
    for copy in copies:
        copy.wait()
    weight, label = weight_at[...].astype(F32), label_at[...].astype(F32)
    row = lax.broadcasted_iota(jnp.int32, (64, LANES), 0)
    lane = lane_ids(64)

    def edge(turn, axis, inside):
        matching = jnp.where(pltpu.roll(label, turn, axis) == label, 1.0 / 64.0, SEAM_FACTOR / 64.0)
        return jnp.where(inside, (weight + pltpu.roll(weight, turn, axis)) * matching, 0.0)

    below, right = edge(63, 0, row < 63), edge(LANES - 1, 1, lane < LANES - 1)

    def put(a, x):
        down[REACH * a : REACH * (a + 1), :] = x[64 - REACH :]
        up[REACH * a : REACH * (a + 1), :] = x[:REACH]

    ends = [guidance[0, c, 63:64, :] for c in range(CHANNELS)]
    for c in range(CHANNELS):
        first, second = below * guidance[0, c], right * guidance[1, c]
        put(c, (pltpu.roll(first, 1, 0) - first) + (pltpu.roll(second, 1, 1) - second))
        last = jnp.broadcast_to(guidance[1, c, :, LANES - 1 :], (64, LANES))
        ends.append(jnp.sum(jnp.where(row == lane, last, 0.0), axis=0, keepdims=True))
    put(WEIGHT, weight)
    put(LABEL, label)
    ends = jnp.concatenate(ends + [jnp.zeros((2, LANES), F32)], axis=0)
    down[FIELDS * REACH :, :] = ends
    up[FIELDS * REACH :, :] = ends


def own_kernel(down, up, own, ends):
    for a in range(FIELDS):
        own[a, :REACH, :] = up[REACH * a : REACH * (a + 1), :]
        own[a, REACH:, :] = down[REACH * (a + 1) - (64 - REACH) : REACH * (a + 1), :]
    ends[...] = up[FIELDS * REACH :, :]


def upright(row, first, count):
    place = first + lax.broadcasted_iota(jnp.int32, (count, LANES), 0)
    return picked(jnp.broadcast_to(row, (count, LANES)), place)


def pack_kernel(place, own, ends, above, below, swap, side, edge):
    first_core = place[2] == 0
    low = lane_ids(88) < 64
    base = FIELDS * REACH

    def halves(x):
        return x[:88], pltpu.roll(x[88:], 64, 1)

    for a in range(FIELDS):
        at = slice(REACH * a, REACH * (a + 1))
        whole = jnp.concatenate([above[at, :], own[a], below[at, :]], axis=0)
        top, bottom = halves(whole)
        to_left = jnp.where(low, top, bottom)
        if a < CHANNELS:
            column = jnp.concatenate(
                [
                    upright(above[base + 3 + a : base + 4 + a, :], 64 - REACH, REACH),
                    upright(ends[3 + a : 4 + a, :], 0, 64),
                    upright(below[base + 3 + a : base + 4 + a, :], 0, REACH),
                ],
                axis=0,
            )
            edge[a] = column
            top, bottom = halves(jnp.where(lane_ids(176) == 64, column, whole))
        to_right = jnp.where(low, bottom, top)
        at = slice(88 * a, 88 * (a + 1))
        swap[at, :] = jnp.where(first_core, to_right, to_left)
        side[at, :] = jnp.where(first_core, to_left, to_right)
    for ref in (swap, side):
        ref[88 * FIELDS : 88 * FIELDS + 8, :] = above[base:, :]
        ref[88 * FIELDS + 8 :, :] = ends[...]


def local_down(level, field, base, work, maps, next_base, next_maps, first_rows, rest_rows, next_rows):
    width = 2**level
    low, high, size = first_rows
    stencil("first", field, base, base, maps, low, high, size, width)
    low, high, size = rest_rows
    stencil("scaled_difference", work, field, base, maps, low, high, size, width)
    if next_base is None:
        return

    low, high, size = next_rows

    def body(start):
        at = pl.ds(start, size)
        for h in range(2):
            inverse = 0.25 * next_maps[INVERSE, h, at, :]
            for c in range(CHANNELS):
                even, odd = even_odd(work, (c, h), 2 * start - PAD, size)
                next_base[c, h, at, :] = pair_sum(even + odd, width) * inverse

    chunks(low, high, size, body)


def own_row(x):
    count = x.shape[0] // 8
    spread = picked(x, 8 * (lane_ids(x.shape[0]) & 15))
    rows = []
    keep = (lane_ids(8) >> 4) == lax.broadcasted_iota(jnp.int32, (8, LANES), 0)
    for i in range(count):
        part = jnp.where(keep, spread[8 * i : 8 * i + 8], 0.0)
        rows.append(jnp.sum(part, axis=0, keepdims=True))
    return rows


def down_levels(fields, bases, work, maps, ranges):
    for level in range(3):
        local_down(
            level,
            fields[level],
            bases[level],
            work[level],
            maps[level],
            bases[level + 1] if level < 2 else None,
            maps[level + 1] if level < 2 else None,
            *ranges[level],
        )
    tiles = []
    for c in range(CHANNELS):
        even, odd = even_odd(work[2], (c, 0), PAD + 16, 8)
        tiles.append(0.25 * pair_sum(even + odd, 4))
    return tiles


FIRST_DOWN = (
    ((8, 184, 176), (8, 184, 176), (0, 96, 96)),
    ((0, 96, 96), (0, 96, 96), (0, 48, 48)),
    ((0, 48, 48), (0, 48, 48), None),
)
LATER_DOWN = (
    ((32, 160, 128), (32, 160, 128), (16, 80, 64)),
    ((16, 80, 64), (16, 80, 64), (8, 40, 32)),
    ((8, 40, 32), (8, 40, 32), None),
)
FIRST_UP = ((32, 160, 128), (8, 88, 80), (0, 48, 48))
LATER_UP = ((56, 136, 80), (24, 72, 48), (8, 40, 32))


def clear(ref, *bounds):
    for index in range(ref.shape[0]):
        for h in range(ref.shape[1]):
            for low, high in bounds:
                ref[index, h, low:high, :] = jnp.zeros((high - low, LANES), F32)


def setup_kernel(
    place, own, ends, above, below, swapped, sided, border,
    m0, m1, m2, source, f0, g1, f1, g2, f2, message,
    cells, raw0, raw1, raw2, w0, w1, w2,
):
    row_at, col_at, first_core = place[0], place[1], place[2] == 0
    rows_of = lambda n, low: low + lax.broadcasted_iota(jnp.int32, (n, LANES), 0)
    edge = jnp.zeros((16, LANES), F32)
    not_top, not_bottom = row_at > 0, row_at < 7
    low = lane_ids(88) < 64
    inside = (low & (col_at < 31)) | (~low & (col_at > 0))

    def sides(start, size):
        one, two = swapped[start : start + size, :], sided[start : start + size, :]
        return jnp.where(first_core, one, two), jnp.where(first_core, two, one)

    for a in range(FIELDS):
        at = slice(REACH * a, REACH * (a + 1))
        for h in range(2):
            cells[a, h, 0:16, :] = edge
            cells[a, h, 192:208, :] = edge
        cells[a, 0, 16:72, :] = jnp.where(not_top, above[at, :], 0.0)
        cells[a, 0, 72:136, :] = own[a]
        cells[a, 0, 136:192, :] = jnp.where(not_bottom, below[at, :], 0.0)
        from_right, from_left = sides(88 * a, 88)
        top = jnp.where(low, from_right, from_left)
        bottom = pltpu.roll(jnp.where(low, from_left, from_right), 64, 1)
        cells[a, 1, 16:104, :] = jnp.where(inside & (not_top | (rows_of(88, 8) >= 64)), top, 0.0)
        cells[a, 1, 104:192, :] = jnp.where(
            inside & (not_bottom | (rows_of(88, 96) < 128)), bottom, 0.0
        )
    for ref in (m0, raw0, source, f0, w0):
        clear(ref, (0, 16), (192, 208))
    for ref, rows in ((m1, 96), (raw1, 96), (g1, 96), (f1, 96), (w1, 96)):
        clear(ref, (0, 8), (rows + 8, rows + 16))
    for ref, rows in ((m2, 48), (raw2, 48), (g2, 48), (f2, 48), (w2, 48)):
        clear(ref, (0, 8), (rows + 8, rows + 16))

    def fine(start):
        size = 176
        at = pl.ds(start, size)
        up_at, down_at = pl.ds(start - 1, size), pl.ds(start + 1, size)
        weights = [cells[WEIGHT, h, at, :] for h in range(2)]
        labels = [cells[LABEL, h, at, :] for h in range(2)]
        weight_sides = beside(weights, 1)
        label_sides = beside(labels, 1)
        coef, shares = [], []
        for h in range(2):
            near_weights = (
                cells[WEIGHT, h, up_at, :], cells[WEIGHT, h, down_at, :], weight_sides[0][h], weight_sides[1][h],
            )
            near_labels = (
                cells[LABEL, h, up_at, :], cells[LABEL, h, down_at, :], label_sides[0][h], label_sides[1][h],
            )
            raw = []
            for m in range(4):
                matching = jnp.where(near_labels[m] == labels[h], 1.0 / 64.0, SEAM_FACTOR / 64.0)
                value = (weights[h] + near_weights[m]) * matching
                value = jnp.where(weights[h] > 0.0, value, 0.0)
                raw.append(value)
                raw0[m, h, at, :] = value
            scaled, scale, share = scaled_maps(raw, 1.0)
            shares.append(share)
            for m in range(4):
                m0[m, h, at, :] = scaled[m]
            m0[SCALE, h, at, :] = scale
            coef.append(scaled)
        for c in range(CHANNELS):
            part = [cells[c, h, at, :] for h in range(2)]
            own_end = border[c]
            left_end = pltpu.roll(part[1], 64, 1), pltpu.roll(part[1], 63, 1)
            first, last = lane_ids(size) == 0, lane_ids(size) == LANES - 1
            flux = jnp.where(first, coef[0][LEFT] * left_end[0], 0.0)
            flux = flux - jnp.where(last, coef[0][RIGHT] * own_end, 0.0)
            source[c, 0, at, :] = shares[0] * part[0] + flux
            flux = jnp.where(first, coef[1][LEFT] * own_end, 0.0)
            flux = flux - jnp.where(last, coef[1][RIGHT] * left_end[1], 0.0)
            source[c, 1, at, :] = shares[1] * part[1] + flux

    chunks(8, 184, 176, fine)
    from_right, from_left = sides(88 * FIELDS, 16)
    beside_own = jnp.where(lane_ids(16) < 64, from_right, from_left)
    for first, upper in ((0, 71), (8, 135)):
        for c in range(CHANNELS):
            if first == 0:
                straight = above[FIELDS * REACH + c : FIELDS * REACH + c + 1, :]
            else:
                straight = ends[c : c + 1, :]
            for h, flow in ((0, straight), (1, beside_own[first + c : first + c + 1])):
                if first == 0:
                    flow = jnp.where(not_top, flow, 0.0)
                one, two = pl.ds(upper, 1), pl.ds(upper + 1, 1)
                source[c, h, one, :] = source[c, h, one, :] - m0[DOWN, h, one, :] * flow
                source[c, h, two, :] = source[c, h, two, :] + m0[UP, h, two, :] * flow

    def coarser(raw, width, start, size, h):
        parts = []
        for m in range(4):
            even, odd = even_odd(raw, (m, h), start, size)
            if m == UP:
                parts.append(0.5 * pair_sum(even, width))
            elif m == DOWN:
                parts.append(0.5 * pair_sum(odd, width))
            elif m == LEFT:
                parts.append(0.5 * low_of_pair(even + odd, width))
            else:
                parts.append(0.5 * high_of_pair(even + odd, width))
        return parts

    for level, fine_raw, raw, maps, rows in ((1, raw0, raw1, m1, 96), (2, raw1, raw2, m2, 48)):

        def coarse(start, level=level, fine_raw=fine_raw, raw=raw, maps=maps, rows=rows):
            size = rows
            at = pl.ds(start, size)
            for h in range(2):
                parts = coarser(fine_raw, 2 ** (level - 1), 2 * start - PAD, size, h)
                scaled, scale, inverse = scaled_maps(parts, 0.5**level)
                for m in range(4):
                    raw[m, h, at, :] = parts[m]
                    maps[m, h, at, :] = scaled[m]
                maps[SCALE, h, at, :] = scale
                maps[INVERSE, h, at, :] = inverse

        chunks(0, rows, rows, coarse)
    tiles = down_levels((f0, f1, f2), (source, g1, g2), (w0, w1, w2), (m0, m1, m2), FIRST_DOWN)
    upward, downward, leftward, rightward = coarser(raw2, 4, PAD + 16, 8, 0)
    row = lax.broadcasted_iota(jnp.int32, (8, LANES), 0)
    cell = lane_ids(8) >> 3
    turned = pltpu.roll(pltpu.roll(rightward, LANES - 8, 1), 7, 0)
    ends = jnp.where(row == 7, downward, jnp.where(cell == 15, rightward, turned))
    rows = own_row(jnp.concatenate(tiles + [upward, leftward, ends], axis=0))
    for i in range(6):
        message[i : i + 1, :] = rows[i]


def unpack(place, mine, other, count, stride, ordered, put):
    core = place[2]
    for f in range(count):
        own = mine[pl.ds(f, 128, stride=stride), :]
        theirs = other[pl.ds(f, 128, stride=stride), :]
        ordered[f, pl.ds(0, 128, stride=2), :] = jnp.where(core == 0, own, theirs)
        ordered[f, pl.ds(1, 128, stride=2), :] = jnp.where(core == 0, theirs, own)
    sub = lax.broadcasted_iota(jnp.int32, (8, LANES), 0)
    part, cell = lane_ids(8) >> 4, lane_ids(8) & 15
    first = (((sub - part) & 7) << 4) + cell
    last = (((part - sub) & 7) << 4) + cell
    for z in range(8):
        for f in range(count):
            for group in range(4):
                x = picked(ordered[f, pl.ds(z * 32 + 8 * group, 8), :], first)
                for k in (1, 2, 4):
                    x = jnp.where((part & k) != 0, pltpu.roll(x, 8 - k, 0), x)
                put(f, PAD + 8 * z, group, picked(x, last))


def folded(halves, kind):
    lane = lane_ids(halves[0].shape[0])
    even = (2 * lane) & (LANES - 1)

    def one(x):
        if kind == "low":
            return picked(x, even)
        if kind == "high":
            return picked(x, even + 1)
        return picked(x, even) + picked(x, even + 1)

    parts = [one(x) for x in halves]
    if len(parts) == 1:
        parts.append(jnp.zeros_like(parts[0]))
    return [jnp.where(lane < 64, parts[i], parts[i + 1]) for i in range(0, len(parts), 2)]


def doubled(x):
    lane = lane_ids(x.shape[0])
    return [picked(x, lane >> 1), picked(x, 64 + (lane >> 1))]


WHOLE = {3: (4, 64, 1), 4: (2, 32, 0), 5: (1, 16, 0), 6: (1, 8, 0)}


def whole_maps(level, raw, maps):
    halves, rows, first = WHOLE[level]
    size = rows

    def body(start):
        at = pl.ds(start, size)
        lane = lane_ids(size)
        for i in range(halves):
            scaled, scale, inverse = scaled_maps(
                [raw[m, first + i, at, :] for m in range(4)], 0.5**level
            )
            if i == 0:
                scaled[LEFT] = jnp.where(lane == 0, 0.0, scaled[LEFT])
            if i == halves - 1:
                last = 63 if level == 6 else LANES - 1
                scaled[RIGHT] = jnp.where(lane == last, 0.0, scaled[RIGHT])
            for m in range(4):
                maps[m, first + i, at, :] = scaled[m]
            maps[SCALE, first + i, at, :] = scale
            maps[INVERSE, first + i, at, :] = inverse

    chunks(0, rows, size, body)


def coarsen_whole(level, raw, next_raw):
    halves, rows, first = WHOLE[level]
    next_halves, next_rows, next_first = WHOLE[level + 1]
    for m in range(4):
        parts = []
        for h in range(halves):
            even, odd = even_odd(raw, (m, first + h), PAD, next_rows)
            parts.append(even if m == UP else odd if m == DOWN else even + odd)
        kind = "sum" if m in (UP, DOWN) else "low" if m == LEFT else "high"
        for h, x in enumerate(folded(parts, kind)):
            next_raw[m, next_first + h, PAD : PAD + next_rows, :] = 0.5 * x


def one_sweep(maps):
    coef = [maps[m, 0, PAD : PAD + 8, :] for m in range(4)]
    row = lax.broadcasted_iota(jnp.int32, (8, LANES), 0)
    coef[UP] = jnp.where(row == 0, 0.0, coef[UP])
    coef[DOWN] = jnp.where(row == 7, 0.0, coef[DOWN])
    steps = ((-1, 0), (1, 0), (0, -1), (0, 1))
    return dict(zip(steps, coef))


def moved(x, rows, columns):
    if rows:
        x = pltpu.roll(x, (-rows) % 8, 0)
    if columns:
        x = pltpu.roll(x, (-columns) % LANES, 1)
    return x


DIAMOND = [(a, b) for a in range(-4, 5) for b in range(-4, 5) if abs(a) + abs(b) <= 4]


def four_sweeps(maps, product):
    sweep = one_sweep(maps)
    whole = dict(sweep)
    whole[0, 0] = jnp.full((8, LANES), 1.0 - RELAX_WEIGHT, F32)
    for _ in range(3):
        grown = {at: (1.0 - RELAX_WEIGHT) * x for at, x in whole.items()}
        for step, coef in sweep.items():
            for at, x in whole.items():
                place = (at[0] + step[0], at[1] + step[1])
                term = coef * moved(x, *step)
                grown[place] = grown[place] + term if place in grown else term
        whole = grown
    for i, at in enumerate(DIAMOND):
        product[i] = moved(whole[at], -at[0], 0)


def coarse_solve(base, maps, product):
    sweep = one_sweep(maps)
    right_side = [base[c, 0, PAD : PAD + 8, :] for c in range(CHANNELS)]
    first = right_side
    for _ in range(3):
        first = [
            (1.0 - RELAX_WEIGHT) * v + g + sum(coef * moved(v, *at) for at, coef in sweep.items())
            for v, g in zip(first, right_side)
        ]
    values = first
    for _ in range(COARSE_SWEEPS // 4 - 1):
        lanes = [[moved(v, 0, b) for b in range(-4, 5)] for v in values]
        totals = [list() for _ in range(CHANNELS)]
        for a in range(-4, 5):
            sums = [None] * CHANNELS
            for i, at in enumerate(DIAMOND):
                if at[0] == a:
                    coef = product[i]
                    for c in range(CHANNELS):
                        term = coef * lanes[c][at[1] + 4]
                        sums[c] = term if sums[c] is None else sums[c] + term
            for c in range(CHANNELS):
                totals[c].append(moved(sums[c], a, 0))
        values = []
        for c in range(CHANNELS):
            t = totals[c]
            even = (t[0] + t[1]) + (t[2] + t[3])
            odd = (t[5] + t[6]) + (t[7] + t[8])
            values.append((first[c] + t[4]) + (even + odd))
    return values


def whole_cycle(level, bases, fields, others, maps, product):
    halves, rows, first = WHOLE[level]
    base, field, other, level_maps = bases[level], fields[level], others[level], maps[level]
    size = rows
    stencil("first", field, base, base, level_maps, 0, rows, size, 1, halves, first)
    stencil("residual", other, field, base, level_maps, 0, rows, size, 1, halves, first)
    next_halves, next_rows, next_first = WHOLE[level + 1]
    summed = []
    for h in range(halves):
        parts = []
        for c in range(CHANNELS):
            even, odd = even_odd(other, (c, first + h), PAD, next_rows)
            parts.append(even + odd)
        summed.append(jnp.concatenate(parts, axis=0))
    for h, x in enumerate(folded(summed, "sum")):
        inverse = 0.25 * maps[level + 1][INVERSE, next_first + h, PAD : PAD + next_rows, :]
        for c in range(CHANNELS):
            part = x[c * next_rows : (c + 1) * next_rows]
            bases[level + 1][c, next_first + h, PAD : PAD + next_rows, :] = part * inverse
    if level == 5:
        coarse = coarse_solve(bases[6], maps[6], product)
        coarse = [jnp.concatenate(coarse, axis=0)]
    else:
        whole_cycle(level + 1, bases, fields, others, maps, product)
        coarse = [
            jnp.concatenate(
                [
                    fields[level + 1][c, next_first + h, PAD : PAD + next_rows, :]
                    for c in range(CHANNELS)
                ],
                axis=0,
            )
            for h in range(next_halves)
        ]
    for m, x in enumerate(coarse):
        wide = doubled(x)
        for i in range(min(halves, 2)):
            h = first + 2 * m + i
            for c in range(CHANNELS):
                part = wide[i][c * next_rows : (c + 1) * next_rows]
                for offset in range(2):
                    at = pl.ds(PAD + offset, next_rows, stride=2)
                    field[c, h, at, :] = field[c, h, at, :] + part
    if level > 3:
        stencil("relax", other, field, base, level_maps, 0, rows, size, 1, halves, first)
        stencil("relax", field, other, base, level_maps, 0, rows, size, 1, halves, first)


def window(ref, index, place):
    group = lax.shift_right_logical(place[1], 3)
    offset = 16 * (place[1] & 7)
    at = pl.ds(pl.multiple_of(8 * place[0], 8), 24)
    lane = lane_ids(24)
    turn = lax.rem(LANES - offset, LANES)
    before, here, after = [pltpu.roll(ref[index, group + i, at, :], turn, 1) for i in range(3)]
    low = lane < 64
    fits = lane + offset < LANES
    return jnp.where(low, jnp.where(fits, here, after), jnp.where(fits, before, here))


def correct_level_two(place, bases, fields, maps, f2, near_maps, near_base, near_a, near_b):
    for m in range(4):
        near_maps[m, 0, PAD : PAD + 24, :] = window(maps[3], m, place)
    edge = jnp.zeros((PAD, LANES), F32)
    for c in range(CHANNELS):
        near_base[c, 0, PAD : PAD + 24, :] = window(bases[3], c, place)
        near_a[c, 0, PAD : PAD + 24, :] = window(fields[3], c, place)
        for ref in (near_a, near_b):
            ref[c, 0, 0:PAD, :] = edge
            ref[c, 0, PAD + 24 : PAD + 32, :] = edge
    stencil("relax", near_b, near_a, near_base, near_maps, 0, 24, 24, 1, 1)
    stencil("relax", near_a, near_b, near_base, near_maps, 0, 24, 24, 1, 1)
    flat = jnp.concatenate([near_a[c, 0, PAD : PAD + 24, :] for c in range(CHANNELS)], axis=0)
    lane = lane_ids(flat.shape[0])
    wide = [picked(flat, lane >> 3), picked(flat, jnp.where(lane < 64, 16, 112) + (lane >> 3))]
    for c in range(CHANNELS):
        for h in range(2):
            part = wide[h][24 * c : 24 * c + 24]
            for offset in range(2):
                at = pl.ds(PAD + offset, 24, stride=2)
                f2[c, h, at, :] = f2[c, h, at, :] + part


def add_rows(field, coarse, low, high, size):
    def body(start):
        for c in range(CHANNELS):
            for h in range(2):
                part = coarse[c, h, pl.ds(start, size), :]
                for offset in range(2):
                    at = pl.ds(2 * start - PAD + offset, size, stride=2)
                    field[c, h, at, :] = field[c, h, at, :] + part

    chunks(low, high, size, body)


def up_levels(ranges, fields, bases, works, maps, extra):
    low, high, size = ranges[2]
    stencil("relax", works[2], fields[2], bases[2], maps[2], low, high, size, 4)
    stencil("relax", fields[2], works[2], bases[2], maps[2], low, high, size, 4)
    add_rows(fields[1], fields[2], 0, 48, 48)
    low, high, size = ranges[1]
    stencil("relax", works[1], fields[1], bases[1], maps[1], low, high, size, 2)
    stencil("relax", fields[1], works[1], bases[1], maps[1], low, high, size, 2)
    add_rows(fields[0], fields[1], 0, 96, 96)
    low, high, size = ranges[0]
    stencil("relax", works[0], fields[0], bases[0], maps[0], low, high, size, 1)
    if extra is None:
        stencil("relax", fields[0], works[0], bases[0], maps[0], low, high, size, 1)
    else:
        stencil(
            "relax_add", fields[0], works[0], bases[0], maps[0], low, high, size, 1, extra=extra
        )


def copy_field(source, target):
    count, halves, rows, _ = source.shape
    for c in range(count):
        for h in range(halves):
            target[c, h] = source[c, h]


def complete_maps(raw):
    size = 64
    at = pl.ds(PAD, size)
    lane = lane_ids(size)
    row = lax.broadcasted_iota(jnp.int32, (size, LANES), 0)
    ends = [raw[RIGHT, h, at, :] for h in range(1, 5)]
    shifted = beside([raw[LEFT, h, at, :] for h in range(1, 5)], 1)[1]
    last = ends[3]
    last = jnp.where((row & 7) == 7, pltpu.roll(pltpu.roll(last, 1, 1), 1, 0), last)
    shifted[3] = jnp.where(lane == LANES - 1, last, shifted[3])
    for i in range(4):
        below = raw[UP, 1 + i, pl.ds(PAD + 1, size), :]
        raw[DOWN, 1 + i, at, :] = jnp.where(row == size - 1, ends[i], below)
        raw[RIGHT, 1 + i, at, :] = shifted[i]


def middle_kernel(
    place, mine, other, m0, m1, m2, source, f0, g1, f1, g2, f2,
    m3, m4, m5, m6, product, solution, n0, h0, k1, h1, k2, h2, message,
    ordered, raw3, raw4, raw5, raw6, b3, v3, o3, b4, v4, o4, b5, v5, o5, b6,
    w0, w1, w2, near_maps, near_base, near_a, near_b,
):
    for ref in (m3, raw3, b3, v3, o3):
        rows = ref.shape[2]
        clear(ref, (0, PAD), (rows - PAD, rows))
        for index in range(ref.shape[0]):
            for h in (0, 5):
                ref[index, h] = jnp.zeros((rows, LANES), F32)
    for ref in (b4, v4, o4, b5, v5, o5):
        rows = ref.shape[2]
        clear(ref, (0, PAD), (rows - PAD, rows))
    for ref in (w0, w1, w2, n0):
        rows = ref.shape[2]
        clear(ref, (0, rows))

    def put(f, start, group, tile):
        if f < CHANNELS:
            b3[f, 1 + group, pl.ds(start, 8), :] = tile
        else:
            slot = (UP, LEFT, RIGHT)[f - CHANNELS]
            raw3[slot, 1 + group, pl.ds(start, 8), :] = tile

    unpack(place, mine, other, 6, 6, ordered, put)
    complete_maps(raw3)
    raws = {3: raw3, 4: raw4, 5: raw5, 6: raw6}
    maps = {3: m3, 4: m4, 5: m5, 6: m6}
    whole_maps(3, raw3, m3)
    for level in (3, 4, 5):
        coarsen_whole(level, raws[level], raws[level + 1])
        whole_maps(level + 1, raws[level + 1], maps[level + 1])
    four_sweeps(m6, product)
    scale_base(b3, m3)
    whole_cycle(
        3, {3: b3, 4: b4, 5: b5, 6: b6}, {3: v3, 4: v4, 5: v5}, {3: o3, 4: o4, 5: o5}, maps,
        product,
    )
    copy_field(f0, solution)
    copy_field(f1, h1)
    copy_field(f2, h2)
    correct_level_two(
        place, {3: b3}, {3: v3}, maps, h2, near_maps, near_base, near_a, near_b
    )
    local_maps = (m0, m1, m2)
    up_levels(FIRST_UP, (solution, h1, h2), (source, g1, g2), (w0, w1, w2), local_maps, None)
    stencil("difference", n0, solution, source, m0, 32, 160, 128, 1)
    for ref in (h0, k1, k2):
        rows = ref.shape[2]
        clear(ref, (0, rows))
    tiles = down_levels((h0, h1, h2), (n0, k1, k2), (w0, w1, w2), local_maps, LATER_DOWN)
    rows = own_row(jnp.concatenate(tiles, axis=0))
    for i in range(CHANNELS):
        message[i : i + 1, :] = rows[i]


def scale_base(base, maps):
    halves, rows, first = WHOLE[3]

    def body(start):
        at = pl.ds(start, rows)
        for i in range(halves):
            inverse = maps[INVERSE, first + i, at, :]
            for c in range(CHANNELS):
                base[c, first + i, at, :] = base[c, first + i, at, :] * inverse

    chunks(0, rows, rows, body)


def last_kernel(
    place, mine, other, m0, m1, m2, source, m3, m4, m5, m6, product, before, n0, f0, k1, f1, k2, f2,
    solution, residual,
    ordered, b3, v3, o3, b4, v4, o4, b5, v5, o5, b6,
    h0, h1, h2, w0, w1, w2, near_maps, near_base, near_a, near_b,
):
    for ref in (b3, v3, o3):
        rows = ref.shape[2]
        clear(ref, (0, PAD), (rows - PAD, rows))
        for index in range(ref.shape[0]):
            for h in (0, 5):
                ref[index, h] = jnp.zeros((rows, LANES), F32)
    for ref in (b4, v4, o4, b5, v5, o5):
        rows = ref.shape[2]
        clear(ref, (0, PAD), (rows - PAD, rows))
    for ref in (w0, w1, w2):
        rows = ref.shape[2]
        clear(ref, (0, rows))

    def put(f, start, group, tile):
        b3[f, 1 + group, pl.ds(start, 8), :] = tile

    unpack(place, mine, other, CHANNELS, CHANNELS, ordered, put)
    maps = {3: m3, 4: m4, 5: m5, 6: m6}
    scale_base(b3, m3)
    whole_cycle(
        3, {3: b3, 4: b4, 5: b5, 6: b6}, {3: v3, 4: v4, 5: v5}, {3: o3, 4: o4, 5: o5}, maps,
        product,
    )
    copy_field(f0, h0)
    copy_field(f1, h1)
    copy_field(f2, h2)
    correct_level_two(
        place, {3: b3}, {3: v3}, maps, h2, near_maps, near_base, near_a, near_b
    )
    local_maps = (m0, m1, m2)
    up_levels(LATER_UP, (h0, h1, h2), (n0, k1, k2), (w0, w1, w2), local_maps, before)
    stencil("final", w0, h0, source, m0, 64, 128, 64, 1)
    for c in range(CHANNELS):
        solution[c] = h0[c, 0, PAD + 64 : PAD + 128, :]
        residual[c] = w0[c, 0, PAD + 64 : PAD + 128, :]


def shape(*dims):
    return jax.ShapeDtypeStruct(dims, F32)


def field_shape(level, count):
    return (count, 2, LOCAL_ROWS[level] + 2 * PAD, LANES)


def whole_shape(level, count):
    halves, rows, first = WHOLE[level]
    return (count, halves + 2 * first, rows + 2 * PAD, LANES)


def call(kernel, outs, scratch, *args):
    in_specs = [pl.BlockSpec(memory_space=pltpu.VMEM) for _ in args]
    if args[0].dtype == jnp.int32 and args[0].ndim == 1:
        in_specs[0] = pl.BlockSpec(memory_space=pltpu.SMEM)
    return pl.pallas_call(
        kernel,
        out_shape=[shape(*o) for o in outs],
        in_specs=in_specs,
        out_specs=[pl.BlockSpec(memory_space=pltpu.VMEM) for _ in outs],
        scratch_shapes=[pltpu.VMEM(s, F32) for s in scratch],
        compiler_params=pltpu.CompilerParams(vmem_limit_bytes=14 * 1024 * 1024),
        cost_estimate=pl.CostEstimate(flops=0, bytes_accessed=8_000_000, transcendentals=0),
    )(*args)


def ring(count, step):
    return [(i, (i + step) % count) for i in range(count)]


def gathered(message):
    rows = message.shape[0]
    sent = jnp.broadcast_to(message.reshape(1, 1, rows * LANES), (128, 1, rows * LANES))
    mine = lax.all_to_all(sent, CHIPS, 0, 0, tiled=True)
    mine = mine.reshape(128 * rows, LANES)
    return mine, lax.ppermute(mine, "core", ring(2, 1))


def local(guidance, seam_weight, source_label):
    place = jnp.stack(
        [lax.axis_index("z"), lax.axis_index(SIDES), lax.axis_index("core")]
    ).astype(jnp.int32)
    down, up = pl.pallas_call(
        stack_kernel,
        out_shape=[shape(UPDOWN_ROWS, LANES)] * 2,
        in_specs=[pl.BlockSpec(memory_space=pltpu.HBM)] * 3,
        out_specs=[pl.BlockSpec(memory_space=pltpu.VMEM)] * 2,
        scratch_shapes=[
            pltpu.VMEM((2, CHANNELS, 64, LANES), F32),
            pltpu.VMEM((64, LANES), jnp.int32),
            pltpu.VMEM((64, LANES), jnp.int32),
            pltpu.SemaphoreType.DMA((3,)),
        ],
        compiler_params=pltpu.CompilerParams(vmem_limit_bytes=58 * 1024 * 1024),
    )(guidance, seam_weight, source_label)
    above = lax.ppermute(down, "z", ring(8, 1))
    below = lax.ppermute(up, "z", ring(8, -1))
    own, ends = call(own_kernel, [(FIELDS, 64, LANES), (8, LANES)], [], down, up)
    swap, side, border = call(
        pack_kernel,
        [(SIDE_ROWS, LANES)] * 2 + [(CHANNELS, 176, LANES)],
        [],
        place, own, ends, above, below,
    )
    swapped = lax.ppermute(swap, "core", ring(2, 1))
    pairs = [(i, min(max(i + 2 * (i % 2) - 1, 0), 31)) for i in range(32)]
    sided = lax.ppermute(side, SIDES, pairs)
    fields = [field_shape(level, CHANNELS) for level in range(3)]
    maps = [field_shape(0, 5), field_shape(1, 6), field_shape(2, 6)]
    raws = [field_shape(level, 4) for level in range(3)]
    m0, m1, m2, source, f0, g1, f1, g2, f2, message = call(
        setup_kernel,
        maps + [fields[0], fields[0], fields[1], fields[1], fields[2], fields[2], (6, LANES)],
        [field_shape(0, FIELDS)] + raws + fields,
        place, own, ends, above, below, swapped, sided, border,
    )
    mine, other = gathered(message)
    wholes = [whole_shape(level, CHANNELS) for level in (3, 4, 5) for _ in range(3)]
    wholes = wholes + [whole_shape(6, CHANNELS)]
    near = [(4, 1, 40, LANES)] + [(CHANNELS, 1, 40, LANES)] * 3
    m3, m4, m5, m6, product, solution, n0, h0, k1, h1, k2, h2, message = call(
        middle_kernel,
        [whole_shape(level, 6) for level in (3, 4, 5, 6)]
        + [(len(DIAMOND), 8, LANES)] + [fields[0]] * 3 + [fields[1]] * 2 + [fields[2]] * 2 + [(CHANNELS, LANES)],
        [(6, 256, LANES)] + [whole_shape(level, 4) for level in (3, 4, 5, 6)]
        + wholes + fields + near,
        place, mine, other, m0, m1, m2, source, f0, g1, f1, g2, f2,
    )
    mine, other = gathered(message)
    outs = call(
        last_kernel,
        [(CHANNELS, 64, LANES)] * 2,
        [(CHANNELS, 256, LANES)] + wholes + fields + fields + near,
        place, mine, other, m0, m1, m2, source, m3, m4, m5, m6, product,
        solution, n0, h0, k1, h1, k2, h2,
    )
    return tuple(outs)


def solution(mesh):
    fine = Mesh(mesh.devices.reshape(8, 4, 4, 2), ("z", "y", "x", "core"))
    return jax.shard_map(
        local,
        mesh=fine,
        in_specs=(P(None, None, "z", SIDES), P("z", SIDES), P("z", SIDES)),
        out_specs=(P(None, "z", SIDES), P(None, "z", SIDES)),
        check_vma=False,
    )
```

```python
import jax
import jax.numpy as jnp
from jax import lax
from jax.experimental import pallas as pl
from jax.experimental.pallas import tpu as pltpu
from jax.sharding import Mesh, PartitionSpec as P

F32 = jnp.float32
CHANNELS = 3
COARSE_SWEEPS = 48
RELAX_WEIGHT = 0.8
SEAM_FACTOR = 0.25
PAD = 8
LANES = 128
REACH = 56
SIDES = ("y", "x", "core")
CHIPS = ("z", "y", "x")
LOCAL_ROWS = (192, 96, 48)
UP, DOWN, LEFT, RIGHT, SCALE, INVERSE = range(6)


def lane_ids(rows):
    return lax.broadcasted_iota(jnp.int32, (rows, LANES), 1)


def beside(halves, width):
    count = len(halves)
    lane = lane_ids(halves[0].shape[0])
    ahead = [pltpu.roll(x, width, 1) for x in halves]
    behind = [pltpu.roll(x, LANES - width, 1) for x in halves]
    if count == 1:
        return ahead, behind
    left = [jnp.where(lane < width, ahead[h - 1], ahead[h]) for h in range(count)]
    right = [
        jnp.where(lane >= LANES - width, behind[(h + 1) % count], behind[h]) for h in range(count)
    ]
    return left, right


def pair_sum(x, width):
    low = (lane_ids(x.shape[0]) & width) == 0
    return x + jnp.where(low, pltpu.roll(x, LANES - width, 1), pltpu.roll(x, width, 1))


def low_of_pair(x, width):
    low = (lane_ids(x.shape[0]) & width) == 0
    return jnp.where(low, x, pltpu.roll(x, width, 1))


def high_of_pair(x, width):
    low = (lane_ids(x.shape[0]) & width) == 0
    return jnp.where(low, pltpu.roll(x, LANES - width, 1), x)


def picked(x, lanes):
    return jnp.take_along_axis(x, lanes, axis=1, mode="promise_in_bounds")


def chunks(low, high, size, body):
    count = (high - low) // size
    assert count * size == high - low

    def step(i, carry):
        body(pl.multiple_of(PAD + low + i * size, 8))
        return carry

    if count == 1:
        body(PAD + low)
    else:
        lax.fori_loop(0, count, step, 0)


def stencil(mode, target, field, base, maps, low, high, size, width=1, halves=2, first=0, extra=None):
    def body(start):
        at = pl.ds(start, size)
        span = range(first, first + halves)
        coef = [[maps[m, h, at, :] for h in span] for m in range(4)]
        for c in range(CHANNELS):
            here = [field[c, h, at, :] for h in span]
            above = [field[c, h, pl.ds(start - 1, size), :] for h in span]
            below = [field[c, h, pl.ds(start + 1, size), :] for h in span]
            left, right = beside(here, width)
            for i, h in enumerate(span):
                near = (above[i], below[i], left[i], right[i])
                if mode in ("difference", "scaled_difference", "final"):
                    near = [n - here[i] for n in near]
                total = coef[0][i] * near[0] + coef[1][i] * near[1]
                total = total + (coef[2][i] * near[2] + coef[3][i] * near[3])
                if mode == "first":
                    result = (2.0 - RELAX_WEIGHT) * here[i] + total
                elif mode == "relax":
                    result = (1.0 - RELAX_WEIGHT) * here[i] + base[c, h, at, :] + total
                elif mode == "relax_add":
                    result = (1.0 - RELAX_WEIGHT) * here[i] + base[c, h, at, :] + total
                    result = extra[c, h, at, :] + result
                elif mode == "residual":
                    result = base[c, h, at, :] - RELAX_WEIGHT * here[i] + total
                    result = maps[SCALE, h, at, :] * result
                elif mode == "difference":
                    result = base[c, h, at, :] + total
                else:
                    result = maps[SCALE, h, at, :] * (base[c, h, at, :] + total)
                target[c, h, at, :] = result

    chunks(low, high, size, body)


def scaled_maps(raw, factor):
    whole = raw[0] + raw[1] + raw[2] + raw[3]
    inside = whole > 0.0
    share = jnp.where(inside, RELAX_WEIGHT / jnp.where(inside, whole, 1.0), 0.0)
    return [r * share for r in raw], whole * (factor / RELAX_WEIGHT), share * (1.0 / factor)


def even_odd(ref, lead, start, count):
    return (
        ref[lead + (pl.ds(start, count, stride=2), slice(None))],
        ref[lead + (pl.ds(start + 1, count, stride=2), slice(None))],
    )


FIELDS = 5
WEIGHT, LABEL = 3, 4
UPDOWN_ROWS = FIELDS * REACH + 8
SIDE_ROWS = FIELDS * 88 + 16


def stack_kernel(guidance_in, weight_in, label_in, down, up, guidance, weight_at, label_at, arrived):
    copies = [
        pltpu.make_async_copy(source, target, arrived.at[i])
        for i, (source, target) in enumerate(
            ((guidance_in, guidance), (weight_in, weight_at), (label_in, label_at))
        )
    ]
    for copy in copies:
        copy.start()
    for copy in copies:
        copy.wait()
    weight, label = weight_at[...].astype(F32), label_at[...].astype(F32)
    row = lax.broadcasted_iota(jnp.int32, (64, LANES), 0)
    lane = lane_ids(64)

    def edge(turn, axis, inside):
        matching = jnp.where(pltpu.roll(label, turn, axis) == label, 1.0 / 64.0, SEAM_FACTOR / 64.0)
        return jnp.where(inside, (weight + pltpu.roll(weight, turn, axis)) * matching, 0.0)

    below, right = edge(63, 0, row < 63), edge(LANES - 1, 1, lane < LANES - 1)

    def put(a, x):
        down[REACH * a : REACH * (a + 1), :] = x[64 - REACH :]
        up[REACH * a : REACH * (a + 1), :] = x[:REACH]

    ends = [guidance[0, c, 63:64, :] for c in range(CHANNELS)]
    for c in range(CHANNELS):
        first, second = below * guidance[0, c], right * guidance[1, c]
        put(c, (pltpu.roll(first, 1, 0) - first) + (pltpu.roll(second, 1, 1) - second))
        last = jnp.broadcast_to(guidance[1, c, :, LANES - 1 :], (64, LANES))
        ends.append(jnp.sum(jnp.where(row == lane, last, 0.0), axis=0, keepdims=True))
    put(WEIGHT, weight)
    put(LABEL, label)
    ends = jnp.concatenate(ends + [jnp.zeros((2, LANES), F32)], axis=0)
    down[FIELDS * REACH :, :] = ends
    up[FIELDS * REACH :, :] = ends


def own_kernel(down, up, own, ends):
    for a in range(FIELDS):
        own[a, :REACH, :] = up[REACH * a : REACH * (a + 1), :]
        own[a, REACH:, :] = down[REACH * (a + 1) - (64 - REACH) : REACH * (a + 1), :]
    ends[...] = up[FIELDS * REACH :, :]


def upright(row, first, count):
    place = first + lax.broadcasted_iota(jnp.int32, (count, LANES), 0)
    return picked(jnp.broadcast_to(row, (count, LANES)), place)


def whereabouts():
    core = lax.axis_index("core")
    chip = lax.axis_index("y") * 4 + lax.axis_index("x")
    return lax.axis_index("z"), 2 * chip + core, core


def pack_kernel(own, ends, above, below, swap, side, edge):
    first_core = whereabouts()[2] == 0
    low = lane_ids(88) < 64
    base = FIELDS * REACH

    def halves(x):
        return x[:88], pltpu.roll(x[88:], 64, 1)

    for a in range(FIELDS):
        at = slice(REACH * a, REACH * (a + 1))
        whole = jnp.concatenate([above[at, :], own[a], below[at, :]], axis=0)
        top, bottom = halves(whole)
        to_left = jnp.where(low, top, bottom)
        if a < CHANNELS:
            column = jnp.concatenate(
                [
                    upright(above[base + 3 + a : base + 4 + a, :], 64 - REACH, REACH),
                    upright(ends[3 + a : 4 + a, :], 0, 64),
                    upright(below[base + 3 + a : base + 4 + a, :], 0, REACH),
                ],
                axis=0,
            )
            edge[a] = column
            top, bottom = halves(jnp.where(lane_ids(176) == 64, column, whole))
        to_right = jnp.where(low, bottom, top)
        at = slice(88 * a, 88 * (a + 1))
        swap[at, :] = jnp.where(first_core, to_right, to_left)
        side[at, :] = jnp.where(first_core, to_left, to_right)
    for ref in (swap, side):
        ref[88 * FIELDS : 88 * FIELDS + 8, :] = above[base:, :]
        ref[88 * FIELDS + 8 :, :] = ends[...]


def local_down(level, field, base, work, maps, next_base, next_maps, first_rows, rest_rows, next_rows):
    width = 2**level
    low, high, size = first_rows
    stencil("first", field, base, base, maps, low, high, size, width)
    low, high, size = rest_rows
    stencil("scaled_difference", work, field, base, maps, low, high, size, width)
    if next_base is None:
        return

    low, high, size = next_rows

    def body(start):
        at = pl.ds(start, size)
        for h in range(2):
            inverse = 0.25 * next_maps[INVERSE, h, at, :]
            for c in range(CHANNELS):
                even, odd = even_odd(work, (c, h), 2 * start - PAD, size)
                next_base[c, h, at, :] = pair_sum(even + odd, width) * inverse

    chunks(low, high, size, body)


def own_row(x):
    count = x.shape[0] // 8
    spread = picked(x, 8 * (lane_ids(x.shape[0]) & 15))
    rows = []
    keep = (lane_ids(8) >> 4) == lax.broadcasted_iota(jnp.int32, (8, LANES), 0)
    for i in range(count):
        part = jnp.where(keep, spread[8 * i : 8 * i + 8], 0.0)
        rows.append(jnp.sum(part, axis=0, keepdims=True))
    return rows


def down_levels(fields, bases, work, maps, ranges):
    for level in range(3):
        local_down(
            level,
            fields[level],
            bases[level],
            work[level],
            maps[level],
            bases[level + 1] if level < 2 else None,
            maps[level + 1] if level < 2 else None,
            *ranges[level],
        )
    tiles = []
    for c in range(CHANNELS):
        even, odd = even_odd(work[2], (c, 0), PAD + 16, 8)
        tiles.append(0.25 * pair_sum(even + odd, 4))
    return tiles


FIRST_DOWN = (
    ((8, 184, 176), (8, 184, 176), (0, 96, 96)),
    ((0, 96, 96), (0, 96, 96), (0, 48, 48)),
    ((0, 48, 48), (0, 48, 48), None),
)
LATER_DOWN = (
    ((32, 160, 128), (32, 160, 128), (16, 80, 64)),
    ((16, 80, 64), (16, 80, 64), (8, 40, 32)),
    ((8, 40, 32), (8, 40, 32), None),
)
FIRST_UP = ((32, 160, 128), (8, 88, 80), (0, 48, 48))
LATER_UP = ((56, 136, 80), (24, 72, 48), (8, 40, 32))


def clear(ref, *bounds):
    for index in range(ref.shape[0]):
        for h in range(ref.shape[1]):
            for low, high in bounds:
                ref[index, h, low:high, :] = jnp.zeros((high - low, LANES), F32)


def setup_kernel(
    own, ends, above, below, swapped, sided, border,
    m0, m1, m2, source, f0, g1, f1, g2, f2, message,
    cells, raw0, raw1, raw2, w0, w1, w2,
):
    row_at, col_at, core = whereabouts()
    first_core = core == 0
    rows_of = lambda n, low: low + lax.broadcasted_iota(jnp.int32, (n, LANES), 0)
    edge = jnp.zeros((16, LANES), F32)
    not_top, not_bottom = row_at > 0, row_at < 7
    low = lane_ids(88) < 64
    inside = (low & (col_at < 31)) | (~low & (col_at > 0))

    def sides(start, size):
        one, two = swapped[start : start + size, :], sided[start : start + size, :]
        return jnp.where(first_core, one, two), jnp.where(first_core, two, one)

    for a in range(FIELDS):
        at = slice(REACH * a, REACH * (a + 1))
        for h in range(2):
            cells[a, h, 0:16, :] = edge
            cells[a, h, 192:208, :] = edge
        cells[a, 0, 16:72, :] = jnp.where(not_top, above[at, :], 0.0)
        cells[a, 0, 72:136, :] = own[a]
        cells[a, 0, 136:192, :] = jnp.where(not_bottom, below[at, :], 0.0)
        from_right, from_left = sides(88 * a, 88)
        top = jnp.where(low, from_right, from_left)
        bottom = pltpu.roll(jnp.where(low, from_left, from_right), 64, 1)
        cells[a, 1, 16:104, :] = jnp.where(inside & (not_top | (rows_of(88, 8) >= 64)), top, 0.0)
        cells[a, 1, 104:192, :] = jnp.where(
            inside & (not_bottom | (rows_of(88, 96) < 128)), bottom, 0.0
        )
    for ref in (m0, raw0, source, f0, w0):
        clear(ref, (0, 16), (192, 208))
    for ref, rows in ((m1, 96), (raw1, 96), (g1, 96), (f1, 96), (w1, 96)):
        clear(ref, (0, 8), (rows + 8, rows + 16))
    for ref, rows in ((m2, 48), (raw2, 48), (g2, 48), (f2, 48), (w2, 48)):
        clear(ref, (0, 8), (rows + 8, rows + 16))

    def fine(start):
        size = 176
        at = pl.ds(start, size)
        up_at, down_at = pl.ds(start - 1, size), pl.ds(start + 1, size)
        weights = [cells[WEIGHT, h, at, :] for h in range(2)]
        labels = [cells[LABEL, h, at, :] for h in range(2)]
        weight_sides = beside(weights, 1)
        label_sides = beside(labels, 1)
        coef, shares = [], []
        for h in range(2):
            near_weights = (
                cells[WEIGHT, h, up_at, :], cells[WEIGHT, h, down_at, :], weight_sides[0][h], weight_sides[1][h],
            )
            near_labels = (
                cells[LABEL, h, up_at, :], cells[LABEL, h, down_at, :], label_sides[0][h], label_sides[1][h],
            )
            raw = []
            for m in range(4):
                matching = jnp.where(near_labels[m] == labels[h], 1.0 / 64.0, SEAM_FACTOR / 64.0)
                value = (weights[h] + near_weights[m]) * matching
                value = jnp.where(weights[h] > 0.0, value, 0.0)
                raw.append(value)
                raw0[m, h, at, :] = value
            scaled, scale, share = scaled_maps(raw, 1.0)
            shares.append(share)
            for m in range(4):
                m0[m, h, at, :] = scaled[m]
            m0[SCALE, h, at, :] = scale
            coef.append(scaled)
        for c in range(CHANNELS):
            part = [cells[c, h, at, :] for h in range(2)]
            own_end = border[c]
            left_end = pltpu.roll(part[1], 64, 1), pltpu.roll(part[1], 63, 1)
            first, last = lane_ids(size) == 0, lane_ids(size) == LANES - 1
            flux = jnp.where(first, coef[0][LEFT] * left_end[0], 0.0)
            flux = flux - jnp.where(last, coef[0][RIGHT] * own_end, 0.0)
            source[c, 0, at, :] = shares[0] * part[0] + flux
            flux = jnp.where(first, coef[1][LEFT] * own_end, 0.0)
            flux = flux - jnp.where(last, coef[1][RIGHT] * left_end[1], 0.0)
            source[c, 1, at, :] = shares[1] * part[1] + flux

    chunks(8, 184, 176, fine)
    from_right, from_left = sides(88 * FIELDS, 16)
    beside_own = jnp.where(lane_ids(16) < 64, from_right, from_left)
    for first, upper in ((0, 71), (8, 135)):
        for c in range(CHANNELS):
            if first == 0:
                straight = above[FIELDS * REACH + c : FIELDS * REACH + c + 1, :]
            else:
                straight = ends[c : c + 1, :]
            for h, flow in ((0, straight), (1, beside_own[first + c : first + c + 1])):
                if first == 0:
                    flow = jnp.where(not_top, flow, 0.0)
                one, two = pl.ds(upper, 1), pl.ds(upper + 1, 1)
                source[c, h, one, :] = source[c, h, one, :] - m0[DOWN, h, one, :] * flow
                source[c, h, two, :] = source[c, h, two, :] + m0[UP, h, two, :] * flow

    def coarser(raw, width, start, size, h):
        parts = []
        for m in range(4):
            even, odd = even_odd(raw, (m, h), start, size)
            if m == UP:
                parts.append(0.5 * pair_sum(even, width))
            elif m == DOWN:
                parts.append(0.5 * pair_sum(odd, width))
            elif m == LEFT:
                parts.append(0.5 * low_of_pair(even + odd, width))
            else:
                parts.append(0.5 * high_of_pair(even + odd, width))
        return parts

    for level, fine_raw, raw, maps, rows in ((1, raw0, raw1, m1, 96), (2, raw1, raw2, m2, 48)):

        def coarse(start, level=level, fine_raw=fine_raw, raw=raw, maps=maps, rows=rows):
            size = rows
            at = pl.ds(start, size)
            for h in range(2):
                parts = coarser(fine_raw, 2 ** (level - 1), 2 * start - PAD, size, h)
                scaled, scale, inverse = scaled_maps(parts, 0.5**level)
                for m in range(4):
                    raw[m, h, at, :] = parts[m]
                    maps[m, h, at, :] = scaled[m]
                maps[SCALE, h, at, :] = scale
                maps[INVERSE, h, at, :] = inverse

        chunks(0, rows, rows, coarse)
    tiles = down_levels((f0, f1, f2), (source, g1, g2), (w0, w1, w2), (m0, m1, m2), FIRST_DOWN)
    upward, downward, leftward, rightward = coarser(raw2, 4, PAD + 16, 8, 0)
    row = lax.broadcasted_iota(jnp.int32, (8, LANES), 0)
    cell = lane_ids(8) >> 3
    turned = pltpu.roll(pltpu.roll(rightward, LANES - 8, 1), 7, 0)
    ends = jnp.where(row == 7, downward, jnp.where(cell == 15, rightward, turned))
    rows = own_row(jnp.concatenate(tiles + [upward, leftward, ends], axis=0))
    for i in range(6):
        message[i : i + 1, :] = rows[i]


def unpack(place, mine, other, count, stride, ordered, put):
    core = place[2]
    for f in range(count):
        own = mine[pl.ds(f, 128, stride=stride), :]
        theirs = other[pl.ds(f, 128, stride=stride), :]
        ordered[f, pl.ds(0, 128, stride=2), :] = jnp.where(core == 0, own, theirs)
        ordered[f, pl.ds(1, 128, stride=2), :] = jnp.where(core == 0, theirs, own)
    sub = lax.broadcasted_iota(jnp.int32, (8, LANES), 0)
    part, cell = lane_ids(8) >> 4, lane_ids(8) & 15
    first = (((sub - part) & 7) << 4) + cell
    last = (((part - sub) & 7) << 4) + cell
    for z in range(8):
        for f in range(count):
            for group in range(4):
                x = picked(ordered[f, pl.ds(z * 32 + 8 * group, 8), :], first)
                for k in (1, 2, 4):
                    x = jnp.where((part & k) != 0, pltpu.roll(x, 8 - k, 0), x)
                put(f, PAD + 8 * z, group, picked(x, last))


def folded(halves, kind):
    lane = lane_ids(halves[0].shape[0])
    even = (2 * lane) & (LANES - 1)

    def one(x):
        if kind == "low":
            return picked(x, even)
        if kind == "high":
            return picked(x, even + 1)
        return picked(x, even) + picked(x, even + 1)

    parts = [one(x) for x in halves]
    if len(parts) == 1:
        parts.append(jnp.zeros_like(parts[0]))
    return [jnp.where(lane < 64, parts[i], parts[i + 1]) for i in range(0, len(parts), 2)]


def doubled(x):
    lane = lane_ids(x.shape[0])
    return [picked(x, lane >> 1), picked(x, 64 + (lane >> 1))]


WHOLE = {3: (4, 64, 1), 4: (2, 32, 0), 5: (1, 16, 0), 6: (1, 8, 0)}


def whole_maps(level, raw, maps):
    halves, rows, first = WHOLE[level]
    size = rows

    def body(start):
        at = pl.ds(start, size)
        lane = lane_ids(size)
        for i in range(halves):
            scaled, scale, inverse = scaled_maps(
                [raw[m, first + i, at, :] for m in range(4)], 0.5**level
            )
            if i == 0:
                scaled[LEFT] = jnp.where(lane == 0, 0.0, scaled[LEFT])
            if i == halves - 1:
                last = 63 if level == 6 else LANES - 1
                scaled[RIGHT] = jnp.where(lane == last, 0.0, scaled[RIGHT])
            for m in range(4):
                maps[m, first + i, at, :] = scaled[m]
            maps[SCALE, first + i, at, :] = scale
            maps[INVERSE, first + i, at, :] = inverse

    chunks(0, rows, size, body)


def coarsen_whole(level, raw, next_raw):
    halves, rows, first = WHOLE[level]
    next_halves, next_rows, next_first = WHOLE[level + 1]
    for m in range(4):
        parts = []
        for h in range(halves):
            even, odd = even_odd(raw, (m, first + h), PAD, next_rows)
            parts.append(even if m == UP else odd if m == DOWN else even + odd)
        kind = "sum" if m in (UP, DOWN) else "low" if m == LEFT else "high"
        for h, x in enumerate(folded(parts, kind)):
            next_raw[m, next_first + h, PAD : PAD + next_rows, :] = 0.5 * x


def one_sweep(maps):
    coef = [maps[m, 0, PAD : PAD + 8, :] for m in range(4)]
    row = lax.broadcasted_iota(jnp.int32, (8, LANES), 0)
    coef[UP] = jnp.where(row == 0, 0.0, coef[UP])
    coef[DOWN] = jnp.where(row == 7, 0.0, coef[DOWN])
    steps = ((-1, 0), (1, 0), (0, -1), (0, 1))
    return dict(zip(steps, coef))


def moved(x, rows, columns):
    if rows:
        x = pltpu.roll(x, (-rows) % 8, 0)
    if columns:
        x = pltpu.roll(x, (-columns) % LANES, 1)
    return x


DIAMOND = [(a, b) for a in range(-4, 5) for b in range(-4, 5) if abs(a) + abs(b) <= 4]


def four_sweeps(maps, product):
    sweep = one_sweep(maps)
    whole = dict(sweep)
    whole[0, 0] = jnp.full((8, LANES), 1.0 - RELAX_WEIGHT, F32)
    for _ in range(3):
        grown = {at: (1.0 - RELAX_WEIGHT) * x for at, x in whole.items()}
        for step, coef in sweep.items():
            for at, x in whole.items():
                place = (at[0] + step[0], at[1] + step[1])
                term = coef * moved(x, *step)
                grown[place] = grown[place] + term if place in grown else term
        whole = grown
    for i, at in enumerate(DIAMOND):
        product[i] = moved(whole[at], -at[0], 0)


def coarse_solve(base, maps, product):
    sweep = one_sweep(maps)
    right_side = [base[c, 0, PAD : PAD + 8, :] for c in range(CHANNELS)]
    first = right_side
    for _ in range(3):
        first = [
            (1.0 - RELAX_WEIGHT) * v + g + sum(coef * moved(v, *at) for at, coef in sweep.items())
            for v, g in zip(first, right_side)
        ]
    values = first
    for _ in range(COARSE_SWEEPS // 4 - 1):
        lanes = [[moved(v, 0, b) for b in range(-4, 5)] for v in values]
        totals = [list() for _ in range(CHANNELS)]
        for a in range(-4, 5):
            sums = [None] * CHANNELS
            for i, at in enumerate(DIAMOND):
                if at[0] == a:
                    coef = product[i]
                    for c in range(CHANNELS):
                        term = coef * lanes[c][at[1] + 4]
                        sums[c] = term if sums[c] is None else sums[c] + term
            for c in range(CHANNELS):
                totals[c].append(moved(sums[c], a, 0))
        values = []
        for c in range(CHANNELS):
            t = totals[c]
            even = (t[0] + t[1]) + (t[2] + t[3])
            odd = (t[5] + t[6]) + (t[7] + t[8])
            values.append((first[c] + t[4]) + (even + odd))
    return values


def whole_cycle(level, bases, fields, others, maps, product):
    halves, rows, first = WHOLE[level]
    base, field, other, level_maps = bases[level], fields[level], others[level], maps[level]
    size = rows
    stencil("first", field, base, base, level_maps, 0, rows, size, 1, halves, first)
    stencil("residual", other, field, base, level_maps, 0, rows, size, 1, halves, first)
    next_halves, next_rows, next_first = WHOLE[level + 1]
    summed = []
    for h in range(halves):
        parts = []
        for c in range(CHANNELS):
            even, odd = even_odd(other, (c, first + h), PAD, next_rows)
            parts.append(even + odd)
        summed.append(jnp.concatenate(parts, axis=0))
    for h, x in enumerate(folded(summed, "sum")):
        inverse = 0.25 * maps[level + 1][INVERSE, next_first + h, PAD : PAD + next_rows, :]
        for c in range(CHANNELS):
            part = x[c * next_rows : (c + 1) * next_rows]
            bases[level + 1][c, next_first + h, PAD : PAD + next_rows, :] = part * inverse
    if level == 5:
        coarse = coarse_solve(bases[6], maps[6], product)
        coarse = [jnp.concatenate(coarse, axis=0)]
    else:
        whole_cycle(level + 1, bases, fields, others, maps, product)
        coarse = [
            jnp.concatenate(
                [
                    fields[level + 1][c, next_first + h, PAD : PAD + next_rows, :]
                    for c in range(CHANNELS)
                ],
                axis=0,
            )
            for h in range(next_halves)
        ]
    for m, x in enumerate(coarse):
        wide = doubled(x)
        for i in range(min(halves, 2)):
            h = first + 2 * m + i
            for c in range(CHANNELS):
                part = wide[i][c * next_rows : (c + 1) * next_rows]
                for offset in range(2):
                    at = pl.ds(PAD + offset, next_rows, stride=2)
                    field[c, h, at, :] = field[c, h, at, :] + part
    if level > 3:
        stencil("relax", other, field, base, level_maps, 0, rows, size, 1, halves, first)
        stencil("relax", field, other, base, level_maps, 0, rows, size, 1, halves, first)


def window(ref, index, place):
    group = lax.shift_right_logical(place[1], 3)
    offset = 16 * (place[1] & 7)
    at = pl.ds(pl.multiple_of(8 * place[0], 8), 24)
    lane = lane_ids(24)
    turn = lax.rem(LANES - offset, LANES)
    before, here, after = [pltpu.roll(ref[index, group + i, at, :], turn, 1) for i in range(3)]
    low = lane < 64
    fits = lane + offset < LANES
    return jnp.where(low, jnp.where(fits, here, after), jnp.where(fits, before, here))


def correct_level_two(place, bases, fields, maps, f2, near_maps, near_base, near_a, near_b):
    for m in range(4):
        near_maps[m, 0, PAD : PAD + 24, :] = window(maps[3], m, place)
    edge = jnp.zeros((PAD, LANES), F32)
    for c in range(CHANNELS):
        near_base[c, 0, PAD : PAD + 24, :] = window(bases[3], c, place)
        near_a[c, 0, PAD : PAD + 24, :] = window(fields[3], c, place)
        for ref in (near_a, near_b):
            ref[c, 0, 0:PAD, :] = edge
            ref[c, 0, PAD + 24 : PAD + 32, :] = edge
    stencil("relax", near_b, near_a, near_base, near_maps, 0, 24, 24, 1, 1)
    stencil("relax", near_a, near_b, near_base, near_maps, 0, 24, 24, 1, 1)
    flat = jnp.concatenate([near_a[c, 0, PAD : PAD + 24, :] for c in range(CHANNELS)], axis=0)
    lane = lane_ids(flat.shape[0])
    wide = [picked(flat, lane >> 3), picked(flat, jnp.where(lane < 64, 16, 112) + (lane >> 3))]
    for c in range(CHANNELS):
        for h in range(2):
            part = wide[h][24 * c : 24 * c + 24]
            for offset in range(2):
                at = pl.ds(PAD + offset, 24, stride=2)
                f2[c, h, at, :] = f2[c, h, at, :] + part


def add_rows(field, coarse, low, high, size):
    def body(start):
        for c in range(CHANNELS):
            for h in range(2):
                part = coarse[c, h, pl.ds(start, size), :]
                for offset in range(2):
                    at = pl.ds(2 * start - PAD + offset, size, stride=2)
                    field[c, h, at, :] = field[c, h, at, :] + part

    chunks(low, high, size, body)


def up_levels(ranges, fields, bases, works, maps, extra):
    low, high, size = ranges[2]
    stencil("relax", works[2], fields[2], bases[2], maps[2], low, high, size, 4)
    stencil("relax", fields[2], works[2], bases[2], maps[2], low, high, size, 4)
    add_rows(fields[1], fields[2], 0, 48, 48)
    low, high, size = ranges[1]
    stencil("relax", works[1], fields[1], bases[1], maps[1], low, high, size, 2)
    stencil("relax", fields[1], works[1], bases[1], maps[1], low, high, size, 2)
    add_rows(fields[0], fields[1], 0, 96, 96)
    low, high, size = ranges[0]
    stencil("relax", works[0], fields[0], bases[0], maps[0], low, high, size, 1)
    if extra is None:
        stencil("relax", fields[0], works[0], bases[0], maps[0], low, high, size, 1)
    else:
        stencil(
            "relax_add", fields[0], works[0], bases[0], maps[0], low, high, size, 1, extra=extra
        )


def copy_field(source, target):
    count, halves, rows, _ = source.shape
    for c in range(count):
        for h in range(halves):
            target[c, h] = source[c, h]


def complete_maps(raw):
    size = 64
    at = pl.ds(PAD, size)
    lane = lane_ids(size)
    row = lax.broadcasted_iota(jnp.int32, (size, LANES), 0)
    ends = [raw[RIGHT, h, at, :] for h in range(1, 5)]
    shifted = beside([raw[LEFT, h, at, :] for h in range(1, 5)], 1)[1]
    last = ends[3]
    last = jnp.where((row & 7) == 7, pltpu.roll(pltpu.roll(last, 1, 1), 1, 0), last)
    shifted[3] = jnp.where(lane == LANES - 1, last, shifted[3])
    for i in range(4):
        below = raw[UP, 1 + i, pl.ds(PAD + 1, size), :]
        raw[DOWN, 1 + i, at, :] = jnp.where(row == size - 1, ends[i], below)
        raw[RIGHT, 1 + i, at, :] = shifted[i]


def middle_kernel(
    mine, other, m0, m1, m2, source, f0, g1, f1, g2, f2,
    m3, m4, m5, m6, product, solution, n0, h0, k1, h1, k2, h2, message,
    ordered, raw3, raw4, raw5, raw6, b3, v3, o3, b4, v4, o4, b5, v5, o5, b6,
    w0, w1, w2, near_maps, near_base, near_a, near_b,
):
    place = whereabouts()
    for ref in (m3, raw3, b3, v3, o3):
        rows = ref.shape[2]
        clear(ref, (0, PAD), (rows - PAD, rows))
        for index in range(ref.shape[0]):
            for h in (0, 5):
                ref[index, h] = jnp.zeros((rows, LANES), F32)
    for ref in (b4, v4, o4, b5, v5, o5):
        rows = ref.shape[2]
        clear(ref, (0, PAD), (rows - PAD, rows))
    for ref in (w0, w1, w2, n0):
        rows = ref.shape[2]
        clear(ref, (0, rows))

    def put(f, start, group, tile):
        if f < CHANNELS:
            b3[f, 1 + group, pl.ds(start, 8), :] = tile
        else:
            slot = (UP, LEFT, RIGHT)[f - CHANNELS]
            raw3[slot, 1 + group, pl.ds(start, 8), :] = tile

    unpack(place, mine, other, 6, 6, ordered, put)
    complete_maps(raw3)
    raws = {3: raw3, 4: raw4, 5: raw5, 6: raw6}
    maps = {3: m3, 4: m4, 5: m5, 6: m6}
    whole_maps(3, raw3, m3)
    for level in (3, 4, 5):
        coarsen_whole(level, raws[level], raws[level + 1])
        whole_maps(level + 1, raws[level + 1], maps[level + 1])
    four_sweeps(m6, product)
    scale_base(b3, m3)
    whole_cycle(
        3, {3: b3, 4: b4, 5: b5, 6: b6}, {3: v3, 4: v4, 5: v5}, {3: o3, 4: o4, 5: o5}, maps,
        product,
    )
    copy_field(f0, solution)
    copy_field(f1, h1)
    copy_field(f2, h2)
    correct_level_two(
        place, {3: b3}, {3: v3}, maps, h2, near_maps, near_base, near_a, near_b
    )
    local_maps = (m0, m1, m2)
    up_levels(FIRST_UP, (solution, h1, h2), (source, g1, g2), (w0, w1, w2), local_maps, None)
    stencil("difference", n0, solution, source, m0, 32, 160, 128, 1)
    for ref in (h0, k1, k2):
        rows = ref.shape[2]
        clear(ref, (0, rows))
    tiles = down_levels((h0, h1, h2), (n0, k1, k2), (w0, w1, w2), local_maps, LATER_DOWN)
    rows = own_row(jnp.concatenate(tiles, axis=0))
    for i in range(CHANNELS):
        message[i : i + 1, :] = rows[i]


def scale_base(base, maps):
    halves, rows, first = WHOLE[3]

    def body(start):
        at = pl.ds(start, rows)
        for i in range(halves):
            inverse = maps[INVERSE, first + i, at, :]
            for c in range(CHANNELS):
                base[c, first + i, at, :] = base[c, first + i, at, :] * inverse

    chunks(0, rows, rows, body)


def last_kernel(
    mine, other, m0, m1, m2, source, m3, m4, m5, m6, product, before, n0, f0, k1, f1, k2, f2,
    solution, residual,
    ordered, b3, v3, o3, b4, v4, o4, b5, v5, o5, b6,
    h0, h1, h2, w0, w1, w2, near_maps, near_base, near_a, near_b,
):
    place = whereabouts()
    for ref in (b3, v3, o3):
        rows = ref.shape[2]
        clear(ref, (0, PAD), (rows - PAD, rows))
        for index in range(ref.shape[0]):
            for h in (0, 5):
                ref[index, h] = jnp.zeros((rows, LANES), F32)
    for ref in (b4, v4, o4, b5, v5, o5):
        rows = ref.shape[2]
        clear(ref, (0, PAD), (rows - PAD, rows))
    for ref in (w0, w1, w2):
        rows = ref.shape[2]
        clear(ref, (0, rows))

    def put(f, start, group, tile):
        b3[f, 1 + group, pl.ds(start, 8), :] = tile

    unpack(place, mine, other, CHANNELS, CHANNELS, ordered, put)
    maps = {3: m3, 4: m4, 5: m5, 6: m6}
    scale_base(b3, m3)
    whole_cycle(
        3, {3: b3, 4: b4, 5: b5, 6: b6}, {3: v3, 4: v4, 5: v5}, {3: o3, 4: o4, 5: o5}, maps,
        product,
    )
    copy_field(f0, h0)
    copy_field(f1, h1)
    copy_field(f2, h2)
    correct_level_two(
        place, {3: b3}, {3: v3}, maps, h2, near_maps, near_base, near_a, near_b
    )
    local_maps = (m0, m1, m2)
    up_levels(LATER_UP, (h0, h1, h2), (n0, k1, k2), (w0, w1, w2), local_maps, before)
    stencil("final", w0, h0, source, m0, 64, 128, 64, 1)
    for c in range(CHANNELS):
        solution[c] = h0[c, 0, PAD + 64 : PAD + 128, :]
        residual[c] = w0[c, 0, PAD + 64 : PAD + 128, :]


def shape(*dims):
    return jax.ShapeDtypeStruct(dims, F32)


def field_shape(level, count):
    return (count, 2, LOCAL_ROWS[level] + 2 * PAD, LANES)


def whole_shape(level, count):
    halves, rows, first = WHOLE[level]
    return (count, halves + 2 * first, rows + 2 * PAD, LANES)


def call(kernel, outs, scratch, *args):
    in_specs = [pl.BlockSpec(memory_space=pltpu.VMEM) for _ in args]
    return pl.pallas_call(
        kernel,
        out_shape=[shape(*o) for o in outs],
        in_specs=in_specs,
        out_specs=[pl.BlockSpec(memory_space=pltpu.VMEM) for _ in outs],
        scratch_shapes=[pltpu.VMEM(s, F32) for s in scratch],
        compiler_params=pltpu.CompilerParams(vmem_limit_bytes=14 * 1024 * 1024),
        cost_estimate=pl.CostEstimate(flops=0, bytes_accessed=8_000_000, transcendentals=0),
    )(*args)


def ring(count, step):
    return [(i, (i + step) % count) for i in range(count)]


def gathered(message):
    rows = message.shape[0]
    sent = jnp.broadcast_to(message.reshape(1, 1, rows * LANES), (128, 1, rows * LANES))
    mine = lax.all_to_all(sent, CHIPS, 0, 0, tiled=True)
    mine = mine.reshape(128 * rows, LANES)
    return mine, lax.ppermute(mine, "core", ring(2, 1))


def local(guidance, seam_weight, source_label):
    down, up = pl.pallas_call(
        stack_kernel,
        out_shape=[pltpu.VMEM((UPDOWN_ROWS, LANES), F32)] * 2,
        in_specs=[pl.BlockSpec(memory_space=pltpu.HBM)] * 3,
        out_specs=[pl.BlockSpec(memory_space=pltpu.VMEM)] * 2,
        scratch_shapes=[
            pltpu.VMEM((2, CHANNELS, 64, LANES), F32),
            pltpu.VMEM((64, LANES), jnp.int32),
            pltpu.VMEM((64, LANES), jnp.int32),
            pltpu.SemaphoreType.DMA((3,)),
        ],
        compiler_params=pltpu.CompilerParams(vmem_limit_bytes=58 * 1024 * 1024),
    )(guidance, seam_weight, source_label)
    above = lax.ppermute(down, "z", ring(8, 1))
    below = lax.ppermute(up, "z", ring(8, -1))
    own, ends = call(own_kernel, [(FIELDS, 64, LANES), (8, LANES)], [], down, up)
    swap, side, border = call(
        pack_kernel,
        [(SIDE_ROWS, LANES)] * 2 + [(CHANNELS, 176, LANES)],
        [],
        own, ends, above, below,
    )
    swapped = lax.ppermute(swap, "core", ring(2, 1))
    pairs = [(i, min(max(i + 2 * (i % 2) - 1, 0), 31)) for i in range(32)]
    sided = lax.ppermute(side, SIDES, pairs)
    fields = [field_shape(level, CHANNELS) for level in range(3)]
    maps = [field_shape(0, 5), field_shape(1, 6), field_shape(2, 6)]
    raws = [field_shape(level, 4) for level in range(3)]
    m0, m1, m2, source, f0, g1, f1, g2, f2, message = call(
        setup_kernel,
        maps + [fields[0], fields[0], fields[1], fields[1], fields[2], fields[2], (6, LANES)],
        [field_shape(0, FIELDS)] + raws + fields,
        own, ends, above, below, swapped, sided, border,
    )
    mine, other = gathered(message)
    wholes = [whole_shape(level, CHANNELS) for level in (3, 4, 5) for _ in range(3)]
    wholes = wholes + [whole_shape(6, CHANNELS)]
    near = [(4, 1, 40, LANES)] + [(CHANNELS, 1, 40, LANES)] * 3
    m3, m4, m5, m6, product, solution, n0, h0, k1, h1, k2, h2, message = call(
        middle_kernel,
        [whole_shape(level, 6) for level in (3, 4, 5, 6)]
        + [(len(DIAMOND), 8, LANES)] + [fields[0]] * 3 + [fields[1]] * 2 + [fields[2]] * 2 + [(CHANNELS, LANES)],
        [(6, 256, LANES)] + [whole_shape(level, 4) for level in (3, 4, 5, 6)]
        + wholes + fields + near,
        mine, other, m0, m1, m2, source, f0, g1, f1, g2, f2,
    )
    mine, other = gathered(message)
    outs = call(
        last_kernel,
        [(CHANNELS, 64, LANES)] * 2,
        [(CHANNELS, 256, LANES)] + wholes + fields + fields + near,
        mine, other, m0, m1, m2, source, m3, m4, m5, m6, product,
        solution, n0, h0, k1, h1, k2, h2,
    )
    return tuple(outs)


def solution(mesh):
    fine = Mesh(mesh.devices.reshape(8, 4, 4, 2), ("z", "y", "x", "core"))
    return jax.shard_map(
        local,
        mesh=fine,
        in_specs=(P(None, None, "z", SIDES), P("z", SIDES), P("z", SIDES)),
        out_specs=(P(None, "z", SIDES), P(None, "z", SIDES)),
        check_vma=False,
    )
```

```python
import jax
import jax.numpy as jnp
from jax import lax
from jax.experimental import pallas as pl
from jax.experimental.pallas import tpu as pltpu
from jax.sharding import Mesh, PartitionSpec as P

F32 = jnp.float32
CHANNELS = 3
COARSE_SWEEPS = 48
RELAX_WEIGHT = 0.8
SEAM_FACTOR = 0.25
PAD = 8
LANES = 128
REACH = 56
SIDES = ("y", "x", "core")
CHIPS = ("z", "y", "x")
LOCAL_ROWS = (192, 96, 48)
UP, DOWN, LEFT, RIGHT, SCALE, INVERSE = range(6)


def lane_ids(rows):
    return lax.broadcasted_iota(jnp.int32, (rows, LANES), 1)


def beside(halves, width):
    count = len(halves)
    lane = lane_ids(halves[0].shape[0])
    ahead = [pltpu.roll(x, width, 1) for x in halves]
    behind = [pltpu.roll(x, LANES - width, 1) for x in halves]
    if count == 1:
        return ahead, behind
    left = [jnp.where(lane < width, ahead[h - 1], ahead[h]) for h in range(count)]
    right = [
        jnp.where(lane >= LANES - width, behind[(h + 1) % count], behind[h]) for h in range(count)
    ]
    return left, right


def pair_sum(x, width):
    low = (lane_ids(x.shape[0]) & width) == 0
    return x + jnp.where(low, pltpu.roll(x, LANES - width, 1), pltpu.roll(x, width, 1))


def low_of_pair(x, width):
    low = (lane_ids(x.shape[0]) & width) == 0
    return jnp.where(low, x, pltpu.roll(x, width, 1))


def high_of_pair(x, width):
    low = (lane_ids(x.shape[0]) & width) == 0
    return jnp.where(low, pltpu.roll(x, LANES - width, 1), x)


def picked(x, lanes):
    return jnp.take_along_axis(x, lanes, axis=1, mode="promise_in_bounds")


def chunks(low, high, size, body):
    count = (high - low) // size
    assert count * size == high - low

    def step(i, carry):
        body(pl.multiple_of(PAD + low + i * size, 8))
        return carry

    if count == 1:
        body(PAD + low)
    else:
        lax.fori_loop(0, count, step, 0)


def stencil(mode, target, field, base, maps, low, high, size, width=1, halves=2, first=0, extra=None):
    def body(start):
        at = pl.ds(start, size)
        span = range(first, first + halves)
        coef = [[maps[m, h, at, :] for h in span] for m in range(4)]
        for c in range(CHANNELS):
            here = [field[c, h, at, :] for h in span]
            above = [field[c, h, pl.ds(start - 1, size), :] for h in span]
            below = [field[c, h, pl.ds(start + 1, size), :] for h in span]
            left, right = beside(here, width)
            for i, h in enumerate(span):
                near = (above[i], below[i], left[i], right[i])
                if mode in ("difference", "scaled_difference", "final"):
                    near = [n - here[i] for n in near]
                total = coef[0][i] * near[0] + coef[1][i] * near[1]
                total = total + (coef[2][i] * near[2] + coef[3][i] * near[3])
                if mode == "first":
                    result = (2.0 - RELAX_WEIGHT) * here[i] + total
                elif mode == "relax":
                    result = (1.0 - RELAX_WEIGHT) * here[i] + base[c, h, at, :] + total
                elif mode == "relax_add":
                    result = (1.0 - RELAX_WEIGHT) * here[i] + base[c, h, at, :] + total
                    result = extra[c, h, at, :] + result
                elif mode == "residual":
                    result = base[c, h, at, :] - RELAX_WEIGHT * here[i] + total
                    result = maps[SCALE, h, at, :] * result
                elif mode == "difference":
                    result = base[c, h, at, :] + total
                else:
                    result = maps[SCALE, h, at, :] * (base[c, h, at, :] + total)
                target[c, h, at, :] = result

    chunks(low, high, size, body)


def scaled_maps(raw, factor):
    whole = raw[0] + raw[1] + raw[2] + raw[3]
    inside = whole > 0.0
    share = jnp.where(inside, RELAX_WEIGHT / jnp.where(inside, whole, 1.0), 0.0)
    return [r * share for r in raw], whole * (factor / RELAX_WEIGHT), share * (1.0 / factor)


def even_odd(ref, lead, start, count):
    return (
        ref[lead + (pl.ds(start, count, stride=2), slice(None))],
        ref[lead + (pl.ds(start + 1, count, stride=2), slice(None))],
    )


FIELDS = 5
WEIGHT, LABEL = 3, 4
UPDOWN_ROWS = FIELDS * REACH + 8
SIDE_ROWS = FIELDS * 88 + 16


def stack_kernel(guidance_in, weight_in, label_in, down, up, guidance, weight_at, label_at, arrived):
    copies = [
        pltpu.make_async_copy(source, target, arrived.at[i])
        for i, (source, target) in enumerate(
            ((guidance_in, guidance), (weight_in, weight_at), (label_in, label_at))
        )
    ]
    for copy in copies:
        copy.start()
    for copy in copies:
        copy.wait()
    weight, label = weight_at[...].astype(F32), label_at[...].astype(F32)
    row = lax.broadcasted_iota(jnp.int32, (64, LANES), 0)
    lane = lane_ids(64)

    def edge(turn, axis, inside):
        matching = jnp.where(pltpu.roll(label, turn, axis) == label, 1.0 / 64.0, SEAM_FACTOR / 64.0)
        return jnp.where(inside, (weight + pltpu.roll(weight, turn, axis)) * matching, 0.0)

    below, right = edge(63, 0, row < 63), edge(LANES - 1, 1, lane < LANES - 1)

    def put(a, x):
        down[REACH * a : REACH * (a + 1), :] = x[64 - REACH :]
        up[REACH * a : REACH * (a + 1), :] = x[:REACH]

    ends = [guidance[0, c, 63:64, :] for c in range(CHANNELS)]
    for c in range(CHANNELS):
        first, second = below * guidance[0, c], right * guidance[1, c]
        put(c, (pltpu.roll(first, 1, 0) - first) + (pltpu.roll(second, 1, 1) - second))
        last = jnp.broadcast_to(guidance[1, c, :, LANES - 1 :], (64, LANES))
        ends.append(jnp.sum(jnp.where(row == lane, last, 0.0), axis=0, keepdims=True))
    put(WEIGHT, weight)
    put(LABEL, label)
    ends = jnp.concatenate(ends + [jnp.zeros((2, LANES), F32)], axis=0)
    down[FIELDS * REACH :, :] = ends
    up[FIELDS * REACH :, :] = ends


def own_kernel(down, up, own, ends):
    for a in range(FIELDS):
        own[a, :REACH, :] = up[REACH * a : REACH * (a + 1), :]
        own[a, REACH:, :] = down[REACH * (a + 1) - (64 - REACH) : REACH * (a + 1), :]
    ends[...] = up[FIELDS * REACH :, :]


def upright(row, first, count):
    place = first + lax.broadcasted_iota(jnp.int32, (count, LANES), 0)
    return picked(jnp.broadcast_to(row, (count, LANES)), place)


def whereabouts():
    core = lax.axis_index("core")
    chip = lax.axis_index("y") * 4 + lax.axis_index("x")
    return lax.axis_index("z"), 2 * chip + core, core


def pack_kernel(own, ends, above, below, swap, side, edge):
    first_core = whereabouts()[2] == 0
    low = lane_ids(88) < 64
    base = FIELDS * REACH

    def halves(x):
        return x[:88], pltpu.roll(x[88:], 64, 1)

    for a in range(FIELDS):
        at = slice(REACH * a, REACH * (a + 1))
        whole = jnp.concatenate([above[at, :], own[a], below[at, :]], axis=0)
        top, bottom = halves(whole)
        to_left = jnp.where(low, top, bottom)
        if a < CHANNELS:
            column = jnp.concatenate(
                [
                    upright(above[base + 3 + a : base + 4 + a, :], 64 - REACH, REACH),
                    upright(ends[3 + a : 4 + a, :], 0, 64),
                    upright(below[base + 3 + a : base + 4 + a, :], 0, REACH),
                ],
                axis=0,
            )
            edge[a] = column
            top, bottom = halves(jnp.where(lane_ids(176) == 64, column, whole))
        to_right = jnp.where(low, bottom, top)
        at = slice(88 * a, 88 * (a + 1))
        swap[at, :] = jnp.where(first_core, to_right, to_left)
        side[at, :] = jnp.where(first_core, to_left, to_right)
    for ref in (swap, side):
        ref[88 * FIELDS : 88 * FIELDS + 8, :] = above[base:, :]
        ref[88 * FIELDS + 8 :, :] = ends[...]


def local_down(level, field, base, work, maps, next_base, next_maps, first_rows, rest_rows, next_rows):
    width = 2**level
    low, high, size = first_rows
    stencil("first", field, base, base, maps, low, high, size, width)
    low, high, size = rest_rows
    stencil("scaled_difference", work, field, base, maps, low, high, size, width)
    if next_base is None:
        return

    low, high, size = next_rows

    def body(start):
        at = pl.ds(start, size)
        for h in range(2):
            inverse = 0.25 * next_maps[INVERSE, h, at, :]
            for c in range(CHANNELS):
                even, odd = even_odd(work, (c, h), 2 * start - PAD, size)
                next_base[c, h, at, :] = pair_sum(even + odd, width) * inverse

    chunks(low, high, size, body)


def own_row(x):
    count = x.shape[0] // 8
    spread = picked(x, 8 * (lane_ids(x.shape[0]) & 15))
    rows = []
    keep = (lane_ids(8) >> 4) == lax.broadcasted_iota(jnp.int32, (8, LANES), 0)
    for i in range(count):
        part = jnp.where(keep, spread[8 * i : 8 * i + 8], 0.0)
        rows.append(jnp.sum(part, axis=0, keepdims=True))
    return rows


def repeat(rows, message):
    block = jnp.concatenate(rows * (24 // len(rows)), axis=0)
    for i in range(message.shape[0] // 24):
        message[24 * i : 24 * i + 24, :] = block


def down_levels(fields, bases, work, maps, ranges):
    for level in range(3):
        local_down(
            level,
            fields[level],
            bases[level],
            work[level],
            maps[level],
            bases[level + 1] if level < 2 else None,
            maps[level + 1] if level < 2 else None,
            *ranges[level],
        )
    tiles = []
    for c in range(CHANNELS):
        even, odd = even_odd(work[2], (c, 0), PAD + 16, 8)
        tiles.append(0.25 * pair_sum(even + odd, 4))
    return tiles


FIRST_DOWN = (
    ((8, 184, 176), (8, 184, 176), (0, 96, 96)),
    ((0, 96, 96), (0, 96, 96), (0, 48, 48)),
    ((0, 48, 48), (0, 48, 48), None),
)
LATER_DOWN = (
    ((32, 160, 128), (32, 160, 128), (16, 80, 64)),
    ((16, 80, 64), (16, 80, 64), (8, 40, 32)),
    ((8, 40, 32), (8, 40, 32), None),
)
FIRST_UP = ((32, 160, 128), (8, 88, 80), (0, 48, 48))
LATER_UP = ((56, 136, 80), (24, 72, 48), (8, 40, 32))
FIRST_SPANS = ((8, 88, 80), (0, 48, 48))
LATER_SPANS = ((24, 72, 48), (8, 40, 32))


def clear(ref, *bounds):
    for index in range(ref.shape[0]):
        for h in range(ref.shape[1]):
            for low, high in bounds:
                ref[index, h, low:high, :] = jnp.zeros((high - low, LANES), F32)


def setup_kernel(
    own, ends, above, below, swapped, sided, border,
    m0, m1, m2, source, f0, g1, f1, g2, f2, message,
    cells, raw0, raw1, raw2, w0, w1, w2,
):
    row_at, col_at, core = whereabouts()
    first_core = core == 0
    rows_of = lambda n, low: low + lax.broadcasted_iota(jnp.int32, (n, LANES), 0)
    edge = jnp.zeros((16, LANES), F32)
    not_top, not_bottom = row_at > 0, row_at < 7
    low = lane_ids(88) < 64
    inside = (low & (col_at < 31)) | (~low & (col_at > 0))

    def sides(start, size):
        one, two = swapped[start : start + size, :], sided[start : start + size, :]
        return jnp.where(first_core, one, two), jnp.where(first_core, two, one)

    for a in range(FIELDS):
        at = slice(REACH * a, REACH * (a + 1))
        for h in range(2):
            cells[a, h, 0:16, :] = edge
            cells[a, h, 192:208, :] = edge
        cells[a, 0, 16:72, :] = jnp.where(not_top, above[at, :], 0.0)
        cells[a, 0, 72:136, :] = own[a]
        cells[a, 0, 136:192, :] = jnp.where(not_bottom, below[at, :], 0.0)
        from_right, from_left = sides(88 * a, 88)
        top = jnp.where(low, from_right, from_left)
        bottom = pltpu.roll(jnp.where(low, from_left, from_right), 64, 1)
        cells[a, 1, 16:104, :] = jnp.where(inside & (not_top | (rows_of(88, 8) >= 64)), top, 0.0)
        cells[a, 1, 104:192, :] = jnp.where(
            inside & (not_bottom | (rows_of(88, 96) < 128)), bottom, 0.0
        )
    def fine(start):
        size = 176
        at = pl.ds(start, size)
        up_at, down_at = pl.ds(start - 1, size), pl.ds(start + 1, size)
        weights = [cells[WEIGHT, h, at, :] for h in range(2)]
        labels = [cells[LABEL, h, at, :] for h in range(2)]
        weight_sides = beside(weights, 1)
        label_sides = beside(labels, 1)
        coef, shares = [], []
        for h in range(2):
            near_weights = (
                cells[WEIGHT, h, up_at, :], cells[WEIGHT, h, down_at, :], weight_sides[0][h], weight_sides[1][h],
            )
            near_labels = (
                cells[LABEL, h, up_at, :], cells[LABEL, h, down_at, :], label_sides[0][h], label_sides[1][h],
            )
            raw = []
            for m in range(4):
                matching = jnp.where(near_labels[m] == labels[h], 1.0 / 64.0, SEAM_FACTOR / 64.0)
                value = (weights[h] + near_weights[m]) * matching
                value = jnp.where(weights[h] > 0.0, value, 0.0)
                raw.append(value)
                raw0[m, h, at, :] = value
            scaled, scale, share = scaled_maps(raw, 1.0)
            shares.append(share)
            for m in range(4):
                m0[m, h, at, :] = scaled[m]
            m0[SCALE, h, at, :] = scale
            coef.append(scaled)
        for c in range(CHANNELS):
            part = [cells[c, h, at, :] for h in range(2)]
            own_end = border[c]
            left_end = pltpu.roll(part[1], 64, 1), pltpu.roll(part[1], 63, 1)
            first, last = lane_ids(size) == 0, lane_ids(size) == LANES - 1
            flux = jnp.where(first, coef[0][LEFT] * left_end[0], 0.0)
            flux = flux - jnp.where(last, coef[0][RIGHT] * own_end, 0.0)
            source[c, 0, at, :] = shares[0] * part[0] + flux
            flux = jnp.where(first, coef[1][LEFT] * own_end, 0.0)
            flux = flux - jnp.where(last, coef[1][RIGHT] * left_end[1], 0.0)
            source[c, 1, at, :] = shares[1] * part[1] + flux

    chunks(8, 184, 176, fine)
    from_right, from_left = sides(88 * FIELDS, 16)
    beside_own = jnp.where(lane_ids(16) < 64, from_right, from_left)
    for first, upper in ((0, 71), (8, 135)):
        for c in range(CHANNELS):
            if first == 0:
                straight = above[FIELDS * REACH + c : FIELDS * REACH + c + 1, :]
            else:
                straight = ends[c : c + 1, :]
            for h, flow in ((0, straight), (1, beside_own[first + c : first + c + 1])):
                if first == 0:
                    flow = jnp.where(not_top, flow, 0.0)
                one, two = pl.ds(upper, 1), pl.ds(upper + 1, 1)
                source[c, h, one, :] = source[c, h, one, :] - m0[DOWN, h, one, :] * flow
                source[c, h, two, :] = source[c, h, two, :] + m0[UP, h, two, :] * flow

    def coarser(raw, width, start, size, h):
        parts = []
        for m in range(4):
            even, odd = even_odd(raw, (m, h), start, size)
            if m == UP:
                parts.append(0.5 * pair_sum(even, width))
            elif m == DOWN:
                parts.append(0.5 * pair_sum(odd, width))
            elif m == LEFT:
                parts.append(0.5 * low_of_pair(even + odd, width))
            else:
                parts.append(0.5 * high_of_pair(even + odd, width))
        return parts

    for level, fine_raw, raw, maps, rows in ((1, raw0, raw1, m1, 96), (2, raw1, raw2, m2, 48)):

        def coarse(start, level=level, fine_raw=fine_raw, raw=raw, maps=maps, rows=rows):
            size = rows
            at = pl.ds(start, size)
            for h in range(2):
                parts = coarser(fine_raw, 2 ** (level - 1), 2 * start - PAD, size, h)
                scaled, scale, inverse = scaled_maps(parts, 0.5**level)
                for m in range(4):
                    raw[m, h, at, :] = parts[m]
                    maps[m, h, at, :] = scaled[m]
                maps[SCALE, h, at, :] = scale
                maps[INVERSE, h, at, :] = inverse

        chunks(0, rows, rows, coarse)
    tiles = down_levels((f0, f1, f2), (source, g1, g2), (w0, w1, w2), (m0, m1, m2), FIRST_DOWN)
    upward, downward, leftward, rightward = coarser(raw2, 4, PAD + 16, 8, 0)
    row = lax.broadcasted_iota(jnp.int32, (8, LANES), 0)
    cell = lane_ids(8) >> 3
    turned = pltpu.roll(pltpu.roll(rightward, LANES - 8, 1), 7, 0)
    ends = jnp.where(row == 7, downward, jnp.where(cell == 15, rightward, turned))
    repeat(own_row(jnp.concatenate(tiles + [upward, leftward, ends], axis=0)), message)


def unpack(place, mine, other, count, stride, ordered, put):
    core = place[2]
    for f in range(count):
        own = mine[pl.ds(f, 128, stride=stride), :]
        theirs = other[pl.ds(f, 128, stride=stride), :]
        ordered[f, pl.ds(0, 128, stride=2), :] = jnp.where(core == 0, own, theirs)
        ordered[f, pl.ds(1, 128, stride=2), :] = jnp.where(core == 0, theirs, own)
    sub = lax.broadcasted_iota(jnp.int32, (8, LANES), 0)
    part, cell = lane_ids(8) >> 4, lane_ids(8) & 15
    first = (((sub - part) & 7) << 4) + cell
    last = (((part - sub) & 7) << 4) + cell
    for z in range(8):
        for f in range(count):
            for group in range(4):
                x = picked(ordered[f, pl.ds(z * 32 + 8 * group, 8), :], first)
                for k in (1, 2, 4):
                    x = jnp.where((part & k) != 0, pltpu.roll(x, 8 - k, 0), x)
                put(f, PAD + 8 * z, group, picked(x, last))


def folded(halves, kind):
    lane = lane_ids(halves[0].shape[0])
    even = (2 * lane) & (LANES - 1)

    def one(x):
        if kind == "low":
            return picked(x, even)
        if kind == "high":
            return picked(x, even + 1)
        return picked(x, even) + picked(x, even + 1)

    parts = [one(x) for x in halves]
    if len(parts) == 1:
        parts.append(jnp.zeros_like(parts[0]))
    return [jnp.where(lane < 64, parts[i], parts[i + 1]) for i in range(0, len(parts), 2)]


def doubled(x):
    lane = lane_ids(x.shape[0])
    return [picked(x, lane >> 1), picked(x, 64 + (lane >> 1))]


WHOLE = {3: (4, 64, 1), 4: (2, 32, 0), 5: (1, 16, 0), 6: (1, 8, 0)}


def whole_maps(level, raw, maps):
    halves, rows, first = WHOLE[level]
    size = rows

    def body(start):
        at = pl.ds(start, size)
        lane = lane_ids(size)
        for i in range(halves):
            scaled, scale, inverse = scaled_maps(
                [raw[m, first + i, at, :] for m in range(4)], 0.5**level
            )
            if i == 0:
                scaled[LEFT] = jnp.where(lane == 0, 0.0, scaled[LEFT])
            if i == halves - 1:
                last = 63 if level == 6 else LANES - 1
                scaled[RIGHT] = jnp.where(lane == last, 0.0, scaled[RIGHT])
            for m in range(4):
                maps[m, first + i, at, :] = scaled[m]
            maps[SCALE, first + i, at, :] = scale
            maps[INVERSE, first + i, at, :] = inverse

    chunks(0, rows, size, body)


def coarsen_whole(level, raw, next_raw):
    halves, rows, first = WHOLE[level]
    next_halves, next_rows, next_first = WHOLE[level + 1]
    for m in range(4):
        parts = []
        for h in range(halves):
            even, odd = even_odd(raw, (m, first + h), PAD, next_rows)
            parts.append(even if m == UP else odd if m == DOWN else even + odd)
        kind = "sum" if m in (UP, DOWN) else "low" if m == LEFT else "high"
        for h, x in enumerate(folded(parts, kind)):
            next_raw[m, next_first + h, PAD : PAD + next_rows, :] = 0.5 * x


def one_sweep(maps):
    coef = [maps[m, 0, PAD : PAD + 8, :] for m in range(4)]
    row = lax.broadcasted_iota(jnp.int32, (8, LANES), 0)
    coef[UP] = jnp.where(row == 0, 0.0, coef[UP])
    coef[DOWN] = jnp.where(row == 7, 0.0, coef[DOWN])
    steps = ((-1, 0), (1, 0), (0, -1), (0, 1))
    return dict(zip(steps, coef))


def moved(x, rows, columns):
    if rows:
        x = pltpu.roll(x, (-rows) % 8, 0)
    if columns:
        x = pltpu.roll(x, (-columns) % LANES, 1)
    return x


DIAMOND = [(a, b) for a in range(-4, 5) for b in range(-4, 5) if abs(a) + abs(b) <= 4]


def four_sweeps(maps, product):
    sweep = one_sweep(maps)
    whole = dict(sweep)
    whole[0, 0] = jnp.full((8, LANES), 1.0 - RELAX_WEIGHT, F32)
    for _ in range(3):
        grown = {at: (1.0 - RELAX_WEIGHT) * x for at, x in whole.items()}
        for step, coef in sweep.items():
            for at, x in whole.items():
                place = (at[0] + step[0], at[1] + step[1])
                term = coef * moved(x, *step)
                grown[place] = grown[place] + term if place in grown else term
        whole = grown
    for i, at in enumerate(DIAMOND):
        product[i] = moved(whole[at], -at[0], 0)


def coarse_solve(base, maps, product):
    sweep = one_sweep(maps)
    right_side = [base[c, 0, PAD : PAD + 8, :] for c in range(CHANNELS)]
    first = right_side
    for _ in range(3):
        first = [
            (1.0 - RELAX_WEIGHT) * v + g + sum(coef * moved(v, *at) for at, coef in sweep.items())
            for v, g in zip(first, right_side)
        ]
    values = first
    for _ in range(COARSE_SWEEPS // 4 - 1):
        lanes = [[moved(v, 0, b) for b in range(-4, 5)] for v in values]
        totals = [list() for _ in range(CHANNELS)]
        for a in range(-4, 5):
            sums = [None] * CHANNELS
            for i, at in enumerate(DIAMOND):
                if at[0] == a:
                    coef = product[i]
                    for c in range(CHANNELS):
                        term = coef * lanes[c][at[1] + 4]
                        sums[c] = term if sums[c] is None else sums[c] + term
            for c in range(CHANNELS):
                totals[c].append(moved(sums[c], a, 0))
        values = []
        for c in range(CHANNELS):
            t = totals[c]
            even = (t[0] + t[1]) + (t[2] + t[3])
            odd = (t[5] + t[6]) + (t[7] + t[8])
            values.append((first[c] + t[4]) + (even + odd))
    return values


def whole_cycle(level, bases, fields, others, maps, product):
    halves, rows, first = WHOLE[level]
    base, field, other, level_maps = bases[level], fields[level], others[level], maps[level]
    size = rows
    stencil("first", field, base, base, level_maps, 0, rows, size, 1, halves, first)
    stencil("residual", other, field, base, level_maps, 0, rows, size, 1, halves, first)
    next_halves, next_rows, next_first = WHOLE[level + 1]
    summed = []
    for h in range(halves):
        parts = []
        for c in range(CHANNELS):
            even, odd = even_odd(other, (c, first + h), PAD, next_rows)
            parts.append(even + odd)
        summed.append(jnp.concatenate(parts, axis=0))
    for h, x in enumerate(folded(summed, "sum")):
        inverse = 0.25 * maps[level + 1][INVERSE, next_first + h, PAD : PAD + next_rows, :]
        for c in range(CHANNELS):
            part = x[c * next_rows : (c + 1) * next_rows]
            bases[level + 1][c, next_first + h, PAD : PAD + next_rows, :] = part * inverse
    if level == 5:
        coarse = coarse_solve(bases[6], maps[6], product)
        coarse = [jnp.concatenate(coarse, axis=0)]
    else:
        whole_cycle(level + 1, bases, fields, others, maps, product)
        coarse = [
            jnp.concatenate(
                [
                    fields[level + 1][c, next_first + h, PAD : PAD + next_rows, :]
                    for c in range(CHANNELS)
                ],
                axis=0,
            )
            for h in range(next_halves)
        ]
    for m, x in enumerate(coarse):
        wide = doubled(x)
        for i in range(min(halves, 2)):
            h = first + 2 * m + i
            for c in range(CHANNELS):
                part = wide[i][c * next_rows : (c + 1) * next_rows]
                for offset in range(2):
                    at = pl.ds(PAD + offset, next_rows, stride=2)
                    field[c, h, at, :] = field[c, h, at, :] + part
    if level > 3:
        stencil("relax", other, field, base, level_maps, 0, rows, size, 1, halves, first)
        stencil("relax", field, other, base, level_maps, 0, rows, size, 1, halves, first)


def window(ref, index, place):
    group = lax.shift_right_logical(place[1], 3)
    offset = 16 * (place[1] & 7)
    at = pl.ds(pl.multiple_of(8 * place[0], 8), 24)
    lane = lane_ids(24)
    turn = lax.rem(LANES - offset, LANES)
    before, here, after = [pltpu.roll(ref[index, group + i, at, :], turn, 1) for i in range(3)]
    low = lane < 64
    fits = lane + offset < LANES
    return jnp.where(low, jnp.where(fits, here, after), jnp.where(fits, before, here))


def correct_level_two(
    place, bases, fields, maps, f2, target, near_maps, near_base, near_a, near_b
):
    for m in range(4):
        near_maps[m, 0, PAD : PAD + 24, :] = window(maps[3], m, place)
    edge = jnp.zeros((PAD, LANES), F32)
    for c in range(CHANNELS):
        near_base[c, 0, PAD : PAD + 24, :] = window(bases[3], c, place)
        near_a[c, 0, PAD : PAD + 24, :] = window(fields[3], c, place)
        for ref in (near_a, near_b):
            ref[c, 0, 0:PAD, :] = edge
            ref[c, 0, PAD + 24 : PAD + 32, :] = edge
    stencil("relax", near_b, near_a, near_base, near_maps, 0, 24, 24, 1, 1)
    stencil("relax", near_a, near_b, near_base, near_maps, 0, 24, 24, 1, 1)
    flat = jnp.concatenate([near_a[c, 0, PAD : PAD + 24, :] for c in range(CHANNELS)], axis=0)
    lane = lane_ids(flat.shape[0])
    wide = [picked(flat, lane >> 3), picked(flat, jnp.where(lane < 64, 16, 112) + (lane >> 3))]
    for c in range(CHANNELS):
        for h in range(2):
            part = wide[h][24 * c : 24 * c + 24]
            for offset in range(2):
                at = pl.ds(PAD + offset, 24, stride=2)
                target[c, h, at, :] = f2[c, h, at, :] + part


def add_rows(target, field, coarse, low, high, size):
    def body(start):
        for c in range(CHANNELS):
            for h in range(2):
                part = coarse[c, h, pl.ds(start, size), :]
                for offset in range(2):
                    at = pl.ds(2 * start - PAD + offset, size, stride=2)
                    target[c, h, at, :] = field[c, h, at, :] + part

    chunks(low, high, size, body)


def up_levels(ranges, spans, before, fields, bases, works, maps, extra):
    low, high, size = ranges[2]
    stencil("relax", works[2], fields[2], bases[2], maps[2], low, high, size, 4)
    stencil("relax", fields[2], works[2], bases[2], maps[2], low, high, size, 4)
    add_rows(fields[1], before[1], fields[2], *spans[1])
    low, high, size = ranges[1]
    stencil("relax", works[1], fields[1], bases[1], maps[1], low, high, size, 2)
    stencil("relax", fields[1], works[1], bases[1], maps[1], low, high, size, 2)
    add_rows(fields[0], before[0], fields[1], *spans[0])
    low, high, size = ranges[0]
    stencil("relax", works[0], fields[0], bases[0], maps[0], low, high, size, 1)
    if extra is None:
        stencil("relax", fields[0], works[0], bases[0], maps[0], low, high, size, 1)
    else:
        stencil(
            "relax_add", fields[0], works[0], bases[0], maps[0], low, high, size, 1, extra=extra
        )


def complete_maps(raw):
    size = 64
    at = pl.ds(PAD, size)
    lane = lane_ids(size)
    row = lax.broadcasted_iota(jnp.int32, (size, LANES), 0)
    ends = [raw[RIGHT, h, at, :] for h in range(1, 5)]
    shifted = beside([raw[LEFT, h, at, :] for h in range(1, 5)], 1)[1]
    last = ends[3]
    last = jnp.where((row & 7) == 7, pltpu.roll(pltpu.roll(last, 1, 1), 1, 0), last)
    shifted[3] = jnp.where(lane == LANES - 1, last, shifted[3])
    for i in range(4):
        below = raw[UP, 1 + i, pl.ds(PAD + 1, size), :]
        raw[DOWN, 1 + i, at, :] = jnp.where(row == size - 1, ends[i], below)
        raw[RIGHT, 1 + i, at, :] = shifted[i]


def middle_kernel(
    mine, other, m0, m1, m2, source, f0, g1, f1, g2, f2,
    m3, m4, m5, m6, product, solution, n0, h0, k1, h1, k2, h2, message,
    ordered, raw3, raw4, raw5, raw6, b3, v3, o3, b4, v4, o4, b5, v5, o5, b6,
    w0, w1, w2, near_maps, near_base, near_a, near_b,
):
    place = whereabouts()
    for ref in (m3, b3, v3):
        rows = ref.shape[2]
        clear(ref, (0, PAD), (rows - PAD, rows))
        for index in range(ref.shape[0]):
            for h in (0, 5):
                ref[index, h] = jnp.zeros((rows, LANES), F32)
    for ref in (b4, v4, o4, b5, v5, o5):
        rows = ref.shape[2]
        clear(ref, (0, PAD), (rows - PAD, rows))

    def put(f, start, group, tile):
        if f < CHANNELS:
            b3[f, 1 + group, pl.ds(start, 8), :] = tile
        else:
            slot = (UP, LEFT, RIGHT)[f - CHANNELS]
            raw3[slot, 1 + group, pl.ds(start, 8), :] = tile

    unpack(place, mine, other, 6, 6, ordered, put)
    complete_maps(raw3)
    raws = {3: raw3, 4: raw4, 5: raw5, 6: raw6}
    maps = {3: m3, 4: m4, 5: m5, 6: m6}
    whole_maps(3, raw3, m3)
    for level in (3, 4, 5):
        coarsen_whole(level, raws[level], raws[level + 1])
        whole_maps(level + 1, raws[level + 1], maps[level + 1])
    four_sweeps(m6, product)
    scale_base(b3, m3)
    whole_cycle(
        3, {3: b3, 4: b4, 5: b5, 6: b6}, {3: v3, 4: v4, 5: v5}, {3: o3, 4: o4, 5: o5}, maps,
        product,
    )
    correct_level_two(
        place, {3: b3}, {3: v3}, maps, f2, h2, near_maps, near_base, near_a, near_b
    )
    local_maps = (m0, m1, m2)
    up_levels(
        FIRST_UP, FIRST_SPANS, (f0, f1), (solution, h1, h2), (source, g1, g2), (w0, w1, w2), local_maps, None,
    )
    stencil("difference", n0, solution, source, m0, 32, 160, 128, 1)
    tiles = down_levels((h0, h1, h2), (n0, k1, k2), (w0, w1, w2), local_maps, LATER_DOWN)
    repeat(own_row(jnp.concatenate(tiles, axis=0)), message)


def scale_base(base, maps):
    halves, rows, first = WHOLE[3]

    def body(start):
        at = pl.ds(start, rows)
        for i in range(halves):
            inverse = maps[INVERSE, first + i, at, :]
            for c in range(CHANNELS):
                base[c, first + i, at, :] = base[c, first + i, at, :] * inverse

    chunks(0, rows, rows, body)


def last_kernel(
    mine, other, m0, m1, m2, source, m3, m4, m5, m6, product, before, n0, f0, k1, f1, k2, f2,
    solution, residual,
    ordered, b3, v3, o3, b4, v4, o4, b5, v5, o5, b6,
    h0, h1, h2, w0, w1, w2, near_maps, near_base, near_a, near_b,
):
    place = whereabouts()
    for ref in (b3, v3):
        rows = ref.shape[2]
        clear(ref, (0, PAD), (rows - PAD, rows))
        for index in range(ref.shape[0]):
            for h in (0, 5):
                ref[index, h] = jnp.zeros((rows, LANES), F32)
    for ref in (b4, v4, o4, b5, v5, o5):
        rows = ref.shape[2]
        clear(ref, (0, PAD), (rows - PAD, rows))

    def put(f, start, group, tile):
        b3[f, 1 + group, pl.ds(start, 8), :] = tile

    unpack(place, mine, other, CHANNELS, CHANNELS, ordered, put)
    maps = {3: m3, 4: m4, 5: m5, 6: m6}
    scale_base(b3, m3)
    whole_cycle(
        3, {3: b3, 4: b4, 5: b5, 6: b6}, {3: v3, 4: v4, 5: v5}, {3: o3, 4: o4, 5: o5}, maps,
        product,
    )
    correct_level_two(
        place, {3: b3}, {3: v3}, maps, f2, h2, near_maps, near_base, near_a, near_b
    )
    local_maps = (m0, m1, m2)
    up_levels(
        LATER_UP, LATER_SPANS, (f0, f1), (h0, h1, h2), (n0, k1, k2), (w0, w1, w2), local_maps, before,
    )
    stencil("final", w0, h0, source, m0, 64, 128, 64, 1)
    for c in range(CHANNELS):
        solution[c] = h0[c, 0, PAD + 64 : PAD + 128, :]
        residual[c] = w0[c, 0, PAD + 64 : PAD + 128, :]


def shape(*dims):
    return jax.ShapeDtypeStruct(dims, F32)


def field_shape(level, count):
    return (count, 2, LOCAL_ROWS[level] + 2 * PAD, LANES)


def whole_shape(level, count):
    halves, rows, first = WHOLE[level]
    return (count, halves + 2 * first, rows + 2 * PAD, LANES)


def call(kernel, outs, scratch, *args):
    in_specs = [pl.BlockSpec(memory_space=pltpu.VMEM) for _ in args]
    return pl.pallas_call(
        kernel,
        out_shape=[shape(*o) for o in outs],
        in_specs=in_specs,
        out_specs=[pl.BlockSpec(memory_space=pltpu.VMEM) for _ in outs],
        scratch_shapes=[pltpu.VMEM(s, F32) for s in scratch],
        compiler_params=pltpu.CompilerParams(vmem_limit_bytes=14 * 1024 * 1024),
        cost_estimate=pl.CostEstimate(flops=0, bytes_accessed=8_000_000, transcendentals=0),
    )(*args)


def ring(count, step):
    return [(i, (i + step) % count) for i in range(count)]


def gathered(message):
    mine = lax.all_to_all(message.reshape(128, 1, -1), CHIPS, 0, 0, tiled=True)
    mine = mine.reshape(message.shape)
    return mine, lax.ppermute(mine, "core", ring(2, 1))


def local(guidance, seam_weight, source_label):
    down, up = pl.pallas_call(
        stack_kernel,
        out_shape=[pltpu.VMEM((UPDOWN_ROWS, LANES), F32)] * 2,
        in_specs=[pl.BlockSpec(memory_space=pltpu.HBM)] * 3,
        out_specs=[pl.BlockSpec(memory_space=pltpu.VMEM)] * 2,
        scratch_shapes=[
            pltpu.VMEM((2, CHANNELS, 64, LANES), F32),
            pltpu.VMEM((64, LANES), jnp.int32),
            pltpu.VMEM((64, LANES), jnp.int32),
            pltpu.SemaphoreType.DMA((3,)),
        ],
        compiler_params=pltpu.CompilerParams(vmem_limit_bytes=58 * 1024 * 1024),
    )(guidance, seam_weight, source_label)
    above = lax.ppermute(down, "z", ring(8, 1))
    below = lax.ppermute(up, "z", ring(8, -1))
    own, ends = call(own_kernel, [(FIELDS, 64, LANES), (8, LANES)], [], down, up)
    swap, side, border = call(
        pack_kernel,
        [(SIDE_ROWS, LANES)] * 2 + [(CHANNELS, 176, LANES)],
        [],
        own, ends, above, below,
    )
    swapped = lax.ppermute(swap, "core", ring(2, 1))
    pairs = [(i, min(max(i + 2 * (i % 2) - 1, 0), 31)) for i in range(32)]
    sided = lax.ppermute(side, SIDES, pairs)
    fields = [field_shape(level, CHANNELS) for level in range(3)]
    maps = [field_shape(0, 5), field_shape(1, 6), field_shape(2, 6)]
    raws = [field_shape(level, 4) for level in range(3)]
    m0, m1, m2, source, f0, g1, f1, g2, f2, message = call(
        setup_kernel,
        maps + [fields[0], fields[0], fields[1], fields[1], fields[2], fields[2], (6 * 128, LANES)],
        [field_shape(0, FIELDS)] + raws + fields,
        own, ends, above, below, swapped, sided, border,
    )
    mine, other = gathered(message)
    wholes = [whole_shape(level, CHANNELS) for level in (3, 4, 5) for _ in range(3)]
    wholes = wholes + [whole_shape(6, CHANNELS)]
    near = [(4, 1, 40, LANES)] + [(CHANNELS, 1, 40, LANES)] * 3
    m3, m4, m5, m6, product, solution, n0, h0, k1, h1, k2, h2, message = call(
        middle_kernel,
        [whole_shape(level, 6) for level in (3, 4, 5, 6)]
        + [(len(DIAMOND), 8, LANES)] + [fields[0]] * 3 + [fields[1]] * 2 + [fields[2]] * 2 + [(CHANNELS * 128, LANES)],
        [(6, 256, LANES)] + [whole_shape(level, 4) for level in (3, 4, 5, 6)]
        + wholes + fields + near,
        mine, other, m0, m1, m2, source, f0, g1, f1, g2, f2,
    )
    mine, other = gathered(message)
    outs = call(
        last_kernel,
        [(CHANNELS, 64, LANES)] * 2,
        [(CHANNELS, 256, LANES)] + wholes + fields + fields + near,
        mine, other, m0, m1, m2, source, m3, m4, m5, m6, product,
        solution, n0, h0, k1, h1, k2, h2,
    )
    return tuple(outs)


def solution(mesh):
    fine = Mesh(mesh.devices.reshape(8, 4, 4, 2), ("z", "y", "x", "core"))
    return jax.shard_map(
        local,
        mesh=fine,
        in_specs=(P(None, None, "z", SIDES), P("z", SIDES), P("z", SIDES)),
        out_specs=(P(None, "z", SIDES), P(None, "z", SIDES)),
        check_vma=False,
    )
```

```python
import jax
import jax.numpy as jnp
from jax import lax
from jax.experimental import pallas as pl
from jax.experimental.pallas import tpu as pltpu
from jax.sharding import Mesh, PartitionSpec as P

F32 = jnp.float32
CHANNELS = 3
COARSE_SWEEPS = 48
RELAX_WEIGHT = 0.8
SEAM_FACTOR = 0.25
PAD = 8
LANES = 128
REACH = 56
SIDES = ("y", "x", "core")
CHIPS = ("z", "y", "x")
LOCAL_ROWS = (192, 96, 48)
STEP, STEP_R, STEP_F, STEP_C, STEP_A, STEP_W = 8, 16, 16, 16, 8, 16
UP, DOWN, LEFT, RIGHT, SCALE, INVERSE = range(6)


def lane_ids(rows):
    return lax.broadcasted_iota(jnp.int32, (rows, LANES), 1)


def beside(halves, width):
    count = len(halves)
    lane = lane_ids(halves[0].shape[0])
    ahead = [pltpu.roll(x, width, 1) for x in halves]
    behind = [pltpu.roll(x, LANES - width, 1) for x in halves]
    if count == 1:
        return ahead, behind
    left = [jnp.where(lane < width, ahead[h - 1], ahead[h]) for h in range(count)]
    right = [
        jnp.where(lane >= LANES - width, behind[(h + 1) % count], behind[h]) for h in range(count)
    ]
    return left, right


def pair_sum(x, width):
    low = (lane_ids(x.shape[0]) & width) == 0
    return x + jnp.where(low, pltpu.roll(x, LANES - width, 1), pltpu.roll(x, width, 1))


def low_of_pair(x, width):
    low = (lane_ids(x.shape[0]) & width) == 0
    return jnp.where(low, x, pltpu.roll(x, width, 1))


def high_of_pair(x, width):
    low = (lane_ids(x.shape[0]) & width) == 0
    return jnp.where(low, pltpu.roll(x, LANES - width, 1), x)


def picked(x, lanes):
    return jnp.take_along_axis(x, lanes, axis=1, mode="promise_in_bounds")


def chunks(low, high, step, body):
    for start in range(low, high, step):
        body(PAD + start, min(step, high - start))


def stencil(mode, target, field, base, maps, low, high, size, width=1, halves=2, first=0, extra=None):
    def body(start, size):
        at = pl.ds(start, size)
        span = range(first, first + halves)
        coef = [[maps[m, h, at, :] for h in span] for m in range(4)]
        for c in range(CHANNELS):
            here = [field[c, h, at, :] for h in span]
            above = [field[c, h, pl.ds(start - 1, size), :] for h in span]
            below = [field[c, h, pl.ds(start + 1, size), :] for h in span]
            left, right = beside(here, width)
            for i, h in enumerate(span):
                near = (above[i], below[i], left[i], right[i])
                if mode in ("difference", "scaled_difference", "final"):
                    near = [n - here[i] for n in near]
                total = coef[0][i] * near[0] + coef[1][i] * near[1]
                total = total + (coef[2][i] * near[2] + coef[3][i] * near[3])
                if mode == "first":
                    result = (2.0 - RELAX_WEIGHT) * here[i] + total
                elif mode == "relax":
                    result = (1.0 - RELAX_WEIGHT) * here[i] + base[c, h, at, :] + total
                elif mode == "relax_add":
                    result = (1.0 - RELAX_WEIGHT) * here[i] + base[c, h, at, :] + total
                    result = extra[c, h, at, :] + result
                elif mode == "residual":
                    result = base[c, h, at, :] - RELAX_WEIGHT * here[i] + total
                    result = maps[SCALE, h, at, :] * result
                elif mode == "difference":
                    result = base[c, h, at, :] + total
                else:
                    result = maps[SCALE, h, at, :] * (base[c, h, at, :] + total)
                target[c, h, at, :] = result

    chunks(low, high, STEP, body)


def scaled_maps(raw, factor):
    whole = raw[0] + raw[1] + raw[2] + raw[3]
    inside = whole > 0.0
    share = jnp.where(inside, RELAX_WEIGHT / jnp.where(inside, whole, 1.0), 0.0)
    return [r * share for r in raw], whole * (factor / RELAX_WEIGHT), share * (1.0 / factor)


def even_odd(ref, lead, start, count):
    return (
        ref[lead + (pl.ds(start, count, stride=2), slice(None))],
        ref[lead + (pl.ds(start + 1, count, stride=2), slice(None))],
    )


FIELDS = 5
WEIGHT, LABEL = 3, 4
UPDOWN_ROWS = FIELDS * REACH + 8
SIDE_ROWS = FIELDS * 88 + 16


def stack_kernel(guidance_in, weight_in, label_in, down, up, guidance, weight_at, label_at, arrived):
    copies = [
        pltpu.make_async_copy(source, target, arrived.at[i])
        for i, (source, target) in enumerate(
            ((guidance_in, guidance), (weight_in, weight_at), (label_in, label_at))
        )
    ]
    for copy in copies:
        copy.start()
    for copy in copies:
        copy.wait()
    weight, label = weight_at[...].astype(F32), label_at[...].astype(F32)
    row = lax.broadcasted_iota(jnp.int32, (64, LANES), 0)
    lane = lane_ids(64)

    def edge(turn, axis, inside):
        matching = jnp.where(pltpu.roll(label, turn, axis) == label, 1.0 / 64.0, SEAM_FACTOR / 64.0)
        return jnp.where(inside, (weight + pltpu.roll(weight, turn, axis)) * matching, 0.0)

    below, right = edge(63, 0, row < 63), edge(LANES - 1, 1, lane < LANES - 1)

    def put(a, x):
        down[REACH * a : REACH * (a + 1), :] = x[64 - REACH :]
        up[REACH * a : REACH * (a + 1), :] = x[:REACH]

    ends = [guidance[0, c, 63:64, :] for c in range(CHANNELS)]
    for c in range(CHANNELS):
        first, second = below * guidance[0, c], right * guidance[1, c]
        put(c, (pltpu.roll(first, 1, 0) - first) + (pltpu.roll(second, 1, 1) - second))
        last = jnp.broadcast_to(guidance[1, c, :, LANES - 1 :], (64, LANES))
        ends.append(jnp.sum(jnp.where(row == lane, last, 0.0), axis=0, keepdims=True))
    put(WEIGHT, weight)
    put(LABEL, label)
    ends = jnp.concatenate(ends + [jnp.zeros((2, LANES), F32)], axis=0)
    down[FIELDS * REACH :, :] = ends
    up[FIELDS * REACH :, :] = ends


def own_kernel(down, up, own, ends):
    for a in range(FIELDS):
        own[a, :REACH, :] = up[REACH * a : REACH * (a + 1), :]
        own[a, REACH:, :] = down[REACH * (a + 1) - (64 - REACH) : REACH * (a + 1), :]
    ends[...] = up[FIELDS * REACH :, :]


def upright(row, first, count):
    place = first + lax.broadcasted_iota(jnp.int32, (count, LANES), 0)
    return picked(jnp.broadcast_to(row, (count, LANES)), place)


def whereabouts():
    core = lax.axis_index("core")
    chip = lax.axis_index("y") * 4 + lax.axis_index("x")
    return lax.axis_index("z"), 2 * chip + core, core


def pack_kernel(own, ends, above, below, swap, side, edge):
    first_core = whereabouts()[2] == 0
    low = lane_ids(88) < 64
    base = FIELDS * REACH

    def halves(x):
        return x[:88], pltpu.roll(x[88:], 64, 1)

    for a in range(FIELDS):
        at = slice(REACH * a, REACH * (a + 1))
        whole = jnp.concatenate([above[at, :], own[a], below[at, :]], axis=0)
        top, bottom = halves(whole)
        to_left = jnp.where(low, top, bottom)
        if a < CHANNELS:
            column = jnp.concatenate(
                [
                    upright(above[base + 3 + a : base + 4 + a, :], 64 - REACH, REACH),
                    upright(ends[3 + a : 4 + a, :], 0, 64),
                    upright(below[base + 3 + a : base + 4 + a, :], 0, REACH),
                ],
                axis=0,
            )
            edge[a] = column
            top, bottom = halves(jnp.where(lane_ids(176) == 64, column, whole))
        to_right = jnp.where(low, bottom, top)
        at = slice(88 * a, 88 * (a + 1))
        swap[at, :] = jnp.where(first_core, to_right, to_left)
        side[at, :] = jnp.where(first_core, to_left, to_right)
    for ref in (swap, side):
        ref[88 * FIELDS : 88 * FIELDS + 8, :] = above[base:, :]
        ref[88 * FIELDS + 8 :, :] = ends[...]


def local_down(level, field, base, work, maps, next_base, next_maps, first_rows, rest_rows, next_rows):
    width = 2**level
    low, high, size = first_rows
    stencil("first", field, base, base, maps, low, high, size, width)
    low, high, size = rest_rows
    stencil("scaled_difference", work, field, base, maps, low, high, size, width)
    if next_base is None:
        return

    low, high, size = next_rows

    def body(start, size):
        at = pl.ds(start, size)
        for h in range(2):
            inverse = 0.25 * next_maps[INVERSE, h, at, :]
            for c in range(CHANNELS):
                even, odd = even_odd(work, (c, h), 2 * start - PAD, size)
                next_base[c, h, at, :] = pair_sum(even + odd, width) * inverse

    chunks(low, high, STEP_R, body)


def own_row(x):
    count = x.shape[0] // 8
    spread = picked(x, 8 * (lane_ids(x.shape[0]) & 15))
    rows = []
    keep = (lane_ids(8) >> 4) == lax.broadcasted_iota(jnp.int32, (8, LANES), 0)
    for i in range(count):
        part = jnp.where(keep, spread[8 * i : 8 * i + 8], 0.0)
        rows.append(jnp.sum(part, axis=0, keepdims=True))
    return rows


def repeat(rows, message):
    block = jnp.concatenate(rows * (24 // len(rows)), axis=0)
    for i in range(message.shape[0] // 24):
        message[24 * i : 24 * i + 24, :] = block


def down_levels(fields, bases, work, maps, ranges):
    for level in range(3):
        local_down(
            level,
            fields[level],
            bases[level],
            work[level],
            maps[level],
            bases[level + 1] if level < 2 else None,
            maps[level + 1] if level < 2 else None,
            *ranges[level],
        )
    tiles = []
    for c in range(CHANNELS):
        even, odd = even_odd(work[2], (c, 0), PAD + 16, 8)
        tiles.append(0.25 * pair_sum(even + odd, 4))
    return tiles


FIRST_DOWN = (
    ((8, 184, 176), (8, 184, 176), (0, 96, 96)),
    ((0, 96, 96), (0, 96, 96), (0, 48, 48)),
    ((0, 48, 48), (0, 48, 48), None),
)
LATER_DOWN = (
    ((32, 160, 128), (32, 160, 128), (16, 80, 64)),
    ((16, 80, 64), (16, 80, 64), (8, 40, 32)),
    ((8, 40, 32), (8, 40, 32), None),
)
FIRST_UP = ((32, 160, 128), (8, 88, 80), (0, 48, 48))
LATER_UP = ((56, 136, 80), (24, 72, 48), (8, 40, 32))
FIRST_SPANS = ((8, 88, 80), (0, 48, 48))
LATER_SPANS = ((24, 72, 48), (8, 40, 32))


def clear(ref, *bounds):
    for index in range(ref.shape[0]):
        for h in range(ref.shape[1]):
            for low, high in bounds:
                ref[index, h, low:high, :] = jnp.zeros((high - low, LANES), F32)


def setup_kernel(
    own, ends, above, below, swapped, sided, border,
    m0, m1, m2, source, f0, g1, f1, g2, f2, message,
    cells, raw0, raw1, raw2, w0, w1, w2,
):
    row_at, col_at, core = whereabouts()
    first_core = core == 0
    rows_of = lambda n, low: low + lax.broadcasted_iota(jnp.int32, (n, LANES), 0)
    edge = jnp.zeros((16, LANES), F32)
    not_top, not_bottom = row_at > 0, row_at < 7
    low = lane_ids(88) < 64
    inside = (low & (col_at < 31)) | (~low & (col_at > 0))

    def sides(start, size):
        one, two = swapped[start : start + size, :], sided[start : start + size, :]
        return jnp.where(first_core, one, two), jnp.where(first_core, two, one)

    for a in range(FIELDS):
        at = slice(REACH * a, REACH * (a + 1))
        for h in range(2):
            cells[a, h, 0:16, :] = edge
            cells[a, h, 192:208, :] = edge
        cells[a, 0, 16:72, :] = jnp.where(not_top, above[at, :], 0.0)
        cells[a, 0, 72:136, :] = own[a]
        cells[a, 0, 136:192, :] = jnp.where(not_bottom, below[at, :], 0.0)
        from_right, from_left = sides(88 * a, 88)
        top = jnp.where(low, from_right, from_left)
        bottom = pltpu.roll(jnp.where(low, from_left, from_right), 64, 1)
        cells[a, 1, 16:104, :] = jnp.where(inside & (not_top | (rows_of(88, 8) >= 64)), top, 0.0)
        cells[a, 1, 104:192, :] = jnp.where(
            inside & (not_bottom | (rows_of(88, 96) < 128)), bottom, 0.0
        )
    def fine(start, size):
        at = pl.ds(start, size)
        up_at, down_at = pl.ds(start - 1, size), pl.ds(start + 1, size)
        weights = [cells[WEIGHT, h, at, :] for h in range(2)]
        labels = [cells[LABEL, h, at, :] for h in range(2)]
        weight_sides = beside(weights, 1)
        label_sides = beside(labels, 1)
        coef, shares = [], []
        for h in range(2):
            near_weights = (
                cells[WEIGHT, h, up_at, :], cells[WEIGHT, h, down_at, :], weight_sides[0][h], weight_sides[1][h],
            )
            near_labels = (
                cells[LABEL, h, up_at, :], cells[LABEL, h, down_at, :], label_sides[0][h], label_sides[1][h],
            )
            raw = []
            for m in range(4):
                matching = jnp.where(near_labels[m] == labels[h], 1.0 / 64.0, SEAM_FACTOR / 64.0)
                value = (weights[h] + near_weights[m]) * matching
                value = jnp.where(weights[h] > 0.0, value, 0.0)
                raw.append(value)
                raw0[m, h, at, :] = value
            scaled, scale, share = scaled_maps(raw, 1.0)
            shares.append(share)
            for m in range(4):
                m0[m, h, at, :] = scaled[m]
            m0[SCALE, h, at, :] = scale
            coef.append(scaled)
        for c in range(CHANNELS):
            part = [cells[c, h, at, :] for h in range(2)]
            own_end = border[c, start - PAD - 8 : start - PAD - 8 + size, :]
            left_end = pltpu.roll(part[1], 64, 1), pltpu.roll(part[1], 63, 1)
            first, last = lane_ids(size) == 0, lane_ids(size) == LANES - 1
            flux = jnp.where(first, coef[0][LEFT] * left_end[0], 0.0)
            flux = flux - jnp.where(last, coef[0][RIGHT] * own_end, 0.0)
            source[c, 0, at, :] = shares[0] * part[0] + flux
            flux = jnp.where(first, coef[1][LEFT] * own_end, 0.0)
            flux = flux - jnp.where(last, coef[1][RIGHT] * left_end[1], 0.0)
            source[c, 1, at, :] = shares[1] * part[1] + flux

    chunks(8, 184, STEP_F, fine)
    from_right, from_left = sides(88 * FIELDS, 16)
    beside_own = jnp.where(lane_ids(16) < 64, from_right, from_left)
    for first, upper in ((0, 71), (8, 135)):
        for c in range(CHANNELS):
            if first == 0:
                straight = above[FIELDS * REACH + c : FIELDS * REACH + c + 1, :]
            else:
                straight = ends[c : c + 1, :]
            for h, flow in ((0, straight), (1, beside_own[first + c : first + c + 1])):
                if first == 0:
                    flow = jnp.where(not_top, flow, 0.0)
                one, two = pl.ds(upper, 1), pl.ds(upper + 1, 1)
                source[c, h, one, :] = source[c, h, one, :] - m0[DOWN, h, one, :] * flow
                source[c, h, two, :] = source[c, h, two, :] + m0[UP, h, two, :] * flow

    def coarser(raw, width, start, size, h):
        parts = []
        for m in range(4):
            even, odd = even_odd(raw, (m, h), start, size)
            if m == UP:
                parts.append(0.5 * pair_sum(even, width))
            elif m == DOWN:
                parts.append(0.5 * pair_sum(odd, width))
            elif m == LEFT:
                parts.append(0.5 * low_of_pair(even + odd, width))
            else:
                parts.append(0.5 * high_of_pair(even + odd, width))
        return parts

    for level, fine_raw, raw, maps, rows in ((1, raw0, raw1, m1, 96), (2, raw1, raw2, m2, 48)):

        def coarse(start, size, level=level, fine_raw=fine_raw, raw=raw, maps=maps):
            at = pl.ds(start, size)
            for h in range(2):
                parts = coarser(fine_raw, 2 ** (level - 1), 2 * start - PAD, size, h)
                scaled, scale, inverse = scaled_maps(parts, 0.5**level)
                for m in range(4):
                    raw[m, h, at, :] = parts[m]
                    maps[m, h, at, :] = scaled[m]
                maps[SCALE, h, at, :] = scale
                maps[INVERSE, h, at, :] = inverse

        chunks(0, rows, STEP_C, coarse)
    tiles = down_levels((f0, f1, f2), (source, g1, g2), (w0, w1, w2), (m0, m1, m2), FIRST_DOWN)
    upward, downward, leftward, rightward = coarser(raw2, 4, PAD + 16, 8, 0)
    row = lax.broadcasted_iota(jnp.int32, (8, LANES), 0)
    cell = lane_ids(8) >> 3
    turned = pltpu.roll(pltpu.roll(rightward, LANES - 8, 1), 7, 0)
    ends = jnp.where(row == 7, downward, jnp.where(cell == 15, rightward, turned))
    repeat(own_row(jnp.concatenate(tiles + [upward, leftward, ends], axis=0)), message)


def unpack(place, mine, other, count, stride, ordered, put):
    core = place[2]
    for f in range(count):
        own = mine[pl.ds(f, 128, stride=stride), :]
        theirs = other[pl.ds(f, 128, stride=stride), :]
        ordered[f, pl.ds(0, 128, stride=2), :] = jnp.where(core == 0, own, theirs)
        ordered[f, pl.ds(1, 128, stride=2), :] = jnp.where(core == 0, theirs, own)
    sub = lax.broadcasted_iota(jnp.int32, (8, LANES), 0)
    part, cell = lane_ids(8) >> 4, lane_ids(8) & 15
    first = (((sub - part) & 7) << 4) + cell
    last = (((part - sub) & 7) << 4) + cell
    for z in range(8):
        for f in range(count):
            for group in range(4):
                x = picked(ordered[f, pl.ds(z * 32 + 8 * group, 8), :], first)
                for k in (1, 2, 4):
                    x = jnp.where((part & k) != 0, pltpu.roll(x, 8 - k, 0), x)
                put(f, PAD + 8 * z, group, picked(x, last))


def folded(halves, kind):
    lane = lane_ids(halves[0].shape[0])
    even = (2 * lane) & (LANES - 1)

    def one(x):
        if kind == "low":
            return picked(x, even)
        if kind == "high":
            return picked(x, even + 1)
        return picked(x, even) + picked(x, even + 1)

    parts = [one(x) for x in halves]
    if len(parts) == 1:
        parts.append(jnp.zeros_like(parts[0]))
    return [jnp.where(lane < 64, parts[i], parts[i + 1]) for i in range(0, len(parts), 2)]


def doubled(x):
    lane = lane_ids(x.shape[0])
    return [picked(x, lane >> 1), picked(x, 64 + (lane >> 1))]


WHOLE = {3: (4, 64, 1), 4: (2, 32, 0), 5: (1, 16, 0), 6: (1, 8, 0)}


def whole_maps(level, raw, maps):
    halves, rows, first = WHOLE[level]

    def body(start, size):
        at = pl.ds(start, size)
        lane = lane_ids(size)
        for i in range(halves):
            scaled, scale, inverse = scaled_maps(
                [raw[m, first + i, at, :] for m in range(4)], 0.5**level
            )
            if i == 0:
                scaled[LEFT] = jnp.where(lane == 0, 0.0, scaled[LEFT])
            if i == halves - 1:
                last = 63 if level == 6 else LANES - 1
                scaled[RIGHT] = jnp.where(lane == last, 0.0, scaled[RIGHT])
            for m in range(4):
                maps[m, first + i, at, :] = scaled[m]
            maps[SCALE, first + i, at, :] = scale
            maps[INVERSE, first + i, at, :] = inverse

    chunks(0, rows, STEP_W, body)


def coarsen_whole(level, raw, next_raw):
    halves, rows, first = WHOLE[level]
    next_halves, next_rows, next_first = WHOLE[level + 1]
    for m in range(4):
        parts = []
        for h in range(halves):
            even, odd = even_odd(raw, (m, first + h), PAD, next_rows)
            parts.append(even if m == UP else odd if m == DOWN else even + odd)
        kind = "sum" if m in (UP, DOWN) else "low" if m == LEFT else "high"
        for h, x in enumerate(folded(parts, kind)):
            next_raw[m, next_first + h, PAD : PAD + next_rows, :] = 0.5 * x


def one_sweep(maps):
    coef = [maps[m, 0, PAD : PAD + 8, :] for m in range(4)]
    row = lax.broadcasted_iota(jnp.int32, (8, LANES), 0)
    coef[UP] = jnp.where(row == 0, 0.0, coef[UP])
    coef[DOWN] = jnp.where(row == 7, 0.0, coef[DOWN])
    steps = ((-1, 0), (1, 0), (0, -1), (0, 1))
    return dict(zip(steps, coef))


def moved(x, rows, columns):
    if rows:
        x = pltpu.roll(x, (-rows) % 8, 0)
    if columns:
        x = pltpu.roll(x, (-columns) % LANES, 1)
    return x


DIAMOND = [(a, b) for a in range(-4, 5) for b in range(-4, 5) if abs(a) + abs(b) <= 4]


def four_sweeps(maps, product):
    sweep = one_sweep(maps)
    whole = dict(sweep)
    whole[0, 0] = jnp.full((8, LANES), 1.0 - RELAX_WEIGHT, F32)
    for _ in range(3):
        grown = {at: (1.0 - RELAX_WEIGHT) * x for at, x in whole.items()}
        for step, coef in sweep.items():
            for at, x in whole.items():
                place = (at[0] + step[0], at[1] + step[1])
                term = coef * moved(x, *step)
                grown[place] = grown[place] + term if place in grown else term
        whole = grown
    for i, at in enumerate(DIAMOND):
        product[i] = moved(whole[at], -at[0], 0)


def coarse_solve(base, maps, product):
    sweep = one_sweep(maps)
    right_side = [base[c, 0, PAD : PAD + 8, :] for c in range(CHANNELS)]
    first = right_side
    for _ in range(3):
        first = [
            (1.0 - RELAX_WEIGHT) * v + g + sum(coef * moved(v, *at) for at, coef in sweep.items())
            for v, g in zip(first, right_side)
        ]
    values = first
    for _ in range(COARSE_SWEEPS // 4 - 1):
        lanes = [[moved(v, 0, b) for b in range(-4, 5)] for v in values]
        totals = [list() for _ in range(CHANNELS)]
        for a in range(-4, 5):
            sums = [None] * CHANNELS
            for i, at in enumerate(DIAMOND):
                if at[0] == a:
                    coef = product[i]
                    for c in range(CHANNELS):
                        term = coef * lanes[c][at[1] + 4]
                        sums[c] = term if sums[c] is None else sums[c] + term
            for c in range(CHANNELS):
                totals[c].append(moved(sums[c], a, 0))
        values = []
        for c in range(CHANNELS):
            t = totals[c]
            even = (t[0] + t[1]) + (t[2] + t[3])
            odd = (t[5] + t[6]) + (t[7] + t[8])
            values.append((first[c] + t[4]) + (even + odd))
    return values


def whole_cycle(level, bases, fields, others, maps, product):
    halves, rows, first = WHOLE[level]
    base, field, other, level_maps = bases[level], fields[level], others[level], maps[level]
    size = rows
    stencil("first", field, base, base, level_maps, 0, rows, size, 1, halves, first)
    stencil("residual", other, field, base, level_maps, 0, rows, size, 1, halves, first)
    next_halves, next_rows, next_first = WHOLE[level + 1]
    summed = []
    for h in range(halves):
        parts = []
        for c in range(CHANNELS):
            even, odd = even_odd(other, (c, first + h), PAD, next_rows)
            parts.append(even + odd)
        summed.append(jnp.concatenate(parts, axis=0))
    for h, x in enumerate(folded(summed, "sum")):
        inverse = 0.25 * maps[level + 1][INVERSE, next_first + h, PAD : PAD + next_rows, :]
        for c in range(CHANNELS):
            part = x[c * next_rows : (c + 1) * next_rows]
            bases[level + 1][c, next_first + h, PAD : PAD + next_rows, :] = part * inverse
    if level == 5:
        coarse = coarse_solve(bases[6], maps[6], product)
        coarse = [jnp.concatenate(coarse, axis=0)]
    else:
        whole_cycle(level + 1, bases, fields, others, maps, product)
        coarse = [
            jnp.concatenate(
                [
                    fields[level + 1][c, next_first + h, PAD : PAD + next_rows, :]
                    for c in range(CHANNELS)
                ],
                axis=0,
            )
            for h in range(next_halves)
        ]
    for m, x in enumerate(coarse):
        wide = doubled(x)
        for i in range(min(halves, 2)):
            h = first + 2 * m + i
            for c in range(CHANNELS):
                part = wide[i][c * next_rows : (c + 1) * next_rows]
                for offset in range(2):
                    at = pl.ds(PAD + offset, next_rows, stride=2)
                    field[c, h, at, :] = field[c, h, at, :] + part
    if level > 3:
        stencil("relax", other, field, base, level_maps, 0, rows, size, 1, halves, first)
        stencil("relax", field, other, base, level_maps, 0, rows, size, 1, halves, first)


def window(ref, index, place):
    group = lax.shift_right_logical(place[1], 3)
    offset = 16 * (place[1] & 7)
    at = pl.ds(pl.multiple_of(8 * place[0], 8), 24)
    lane = lane_ids(24)
    turn = lax.rem(LANES - offset, LANES)
    before, here, after = [pltpu.roll(ref[index, group + i, at, :], turn, 1) for i in range(3)]
    low = lane < 64
    fits = lane + offset < LANES
    return jnp.where(low, jnp.where(fits, here, after), jnp.where(fits, before, here))


def correct_level_two(
    place, bases, fields, maps, f2, target, near_maps, near_base, near_a, near_b
):
    for m in range(4):
        near_maps[m, 0, PAD : PAD + 24, :] = window(maps[3], m, place)
    edge = jnp.zeros((PAD, LANES), F32)
    for c in range(CHANNELS):
        near_base[c, 0, PAD : PAD + 24, :] = window(bases[3], c, place)
        near_a[c, 0, PAD : PAD + 24, :] = window(fields[3], c, place)
        for ref in (near_a, near_b):
            ref[c, 0, 0:PAD, :] = edge
            ref[c, 0, PAD + 24 : PAD + 32, :] = edge
    stencil("relax", near_b, near_a, near_base, near_maps, 0, 24, 24, 1, 1)
    stencil("relax", near_a, near_b, near_base, near_maps, 0, 24, 24, 1, 1)
    flat = jnp.concatenate([near_a[c, 0, PAD : PAD + 24, :] for c in range(CHANNELS)], axis=0)
    lane = lane_ids(flat.shape[0])
    wide = [picked(flat, lane >> 3), picked(flat, jnp.where(lane < 64, 16, 112) + (lane >> 3))]
    for c in range(CHANNELS):
        for h in range(2):
            part = wide[h][24 * c : 24 * c + 24]
            for offset in range(2):
                at = pl.ds(PAD + offset, 24, stride=2)
                target[c, h, at, :] = f2[c, h, at, :] + part


def add_rows(target, field, coarse, low, high, size):
    def body(start, size):
        for c in range(CHANNELS):
            for h in range(2):
                part = coarse[c, h, pl.ds(start, size), :]
                for offset in range(2):
                    at = pl.ds(2 * start - PAD + offset, size, stride=2)
                    target[c, h, at, :] = field[c, h, at, :] + part

    chunks(low, high, STEP_A, body)


def up_levels(ranges, spans, before, fields, bases, works, maps, extra):
    low, high, size = ranges[2]
    stencil("relax", works[2], fields[2], bases[2], maps[2], low, high, size, 4)
    stencil("relax", fields[2], works[2], bases[2], maps[2], low, high, size, 4)
    add_rows(fields[1], before[1], fields[2], *spans[1])
    low, high, size = ranges[1]
    stencil("relax", works[1], fields[1], bases[1], maps[1], low, high, size, 2)
    stencil("relax", fields[1], works[1], bases[1], maps[1], low, high, size, 2)
    add_rows(fields[0], before[0], fields[1], *spans[0])
    low, high, size = ranges[0]
    stencil("relax", works[0], fields[0], bases[0], maps[0], low, high, size, 1)
    if extra is None:
        stencil("relax", fields[0], works[0], bases[0], maps[0], low, high, size, 1)
    else:
        stencil(
            "relax_add", fields[0], works[0], bases[0], maps[0], low, high, size, 1, extra=extra
        )


def complete_maps(raw):
    size = 64
    at = pl.ds(PAD, size)
    lane = lane_ids(size)
    row = lax.broadcasted_iota(jnp.int32, (size, LANES), 0)
    ends = [raw[RIGHT, h, at, :] for h in range(1, 5)]
    shifted = beside([raw[LEFT, h, at, :] for h in range(1, 5)], 1)[1]
    last = ends[3]
    last = jnp.where((row & 7) == 7, pltpu.roll(pltpu.roll(last, 1, 1), 1, 0), last)
    shifted[3] = jnp.where(lane == LANES - 1, last, shifted[3])
    for i in range(4):
        below = raw[UP, 1 + i, pl.ds(PAD + 1, size), :]
        raw[DOWN, 1 + i, at, :] = jnp.where(row == size - 1, ends[i], below)
        raw[RIGHT, 1 + i, at, :] = shifted[i]


def middle_kernel(
    mine, other, m0, m1, m2, source, f0, g1, f1, g2, f2,
    m3, m4, m5, m6, product, solution, n0, h0, k1, h1, k2, h2, message,
    ordered, raw3, raw4, raw5, raw6, b3, v3, o3, b4, v4, o4, b5, v5, o5, b6,
    w0, w1, w2, near_maps, near_base, near_a, near_b,
):
    place = whereabouts()
    for ref in (m3, b3, v3):
        rows = ref.shape[2]
        clear(ref, (0, PAD), (rows - PAD, rows))
        for index in range(ref.shape[0]):
            for h in (0, 5):
                ref[index, h] = jnp.zeros((rows, LANES), F32)
    for ref in (b4, v4, o4, b5, v5, o5):
        rows = ref.shape[2]
        clear(ref, (0, PAD), (rows - PAD, rows))

    def put(f, start, group, tile):
        if f < CHANNELS:
            b3[f, 1 + group, pl.ds(start, 8), :] = tile
        else:
            slot = (UP, LEFT, RIGHT)[f - CHANNELS]
            raw3[slot, 1 + group, pl.ds(start, 8), :] = tile

    unpack(place, mine, other, 6, 6, ordered, put)
    complete_maps(raw3)
    raws = {3: raw3, 4: raw4, 5: raw5, 6: raw6}
    maps = {3: m3, 4: m4, 5: m5, 6: m6}
    whole_maps(3, raw3, m3)
    for level in (3, 4, 5):
        coarsen_whole(level, raws[level], raws[level + 1])
        whole_maps(level + 1, raws[level + 1], maps[level + 1])
    four_sweeps(m6, product)
    scale_base(b3, m3)
    whole_cycle(
        3, {3: b3, 4: b4, 5: b5, 6: b6}, {3: v3, 4: v4, 5: v5}, {3: o3, 4: o4, 5: o5}, maps,
        product,
    )
    correct_level_two(
        place, {3: b3}, {3: v3}, maps, f2, h2, near_maps, near_base, near_a, near_b
    )
    local_maps = (m0, m1, m2)
    up_levels(
        FIRST_UP, FIRST_SPANS, (f0, f1), (solution, h1, h2), (source, g1, g2), (w0, w1, w2), local_maps, None,
    )
    stencil("difference", n0, solution, source, m0, 32, 160, 128, 1)
    tiles = down_levels((h0, h1, h2), (n0, k1, k2), (w0, w1, w2), local_maps, LATER_DOWN)
    repeat(own_row(jnp.concatenate(tiles, axis=0)), message)


def scale_base(base, maps):
    halves, rows, first = WHOLE[3]

    def body(start, size):
        at = pl.ds(start, size)
        for i in range(halves):
            inverse = maps[INVERSE, first + i, at, :]
            for c in range(CHANNELS):
                base[c, first + i, at, :] = base[c, first + i, at, :] * inverse

    chunks(0, rows, STEP_W, body)


def last_kernel(
    mine, other, m0, m1, m2, source, m3, m4, m5, m6, product, before, n0, f0, k1, f1, k2, f2,
    solution, residual,
    ordered, b3, v3, o3, b4, v4, o4, b5, v5, o5, b6,
    h0, h1, h2, w0, w1, w2, near_maps, near_base, near_a, near_b,
):
    place = whereabouts()
    for ref in (b3, v3):
        rows = ref.shape[2]
        clear(ref, (0, PAD), (rows - PAD, rows))
        for index in range(ref.shape[0]):
            for h in (0, 5):
                ref[index, h] = jnp.zeros((rows, LANES), F32)
    for ref in (b4, v4, o4, b5, v5, o5):
        rows = ref.shape[2]
        clear(ref, (0, PAD), (rows - PAD, rows))

    def put(f, start, group, tile):
        b3[f, 1 + group, pl.ds(start, 8), :] = tile

    unpack(place, mine, other, CHANNELS, CHANNELS, ordered, put)
    maps = {3: m3, 4: m4, 5: m5, 6: m6}
    scale_base(b3, m3)
    whole_cycle(
        3, {3: b3, 4: b4, 5: b5, 6: b6}, {3: v3, 4: v4, 5: v5}, {3: o3, 4: o4, 5: o5}, maps,
        product,
    )
    correct_level_two(
        place, {3: b3}, {3: v3}, maps, f2, h2, near_maps, near_base, near_a, near_b
    )
    local_maps = (m0, m1, m2)
    up_levels(
        LATER_UP, LATER_SPANS, (f0, f1), (h0, h1, h2), (n0, k1, k2), (w0, w1, w2), local_maps, before,
    )
    stencil("final", w0, h0, source, m0, 64, 128, 64, 1)
    for c in range(CHANNELS):
        solution[c] = h0[c, 0, PAD + 64 : PAD + 128, :]
        residual[c] = w0[c, 0, PAD + 64 : PAD + 128, :]


def shape(*dims):
    return jax.ShapeDtypeStruct(dims, F32)


def field_shape(level, count):
    return (count, 2, LOCAL_ROWS[level] + 2 * PAD, LANES)


def whole_shape(level, count):
    halves, rows, first = WHOLE[level]
    return (count, halves + 2 * first, rows + 2 * PAD, LANES)


def call(kernel, outs, scratch, *args):
    in_specs = [pl.BlockSpec(memory_space=pltpu.VMEM) for _ in args]
    return pl.pallas_call(
        kernel,
        out_shape=[shape(*o) for o in outs],
        in_specs=in_specs,
        out_specs=[pl.BlockSpec(memory_space=pltpu.VMEM) for _ in outs],
        scratch_shapes=[pltpu.VMEM(s, F32) for s in scratch],
        compiler_params=pltpu.CompilerParams(vmem_limit_bytes=14 * 1024 * 1024),
        cost_estimate=pl.CostEstimate(flops=0, bytes_accessed=8_000_000, transcendentals=0),
    )(*args)


def ring(count, step):
    return [(i, (i + step) % count) for i in range(count)]


def gathered(message):
    mine = lax.all_to_all(message.reshape(128, 1, -1), CHIPS, 0, 0, tiled=True)
    mine = mine.reshape(message.shape)
    return mine, lax.ppermute(mine, "core", ring(2, 1))


def local(guidance, seam_weight, source_label):
    down, up = pl.pallas_call(
        stack_kernel,
        out_shape=[pltpu.VMEM((UPDOWN_ROWS, LANES), F32)] * 2,
        in_specs=[pl.BlockSpec(memory_space=pltpu.HBM)] * 3,
        out_specs=[pl.BlockSpec(memory_space=pltpu.VMEM)] * 2,
        scratch_shapes=[
            pltpu.VMEM((2, CHANNELS, 64, LANES), F32),
            pltpu.VMEM((64, LANES), jnp.int32),
            pltpu.VMEM((64, LANES), jnp.int32),
            pltpu.SemaphoreType.DMA((3,)),
        ],
        compiler_params=pltpu.CompilerParams(vmem_limit_bytes=58 * 1024 * 1024),
    )(guidance, seam_weight, source_label)
    above = lax.ppermute(down, "z", ring(8, 1))
    below = lax.ppermute(up, "z", ring(8, -1))
    own, ends = call(own_kernel, [(FIELDS, 64, LANES), (8, LANES)], [], down, up)
    swap, side, border = call(
        pack_kernel,
        [(SIDE_ROWS, LANES)] * 2 + [(CHANNELS, 176, LANES)],
        [],
        own, ends, above, below,
    )
    swapped = lax.ppermute(swap, "core", ring(2, 1))
    pairs = [(i, min(max(i + 2 * (i % 2) - 1, 0), 31)) for i in range(32)]
    sided = lax.ppermute(side, SIDES, pairs)
    fields = [field_shape(level, CHANNELS) for level in range(3)]
    maps = [field_shape(0, 5), field_shape(1, 6), field_shape(2, 6)]
    raws = [field_shape(level, 4) for level in range(3)]
    m0, m1, m2, source, f0, g1, f1, g2, f2, message = call(
        setup_kernel,
        maps + [fields[0], fields[0], fields[1], fields[1], fields[2], fields[2], (6 * 128, LANES)],
        [field_shape(0, FIELDS)] + raws + fields,
        own, ends, above, below, swapped, sided, border,
    )
    mine, other = gathered(message)
    wholes = [whole_shape(level, CHANNELS) for level in (3, 4, 5) for _ in range(3)]
    wholes = wholes + [whole_shape(6, CHANNELS)]
    near = [(4, 1, 40, LANES)] + [(CHANNELS, 1, 40, LANES)] * 3
    m3, m4, m5, m6, product, solution, n0, h0, k1, h1, k2, h2, message = call(
        middle_kernel,
        [whole_shape(level, 6) for level in (3, 4, 5, 6)]
        + [(len(DIAMOND), 8, LANES)] + [fields[0]] * 3 + [fields[1]] * 2 + [fields[2]] * 2 + [(CHANNELS * 128, LANES)],
        [(6, 256, LANES)] + [whole_shape(level, 4) for level in (3, 4, 5, 6)]
        + wholes + fields + near,
        mine, other, m0, m1, m2, source, f0, g1, f1, g2, f2,
    )
    mine, other = gathered(message)
    outs = call(
        last_kernel,
        [(CHANNELS, 64, LANES)] * 2,
        [(CHANNELS, 256, LANES)] + wholes + fields + fields + near,
        mine, other, m0, m1, m2, source, m3, m4, m5, m6, product,
        solution, n0, h0, k1, h1, k2, h2,
    )
    return tuple(outs)


def solution(mesh):
    fine = Mesh(mesh.devices.reshape(8, 4, 4, 2), ("z", "y", "x", "core"))
    return jax.shard_map(
        local,
        mesh=fine,
        in_specs=(P(None, None, "z", SIDES), P("z", SIDES), P("z", SIDES)),
        out_specs=(P(None, "z", SIDES), P(None, "z", SIDES)),
        check_vma=False,
    )
```

```python
import jax
import jax.numpy as jnp
from jax import lax
from jax.experimental import pallas as pl
from jax.experimental.pallas import tpu as pltpu
from jax.sharding import Mesh, PartitionSpec as P

F32 = jnp.float32
CHANNELS = 3
COARSE_SWEEPS = 48
RELAX_WEIGHT = 0.8
SEAM_FACTOR = 0.25
PAD = 8
LANES = 128
REACH = 56
SIDES = ("y", "x", "core")
CHIPS = ("y", "x", "z")
LOCAL_ROWS = (192, 96, 48)
STEP, STEP_R, STEP_F, STEP_C, STEP_A, STEP_W = 8, 16, 16, 16, 8, 16
UP, DOWN, LEFT, RIGHT, SCALE, INVERSE = range(6)


def lane_ids(rows):
    return lax.broadcasted_iota(jnp.int32, (rows, LANES), 1)


def beside(halves, width):
    count = len(halves)
    lane = lane_ids(halves[0].shape[0])
    ahead = [pltpu.roll(x, width, 1) for x in halves]
    behind = [pltpu.roll(x, LANES - width, 1) for x in halves]
    if count == 1:
        return ahead, behind
    left = [jnp.where(lane < width, ahead[h - 1], ahead[h]) for h in range(count)]
    right = [
        jnp.where(lane >= LANES - width, behind[(h + 1) % count], behind[h]) for h in range(count)
    ]
    return left, right


def pair_sum(x, width):
    low = (lane_ids(x.shape[0]) & width) == 0
    return x + jnp.where(low, pltpu.roll(x, LANES - width, 1), pltpu.roll(x, width, 1))


def low_of_pair(x, width):
    low = (lane_ids(x.shape[0]) & width) == 0
    return jnp.where(low, x, pltpu.roll(x, width, 1))


def high_of_pair(x, width):
    low = (lane_ids(x.shape[0]) & width) == 0
    return jnp.where(low, pltpu.roll(x, LANES - width, 1), x)


def picked(x, lanes):
    return jnp.take_along_axis(x, lanes, axis=1, mode="promise_in_bounds")


def chunks(low, high, step, body):
    for start in range(low, high, step):
        body(PAD + start, min(step, high - start))


def stencil(mode, target, field, base, maps, low, high, size, width=1, halves=2, first=0, extra=None):
    def body(start, size):
        at = pl.ds(start, size)
        span = range(first, first + halves)
        coef = [[maps[m, h, at, :] for h in span] for m in range(4)]
        for c in range(CHANNELS):
            here = [field[c, h, at, :] for h in span]
            above = [field[c, h, pl.ds(start - 1, size), :] for h in span]
            below = [field[c, h, pl.ds(start + 1, size), :] for h in span]
            left, right = beside(here, width)
            for i, h in enumerate(span):
                near = (above[i], below[i], left[i], right[i])
                if mode in ("difference", "scaled_difference", "final"):
                    near = [n - here[i] for n in near]
                total = coef[0][i] * near[0] + coef[1][i] * near[1]
                total = total + (coef[2][i] * near[2] + coef[3][i] * near[3])
                if mode == "first":
                    result = (2.0 - RELAX_WEIGHT) * here[i] + total
                elif mode == "relax":
                    result = (1.0 - RELAX_WEIGHT) * here[i] + base[c, h, at, :] + total
                elif mode == "relax_add":
                    result = (1.0 - RELAX_WEIGHT) * here[i] + base[c, h, at, :] + total
                    result = extra[c, h, at, :] + result
                elif mode == "residual":
                    result = base[c, h, at, :] - RELAX_WEIGHT * here[i] + total
                    result = maps[SCALE, h, at, :] * result
                elif mode == "difference":
                    result = base[c, h, at, :] + total
                else:
                    result = maps[SCALE, h, at, :] * (base[c, h, at, :] + total)
                target[c, h, at, :] = result

    chunks(low, high, STEP, body)


def scaled_maps(raw, factor):
    whole = raw[0] + raw[1] + raw[2] + raw[3]
    inside = whole > 0.0
    share = jnp.where(inside, RELAX_WEIGHT / jnp.where(inside, whole, 1.0), 0.0)
    return [r * share for r in raw], whole * (factor / RELAX_WEIGHT), share * (1.0 / factor)


def even_odd(ref, lead, start, count):
    return (
        ref[lead + (pl.ds(start, count, stride=2), slice(None))],
        ref[lead + (pl.ds(start + 1, count, stride=2), slice(None))],
    )


FIELDS = 5
WEIGHT, LABEL = 3, 4
UPDOWN_ROWS = FIELDS * REACH + 8
SIDE_ROWS = FIELDS * 88 + 16


def stack_kernel(guidance_in, weight_in, label_in, down, up, guidance, weight_at, label_at, arrived):
    copies = [
        pltpu.make_async_copy(source, target, arrived.at[i])
        for i, (source, target) in enumerate(
            ((guidance_in, guidance), (weight_in, weight_at), (label_in, label_at))
        )
    ]
    for copy in copies:
        copy.start()
    for copy in copies:
        copy.wait()
    weight, label = weight_at[...].astype(F32), label_at[...].astype(F32)
    row = lax.broadcasted_iota(jnp.int32, (64, LANES), 0)
    lane = lane_ids(64)

    def edge(turn, axis, inside):
        matching = jnp.where(pltpu.roll(label, turn, axis) == label, 1.0 / 64.0, SEAM_FACTOR / 64.0)
        return jnp.where(inside, (weight + pltpu.roll(weight, turn, axis)) * matching, 0.0)

    below, right = edge(63, 0, row < 63), edge(LANES - 1, 1, lane < LANES - 1)

    def put(a, x):
        down[REACH * a : REACH * (a + 1), :] = x[64 - REACH :]
        up[REACH * a : REACH * (a + 1), :] = x[:REACH]

    ends = [guidance[0, c, 63:64, :] for c in range(CHANNELS)]
    for c in range(CHANNELS):
        first, second = below * guidance[0, c], right * guidance[1, c]
        put(c, (pltpu.roll(first, 1, 0) - first) + (pltpu.roll(second, 1, 1) - second))
        last = jnp.broadcast_to(guidance[1, c, :, LANES - 1 :], (64, LANES))
        ends.append(jnp.sum(jnp.where(row == lane, last, 0.0), axis=0, keepdims=True))
    put(WEIGHT, weight)
    put(LABEL, label)
    ends = jnp.concatenate(ends + [jnp.zeros((2, LANES), F32)], axis=0)
    down[FIELDS * REACH :, :] = ends
    up[FIELDS * REACH :, :] = ends


def own_kernel(down, up, own, ends):
    for a in range(FIELDS):
        own[a, :REACH, :] = up[REACH * a : REACH * (a + 1), :]
        own[a, REACH:, :] = down[REACH * (a + 1) - (64 - REACH) : REACH * (a + 1), :]
    ends[...] = up[FIELDS * REACH :, :]


def upright(row, first, count):
    place = first + lax.broadcasted_iota(jnp.int32, (count, LANES), 0)
    return picked(jnp.broadcast_to(row, (count, LANES)), place)


def whereabouts():
    core = lax.axis_index("core")
    chip = lax.axis_index("y") * 4 + lax.axis_index("x")
    return lax.axis_index("z"), 2 * chip + core, core


def pack_kernel(own, ends, above, below, swap, side, edge):
    first_core = whereabouts()[2] == 0
    low = lane_ids(88) < 64
    base = FIELDS * REACH

    def halves(x):
        return x[:88], pltpu.roll(x[88:], 64, 1)

    for a in range(FIELDS):
        at = slice(REACH * a, REACH * (a + 1))
        whole = jnp.concatenate([above[at, :], own[a], below[at, :]], axis=0)
        top, bottom = halves(whole)
        to_left = jnp.where(low, top, bottom)
        if a < CHANNELS:
            column = jnp.concatenate(
                [
                    upright(above[base + 3 + a : base + 4 + a, :], 64 - REACH, REACH),
                    upright(ends[3 + a : 4 + a, :], 0, 64),
                    upright(below[base + 3 + a : base + 4 + a, :], 0, REACH),
                ],
                axis=0,
            )
            edge[a] = column
            top, bottom = halves(jnp.where(lane_ids(176) == 64, column, whole))
        to_right = jnp.where(low, bottom, top)
        at = slice(88 * a, 88 * (a + 1))
        swap[at, :] = jnp.where(first_core, to_right, to_left)
        side[at, :] = jnp.where(first_core, to_left, to_right)
    for ref in (swap, side):
        ref[88 * FIELDS : 88 * FIELDS + 8, :] = above[base:, :]
        ref[88 * FIELDS + 8 :, :] = ends[...]


def local_down(level, field, base, work, maps, next_base, next_maps, first_rows, rest_rows, next_rows):
    width = 2**level
    low, high, size = first_rows
    stencil("first", field, base, base, maps, low, high, size, width)
    low, high, size = rest_rows
    stencil("scaled_difference", work, field, base, maps, low, high, size, width)
    if next_base is None:
        return

    low, high, size = next_rows

    def body(start, size):
        at = pl.ds(start, size)
        for h in range(2):
            inverse = 0.25 * next_maps[INVERSE, h, at, :]
            for c in range(CHANNELS):
                even, odd = even_odd(work, (c, h), 2 * start - PAD, size)
                next_base[c, h, at, :] = pair_sum(even + odd, width) * inverse

    chunks(low, high, STEP_R, body)


def own_row(x):
    count = x.shape[0] // 8
    spread = picked(x, 8 * (lane_ids(x.shape[0]) & 15))
    rows = []
    keep = (lane_ids(8) >> 4) == lax.broadcasted_iota(jnp.int32, (8, LANES), 0)
    for i in range(count):
        part = jnp.where(keep, spread[8 * i : 8 * i + 8], 0.0)
        rows.append(jnp.sum(part, axis=0, keepdims=True))
    return rows


def repeat(rows, message):
    block = jnp.concatenate(rows * (24 // len(rows)), axis=0)
    for i in range(message.shape[0] // 24):
        message[24 * i : 24 * i + 24, :] = block


def down_levels(fields, bases, work, maps, ranges):
    for level in range(3):
        local_down(
            level,
            fields[level],
            bases[level],
            work[level],
            maps[level],
            bases[level + 1] if level < 2 else None,
            maps[level + 1] if level < 2 else None,
            *ranges[level],
        )
    tiles = []
    for c in range(CHANNELS):
        even, odd = even_odd(work[2], (c, 0), PAD + 16, 8)
        tiles.append(0.25 * pair_sum(even + odd, 4))
    return tiles


FIRST_DOWN = (
    ((8, 184, 176), (8, 184, 176), (0, 96, 96)),
    ((0, 96, 96), (0, 96, 96), (0, 48, 48)),
    ((0, 48, 48), (0, 48, 48), None),
)
LATER_DOWN = (
    ((32, 160, 128), (32, 160, 128), (16, 80, 64)),
    ((16, 80, 64), (16, 80, 64), (8, 40, 32)),
    ((8, 40, 32), (8, 40, 32), None),
)
FIRST_UP = ((32, 160, 128), (8, 88, 80), (0, 48, 48))
LATER_UP = ((56, 136, 80), (24, 72, 48), (8, 40, 32))
FIRST_SPANS = ((8, 88, 80), (0, 48, 48))
LATER_SPANS = ((24, 72, 48), (8, 40, 32))


def clear(ref, *bounds):
    for index in range(ref.shape[0]):
        for h in range(ref.shape[1]):
            for low, high in bounds:
                ref[index, h, low:high, :] = jnp.zeros((high - low, LANES), F32)


def setup_kernel(
    own, ends, above, below, swapped, sided, border,
    m0, m1, m2, source, f0, g1, f1, g2, f2, message,
    cells, raw0, raw1, raw2, w0, w1, w2,
):
    row_at, col_at, core = whereabouts()
    first_core = core == 0
    rows_of = lambda n, low: low + lax.broadcasted_iota(jnp.int32, (n, LANES), 0)
    edge = jnp.zeros((16, LANES), F32)
    not_top, not_bottom = row_at > 0, row_at < 7
    low = lane_ids(88) < 64
    inside = (low & (col_at < 31)) | (~low & (col_at > 0))

    def sides(start, size):
        one, two = swapped[start : start + size, :], sided[start : start + size, :]
        return jnp.where(first_core, one, two), jnp.where(first_core, two, one)

    for a in range(FIELDS):
        at = slice(REACH * a, REACH * (a + 1))
        for h in range(2):
            cells[a, h, 0:16, :] = edge
            cells[a, h, 192:208, :] = edge
        cells[a, 0, 16:72, :] = jnp.where(not_top, above[at, :], 0.0)
        cells[a, 0, 72:136, :] = own[a]
        cells[a, 0, 136:192, :] = jnp.where(not_bottom, below[at, :], 0.0)
        from_right, from_left = sides(88 * a, 88)
        top = jnp.where(low, from_right, from_left)
        bottom = pltpu.roll(jnp.where(low, from_left, from_right), 64, 1)
        cells[a, 1, 16:104, :] = jnp.where(inside & (not_top | (rows_of(88, 8) >= 64)), top, 0.0)
        cells[a, 1, 104:192, :] = jnp.where(
            inside & (not_bottom | (rows_of(88, 96) < 128)), bottom, 0.0
        )
    def fine(start, size):
        at = pl.ds(start, size)
        up_at, down_at = pl.ds(start - 1, size), pl.ds(start + 1, size)
        weights = [cells[WEIGHT, h, at, :] for h in range(2)]
        labels = [cells[LABEL, h, at, :] for h in range(2)]
        weight_sides = beside(weights, 1)
        label_sides = beside(labels, 1)
        coef, shares = [], []
        for h in range(2):
            near_weights = (
                cells[WEIGHT, h, up_at, :], cells[WEIGHT, h, down_at, :], weight_sides[0][h], weight_sides[1][h],
            )
            near_labels = (
                cells[LABEL, h, up_at, :], cells[LABEL, h, down_at, :], label_sides[0][h], label_sides[1][h],
            )
            raw = []
            for m in range(4):
                matching = jnp.where(near_labels[m] == labels[h], 1.0 / 64.0, SEAM_FACTOR / 64.0)
                value = (weights[h] + near_weights[m]) * matching
                value = jnp.where(weights[h] > 0.0, value, 0.0)
                raw.append(value)
                raw0[m, h, at, :] = value
            scaled, scale, share = scaled_maps(raw, 1.0)
            shares.append(share)
            for m in range(4):
                m0[m, h, at, :] = scaled[m]
            m0[SCALE, h, at, :] = scale
            coef.append(scaled)
        for c in range(CHANNELS):
            part = [cells[c, h, at, :] for h in range(2)]
            own_end = border[c, start - PAD - 8 : start - PAD - 8 + size, :]
            left_end = pltpu.roll(part[1], 64, 1), pltpu.roll(part[1], 63, 1)
            first, last = lane_ids(size) == 0, lane_ids(size) == LANES - 1
            flux = jnp.where(first, coef[0][LEFT] * left_end[0], 0.0)
            flux = flux - jnp.where(last, coef[0][RIGHT] * own_end, 0.0)
            source[c, 0, at, :] = shares[0] * part[0] + flux
            flux = jnp.where(first, coef[1][LEFT] * own_end, 0.0)
            flux = flux - jnp.where(last, coef[1][RIGHT] * left_end[1], 0.0)
            source[c, 1, at, :] = shares[1] * part[1] + flux

    chunks(8, 184, STEP_F, fine)
    from_right, from_left = sides(88 * FIELDS, 16)
    beside_own = jnp.where(lane_ids(16) < 64, from_right, from_left)
    for first, upper in ((0, 71), (8, 135)):
        for c in range(CHANNELS):
            if first == 0:
                straight = above[FIELDS * REACH + c : FIELDS * REACH + c + 1, :]
            else:
                straight = ends[c : c + 1, :]
            for h, flow in ((0, straight), (1, beside_own[first + c : first + c + 1])):
                if first == 0:
                    flow = jnp.where(not_top, flow, 0.0)
                one, two = pl.ds(upper, 1), pl.ds(upper + 1, 1)
                source[c, h, one, :] = source[c, h, one, :] - m0[DOWN, h, one, :] * flow
                source[c, h, two, :] = source[c, h, two, :] + m0[UP, h, two, :] * flow

    def coarser(raw, width, start, size, h):
        parts = []
        for m in range(4):
            even, odd = even_odd(raw, (m, h), start, size)
            if m == UP:
                parts.append(0.5 * pair_sum(even, width))
            elif m == DOWN:
                parts.append(0.5 * pair_sum(odd, width))
            elif m == LEFT:
                parts.append(0.5 * low_of_pair(even + odd, width))
            else:
                parts.append(0.5 * high_of_pair(even + odd, width))
        return parts

    for level, fine_raw, raw, maps, rows in ((1, raw0, raw1, m1, 96), (2, raw1, raw2, m2, 48)):

        def coarse(start, size, level=level, fine_raw=fine_raw, raw=raw, maps=maps):
            at = pl.ds(start, size)
            for h in range(2):
                parts = coarser(fine_raw, 2 ** (level - 1), 2 * start - PAD, size, h)
                scaled, scale, inverse = scaled_maps(parts, 0.5**level)
                for m in range(4):
                    raw[m, h, at, :] = parts[m]
                    maps[m, h, at, :] = scaled[m]
                maps[SCALE, h, at, :] = scale
                maps[INVERSE, h, at, :] = inverse

        chunks(0, rows, STEP_C, coarse)
    tiles = down_levels((f0, f1, f2), (source, g1, g2), (w0, w1, w2), (m0, m1, m2), FIRST_DOWN)
    upward, downward, leftward, rightward = coarser(raw2, 4, PAD + 16, 8, 0)
    row = lax.broadcasted_iota(jnp.int32, (8, LANES), 0)
    cell = lane_ids(8) >> 3
    turned = pltpu.roll(pltpu.roll(rightward, LANES - 8, 1), 7, 0)
    ends = jnp.where(row == 7, downward, jnp.where(cell == 15, rightward, turned))
    repeat(own_row(jnp.concatenate(tiles + [upward, leftward, ends], axis=0)), message)


def unpack(place, mine, other, count, stride, ordered, put):
    core = place[2]
    for f in range(count):
        for z in range(8):
            at = pl.ds(f + stride * z, 16, stride=8 * stride)
            own, theirs = mine[at, :], other[at, :]
            ordered[f, pl.ds(32 * z, 16, stride=2), :] = jnp.where(core == 0, own, theirs)
            ordered[f, pl.ds(32 * z + 1, 16, stride=2), :] = jnp.where(core == 0, theirs, own)
    sub = lax.broadcasted_iota(jnp.int32, (8, LANES), 0)
    part, cell = lane_ids(8) >> 4, lane_ids(8) & 15
    first = (((sub - part) & 7) << 4) + cell
    last = (((part - sub) & 7) << 4) + cell
    for z in range(8):
        for f in range(count):
            for group in range(4):
                x = picked(ordered[f, pl.ds(z * 32 + 8 * group, 8), :], first)
                for k in (1, 2, 4):
                    x = jnp.where((part & k) != 0, pltpu.roll(x, 8 - k, 0), x)
                put(f, PAD + 8 * z, group, picked(x, last))


def folded(halves, kind):
    lane = lane_ids(halves[0].shape[0])
    even = (2 * lane) & (LANES - 1)

    def one(x):
        if kind == "low":
            return picked(x, even)
        if kind == "high":
            return picked(x, even + 1)
        return picked(x, even) + picked(x, even + 1)

    parts = [one(x) for x in halves]
    if len(parts) == 1:
        parts.append(jnp.zeros_like(parts[0]))
    return [jnp.where(lane < 64, parts[i], parts[i + 1]) for i in range(0, len(parts), 2)]


def doubled(x):
    lane = lane_ids(x.shape[0])
    return [picked(x, lane >> 1), picked(x, 64 + (lane >> 1))]


WHOLE = {3: (4, 64, 1), 4: (2, 32, 0), 5: (1, 16, 0), 6: (1, 8, 0)}


def whole_maps(level, raw, maps):
    halves, rows, first = WHOLE[level]

    def body(start, size):
        at = pl.ds(start, size)
        lane = lane_ids(size)
        for i in range(halves):
            scaled, scale, inverse = scaled_maps(
                [raw[m, first + i, at, :] for m in range(4)], 0.5**level
            )
            breadth = 64 if level == 6 else LANES
            if i == 0:
                scaled[LEFT] = jnp.where((lane & (breadth - 1)) == 0, 0.0, scaled[LEFT])
            if i == halves - 1:
                at_last = (lane & (breadth - 1)) == breadth - 1
                scaled[RIGHT] = jnp.where(at_last, 0.0, scaled[RIGHT])
            for m in range(4):
                maps[m, first + i, at, :] = scaled[m]
            maps[SCALE, first + i, at, :] = scale
            maps[INVERSE, first + i, at, :] = inverse

    chunks(0, rows, STEP_W, body)


def coarsen_whole(level, raw, next_raw):
    halves, rows, first = WHOLE[level]
    next_halves, next_rows, next_first = WHOLE[level + 1]
    for m in range(4):
        parts = []
        for h in range(halves):
            even, odd = even_odd(raw, (m, first + h), PAD, next_rows)
            parts.append(even if m == UP else odd if m == DOWN else even + odd)
        kind = "sum" if m in (UP, DOWN) else "low" if m == LEFT else "high"
        if level == 5:
            parts = parts * 2
        for h, x in enumerate(folded(parts, kind)):
            next_raw[m, next_first + h, PAD : PAD + next_rows, :] = 0.5 * x


def one_sweep(maps):
    coef = [maps[m, 0, PAD : PAD + 8, :] for m in range(4)]
    row = lax.broadcasted_iota(jnp.int32, (8, LANES), 0)
    coef[UP] = jnp.where(row == 0, 0.0, coef[UP])
    coef[DOWN] = jnp.where(row == 7, 0.0, coef[DOWN])
    steps = ((-1, 0), (1, 0), (0, -1), (0, 1))
    return dict(zip(steps, coef))


def moved(x, rows, columns):
    if rows:
        x = pltpu.roll(x, (-rows) % 8, 0)
    if columns:
        x = pltpu.roll(x, (-columns) % LANES, 1)
    return x


DIAMOND = [(a, b) for a in range(-4, 5) for b in range(-4, 5) if abs(a) + abs(b) <= 4]


def four_sweeps(maps, product):
    sweep = one_sweep(maps)
    whole = dict(sweep)
    whole[0, 0] = jnp.full((8, LANES), 1.0 - RELAX_WEIGHT, F32)
    for _ in range(3):
        grown = {at: (1.0 - RELAX_WEIGHT) * x for at, x in whole.items()}
        for step, coef in sweep.items():
            for at, x in whole.items():
                place = (at[0] + step[0], at[1] + step[1])
                term = coef * moved(x, *step)
                grown[place] = grown[place] + term if place in grown else term
        whole = grown
    for i, at in enumerate(DIAMOND):
        product[i] = moved(whole[at], -at[0], 0)


def coarse_solve(base, maps, product):
    sweep = one_sweep(maps)
    right_side = [base[i, 0, PAD : PAD + 8, :] for i in range(2)]
    first = right_side
    for _ in range(3):
        first = [
            (1.0 - RELAX_WEIGHT) * v + g + sum(coef * moved(v, *at) for at, coef in sweep.items())
            for v, g in zip(first, right_side)
        ]
    values = first
    for _ in range(COARSE_SWEEPS // 4 - 1):
        lanes = [[moved(v, 0, b) for b in range(-4, 5)] for v in values]
        totals = [list() for _ in values]
        for a in range(-4, 5):
            sums = [None] * len(values)
            for i, at in enumerate(DIAMOND):
                if at[0] == a:
                    coef = product[i]
                    for c in range(len(values)):
                        term = coef * lanes[c][at[1] + 4]
                        sums[c] = term if sums[c] is None else sums[c] + term
            for c in range(len(values)):
                totals[c].append(moved(sums[c], a, 0))
        values = []
        for c in range(len(first)):
            t = totals[c]
            even = (t[0] + t[1]) + (t[2] + t[3])
            odd = (t[5] + t[6]) + (t[7] + t[8])
            values.append((first[c] + t[4]) + (even + odd))
    return values


def whole_cycle(level, bases, fields, others, maps, product):
    halves, rows, first = WHOLE[level]
    base, field, other, level_maps = bases[level], fields[level], others[level], maps[level]
    size = rows
    stencil("first", field, base, base, level_maps, 0, rows, size, 1, halves, first)
    stencil("residual", other, field, base, level_maps, 0, rows, size, 1, halves, first)
    next_halves, next_rows, next_first = WHOLE[level + 1]
    summed = []
    for h in range(halves):
        parts = []
        for c in range(CHANNELS):
            even, odd = even_odd(other, (c, first + h), PAD, next_rows)
            parts.append(even + odd)
        summed.append(jnp.concatenate(parts, axis=0))
    if level == 5:
        parts = [summed[0][c * next_rows : (c + 1) * next_rows] for c in range(CHANNELS)]
        inverse = 0.25 * maps[6][INVERSE, 0, PAD : PAD + next_rows, :]
        for i, group in enumerate((parts[:2], parts[2:])):
            bases[6][i, 0, PAD : PAD + next_rows, :] = folded(group, "sum")[0] * inverse
        summed = []
    for h, x in enumerate(folded(summed, "sum") if summed else []):
        inverse = 0.25 * maps[level + 1][INVERSE, next_first + h, PAD : PAD + next_rows, :]
        for c in range(CHANNELS):
            part = x[c * next_rows : (c + 1) * next_rows]
            bases[level + 1][c, next_first + h, PAD : PAD + next_rows, :] = part * inverse
    if level == 5:
        both, third = coarse_solve(bases[6], maps[6], product)
        coarse = [None]
    else:
        whole_cycle(level + 1, bases, fields, others, maps, product)
        coarse = [
            jnp.concatenate(
                [
                    fields[level + 1][c, next_first + h, PAD : PAD + next_rows, :]
                    for c in range(CHANNELS)
                ],
                axis=0,
            )
            for h in range(next_halves)
        ]
    for m, x in enumerate(coarse):
        if x is None:
            wide = [jnp.concatenate(doubled(both) + doubled(third)[:1], axis=0)]
        else:
            wide = doubled(x)
        for i in range(min(halves, 2)):
            h = first + 2 * m + i
            for c in range(CHANNELS):
                part = wide[i][c * next_rows : (c + 1) * next_rows]
                for offset in range(2):
                    at = pl.ds(PAD + offset, next_rows, stride=2)
                    field[c, h, at, :] = field[c, h, at, :] + part
    if level > 3:
        stencil("relax", other, field, base, level_maps, 0, rows, size, 1, halves, first)
        stencil("relax", field, other, base, level_maps, 0, rows, size, 1, halves, first)


def window(ref, index, place):
    group = lax.shift_right_logical(place[1], 3)
    offset = 16 * (place[1] & 7)
    at = pl.ds(pl.multiple_of(8 * place[0], 8), 24)
    lane = lane_ids(24)
    turn = lax.rem(LANES - offset, LANES)
    before, here, after = [pltpu.roll(ref[index, group + i, at, :], turn, 1) for i in range(3)]
    low = lane < 64
    fits = lane + offset < LANES
    return jnp.where(low, jnp.where(fits, here, after), jnp.where(fits, before, here))


def correct_level_two(
    place, bases, fields, maps, f2, target, near_maps, near_base, near_a, near_b
):
    if maps is not None:
        for m in range(4):
            near_maps[m, 0, PAD : PAD + 24, :] = window(maps[3], m, place)
    edge = jnp.zeros((PAD, LANES), F32)
    for c in range(CHANNELS):
        near_base[c, 0, PAD : PAD + 24, :] = window(bases[3], c, place)
        near_a[c, 0, PAD : PAD + 24, :] = window(fields[3], c, place)
        for ref in (near_a, near_b):
            ref[c, 0, 0:PAD, :] = edge
            ref[c, 0, PAD + 24 : PAD + 32, :] = edge
    stencil("relax", near_b, near_a, near_base, near_maps, 0, 24, 24, 1, 1)
    stencil("relax", near_a, near_b, near_base, near_maps, 0, 24, 24, 1, 1)
    flat = jnp.concatenate([near_a[c, 0, PAD : PAD + 24, :] for c in range(CHANNELS)], axis=0)
    lane = lane_ids(flat.shape[0])
    wide = [picked(flat, lane >> 3), picked(flat, jnp.where(lane < 64, 16, 112) + (lane >> 3))]
    for c in range(CHANNELS):
        for h in range(2):
            part = wide[h][24 * c : 24 * c + 24]
            for offset in range(2):
                at = pl.ds(PAD + offset, 24, stride=2)
                target[c, h, at, :] = f2[c, h, at, :] + part


def add_rows(target, field, coarse, low, high, size):
    def body(start, size):
        for c in range(CHANNELS):
            for h in range(2):
                part = coarse[c, h, pl.ds(start, size), :]
                for offset in range(2):
                    at = pl.ds(2 * start - PAD + offset, size, stride=2)
                    target[c, h, at, :] = field[c, h, at, :] + part

    chunks(low, high, STEP_A, body)


def up_levels(ranges, spans, before, fields, bases, works, maps, extra):
    low, high, size = ranges[2]
    stencil("relax", works[2], fields[2], bases[2], maps[2], low, high, size, 4)
    stencil("relax", fields[2], works[2], bases[2], maps[2], low, high, size, 4)
    add_rows(fields[1], before[1], fields[2], *spans[1])
    low, high, size = ranges[1]
    stencil("relax", works[1], fields[1], bases[1], maps[1], low, high, size, 2)
    stencil("relax", fields[1], works[1], bases[1], maps[1], low, high, size, 2)
    add_rows(fields[0], before[0], fields[1], *spans[0])
    low, high, size = ranges[0]
    stencil("relax", works[0], fields[0], bases[0], maps[0], low, high, size, 1)
    if extra is None:
        stencil("relax", fields[0], works[0], bases[0], maps[0], low, high, size, 1)
    else:
        stencil(
            "relax_add", fields[0], works[0], bases[0], maps[0], low, high, size, 1, extra=extra
        )


def complete_maps(raw):
    size = 64
    at = pl.ds(PAD, size)
    lane = lane_ids(size)
    row = lax.broadcasted_iota(jnp.int32, (size, LANES), 0)
    ends = [raw[RIGHT, h, at, :] for h in range(1, 5)]
    shifted = beside([raw[LEFT, h, at, :] for h in range(1, 5)], 1)[1]
    last = ends[3]
    last = jnp.where((row & 7) == 7, pltpu.roll(pltpu.roll(last, 1, 1), 1, 0), last)
    shifted[3] = jnp.where(lane == LANES - 1, last, shifted[3])
    for i in range(4):
        below = raw[UP, 1 + i, pl.ds(PAD + 1, size), :]
        raw[DOWN, 1 + i, at, :] = jnp.where(row == size - 1, ends[i], below)
        raw[RIGHT, 1 + i, at, :] = shifted[i]


def middle_kernel(
    mine, other, m0, m1, m2, source, f0, g1, f1, g2, f2,
    m3, m4, m5, m6, product, near_maps, solution, n0, h0, k1, h1, k2, h2, message,
    ordered, raw3, raw4, raw5, raw6, b3, v3, o3, b4, v4, o4, b5, v5, o5, b6,
    w0, w1, w2, near_base, near_a, near_b,
):
    place = whereabouts()
    for ref in (m3, b3, v3):
        rows = ref.shape[2]
        clear(ref, (0, PAD), (rows - PAD, rows))
        for index in range(ref.shape[0]):
            for h in (0, 5):
                ref[index, h] = jnp.zeros((rows, LANES), F32)
    for ref in (b4, v4, o4, b5, v5, o5):
        rows = ref.shape[2]
        clear(ref, (0, PAD), (rows - PAD, rows))

    def put(f, start, group, tile):
        if f < CHANNELS:
            b3[f, 1 + group, pl.ds(start, 8), :] = tile
        else:
            slot = (UP, LEFT, RIGHT)[f - CHANNELS]
            raw3[slot, 1 + group, pl.ds(start, 8), :] = tile

    unpack(place, mine, other, 6, 6, ordered, put)
    complete_maps(raw3)
    raws = {3: raw3, 4: raw4, 5: raw5, 6: raw6}
    maps = {3: m3, 4: m4, 5: m5, 6: m6}
    whole_maps(3, raw3, m3)
    for level in (3, 4, 5):
        coarsen_whole(level, raws[level], raws[level + 1])
        whole_maps(level + 1, raws[level + 1], maps[level + 1])
    four_sweeps(m6, product)
    scale_base(b3, m3)
    whole_cycle(
        3, {3: b3, 4: b4, 5: b5, 6: b6}, {3: v3, 4: v4, 5: v5}, {3: o3, 4: o4, 5: o5}, maps,
        product,
    )
    correct_level_two(
        place, {3: b3}, {3: v3}, maps, f2, h2, near_maps, near_base, near_a, near_b
    )
    local_maps = (m0, m1, m2)
    up_levels(
        FIRST_UP, FIRST_SPANS, (f0, f1), (solution, h1, h2), (source, g1, g2), (w0, w1, w2), local_maps, None,
    )
    stencil("difference", n0, solution, source, m0, 32, 160, 128, 1)
    tiles = down_levels((h0, h1, h2), (n0, k1, k2), (w0, w1, w2), local_maps, LATER_DOWN)
    repeat(own_row(jnp.concatenate(tiles, axis=0)), message)


def scale_base(base, maps):
    halves, rows, first = WHOLE[3]

    def body(start, size):
        at = pl.ds(start, size)
        for i in range(halves):
            inverse = maps[INVERSE, first + i, at, :]
            for c in range(CHANNELS):
                base[c, first + i, at, :] = base[c, first + i, at, :] * inverse

    chunks(0, rows, STEP_W, body)


def last_kernel(
    mine, other, m0, m1, m2, source, m3, m4, m5, m6, product, near_maps, before, n0, f0, k1, f1, k2, f2,
    solution, residual,
    ordered, b3, v3, o3, b4, v4, o4, b5, v5, o5, b6,
    h0, h1, h2, w0, w1, w2, near_base, near_a, near_b, left,
):
    place = whereabouts()
    for ref in (b3, v3):
        rows = ref.shape[2]
        clear(ref, (0, PAD), (rows - PAD, rows))
        for index in range(ref.shape[0]):
            for h in (0, 5):
                ref[index, h] = jnp.zeros((rows, LANES), F32)
    for ref in (b4, v4, o4, b5, v5, o5):
        rows = ref.shape[2]
        clear(ref, (0, PAD), (rows - PAD, rows))

    def put(f, start, group, tile):
        b3[f, 1 + group, pl.ds(start, 8), :] = tile

    unpack(place, mine, other, CHANNELS, CHANNELS, ordered, put)
    maps = {3: m3, 4: m4, 5: m5, 6: m6}
    scale_base(b3, m3)
    whole_cycle(
        3, {3: b3, 4: b4, 5: b5, 6: b6}, {3: v3, 4: v4, 5: v5}, {3: o3, 4: o4, 5: o5}, maps,
        product,
    )
    correct_level_two(
        place, {3: b3}, {3: v3}, None, f2, h2, near_maps, near_base, near_a, near_b
    )
    local_maps = (m0, m1, m2)
    up_levels(
        LATER_UP, LATER_SPANS, (f0, f1), (h0, h1, h2), (n0, k1, k2), (w0, w1, w2), local_maps, before,
    )
    own = pl.ds(PAD + 64, 64)
    copies = [
        pltpu.make_async_copy(field.at[:, 0, own, :], target, left.at[i])
        for i, (field, target) in enumerate(((h0, solution), (w0, residual)))
    ]
    copies[0].start()
    stencil("final", w0, h0, source, m0, 64, 128, 64, 1)
    copies[1].start()
    for copy in copies:
        copy.wait()


def shape(*dims):
    return jax.ShapeDtypeStruct(dims, F32)


def field_shape(level, count):
    return (count, 2, LOCAL_ROWS[level] + 2 * PAD, LANES)


def whole_shape(level, count):
    halves, rows, first = WHOLE[level]
    return (count, halves + 2 * first, rows + 2 * PAD, LANES)


def call(kernel, outs, scratch, *args, out_space=pltpu.VMEM, semaphores=()):
    in_specs = [pl.BlockSpec(memory_space=pltpu.VMEM) for _ in args]
    return pl.pallas_call(
        kernel,
        out_shape=[shape(*o) for o in outs],
        in_specs=in_specs,
        out_specs=[pl.BlockSpec(memory_space=out_space) for _ in outs],
        scratch_shapes=[pltpu.VMEM(s, F32) for s in scratch] + list(semaphores),
        compiler_params=pltpu.CompilerParams(vmem_limit_bytes=14 * 1024 * 1024),
        cost_estimate=pl.CostEstimate(flops=0, bytes_accessed=8_000_000, transcendentals=0),
    )(*args)


def ring(count, step):
    return [(i, (i + step) % count) for i in range(count)]


def gathered(message):
    mine = lax.all_to_all(message.reshape(128, 1, -1), CHIPS, 0, 0, tiled=True)
    mine = mine.reshape(message.shape)
    return mine, lax.ppermute(mine, "core", ring(2, 1))


def local(guidance, seam_weight, source_label):
    down, up = pl.pallas_call(
        stack_kernel,
        out_shape=[pltpu.VMEM((UPDOWN_ROWS, LANES), F32)] * 2,
        in_specs=[pl.BlockSpec(memory_space=pltpu.HBM)] * 3,
        out_specs=[pl.BlockSpec(memory_space=pltpu.VMEM)] * 2,
        scratch_shapes=[
            pltpu.VMEM((2, CHANNELS, 64, LANES), F32),
            pltpu.VMEM((64, LANES), jnp.int32),
            pltpu.VMEM((64, LANES), jnp.int32),
            pltpu.SemaphoreType.DMA((3,)),
        ],
        compiler_params=pltpu.CompilerParams(vmem_limit_bytes=58 * 1024 * 1024),
    )(guidance, seam_weight, source_label)
    above = lax.ppermute(down, "z", ring(8, 1))
    below = lax.ppermute(up, "z", ring(8, -1))
    own, ends = call(own_kernel, [(FIELDS, 64, LANES), (8, LANES)], [], down, up)
    swap, side, border = call(
        pack_kernel,
        [(SIDE_ROWS, LANES)] * 2 + [(CHANNELS, 176, LANES)],
        [],
        own, ends, above, below,
    )
    swapped = lax.ppermute(swap, "core", ring(2, 1))
    pairs = [(i, min(max(i + 2 * (i % 2) - 1, 0), 31)) for i in range(32)]
    sided = lax.ppermute(side, SIDES, pairs)
    fields = [field_shape(level, CHANNELS) for level in range(3)]
    maps = [field_shape(0, 5), field_shape(1, 6), field_shape(2, 6)]
    raws = [field_shape(level, 4) for level in range(3)]
    m0, m1, m2, source, f0, g1, f1, g2, f2, message = call(
        setup_kernel,
        maps + [fields[0], fields[0], fields[1], fields[1], fields[2], fields[2], (6 * 128, LANES)],
        [field_shape(0, FIELDS)] + raws + fields,
        own, ends, above, below, swapped, sided, border,
    )
    mine, other = gathered(message)
    wholes = [whole_shape(level, CHANNELS) for level in (3, 4, 5) for _ in range(3)]
    wholes = wholes + [whole_shape(6, CHANNELS)]
    near = [(CHANNELS, 1, 40, LANES)] * 3
    m3, m4, m5, m6, product, near_maps, solution, n0, h0, k1, h1, k2, h2, message = call(
        middle_kernel,
        [whole_shape(level, 6) for level in (3, 4, 5, 6)]
        + [(len(DIAMOND), 8, LANES), (4, 1, 40, LANES)] + [fields[0]] * 3 + [fields[1]] * 2 + [fields[2]] * 2 + [(CHANNELS * 128, LANES)],
        [(6, 256, LANES)] + [whole_shape(level, 4) for level in (3, 4, 5, 6)]
        + wholes + fields + near,
        mine, other, m0, m1, m2, source, f0, g1, f1, g2, f2,
    )
    mine, other = gathered(message)
    outs = call(
        last_kernel,
        [(CHANNELS, 64, LANES)] * 2,
        [(CHANNELS, 256, LANES)] + wholes + fields + fields + near,
        mine, other, m0, m1, m2, source, m3, m4, m5, m6, product, near_maps,
        solution, n0, h0, k1, h1, k2, h2,
        out_space=pltpu.HBM, semaphores=[pltpu.SemaphoreType.DMA((2,))],
    )
    return tuple(outs)


def solution(mesh):
    fine = Mesh(mesh.devices.reshape(8, 4, 4, 2), ("z", "y", "x", "core"))
    return jax.shard_map(
        local,
        mesh=fine,
        in_specs=(P(None, None, "z", SIDES), P("z", SIDES), P("z", SIDES)),
        out_specs=(P(None, "z", SIDES), P(None, "z", SIDES)),
        check_vma=False,
    )
```

```python
import jax
import jax.numpy as jnp
from jax import lax
from jax.experimental import pallas as pl
from jax.experimental.pallas import tpu as pltpu
from jax.sharding import Mesh, PartitionSpec as P

F32 = jnp.float32
CHANNELS = 3
COARSE_SWEEPS = 48
RELAX_WEIGHT = 0.8
SEAM_FACTOR = 0.25
PAD = 8
LANES = 128
REACH = 56
SIDES = ("y", "x", "core")
CHIPS = ("y", "x", "z")
LOCAL_ROWS = (192, 96, 48)
STEP, STEP_R, STEP_F, STEP_C, STEP_A, STEP_W = 8, 16, 16, 16, 8, 16
UP, DOWN, LEFT, RIGHT, SCALE, INVERSE = range(6)


def lane_ids(rows):
    return lax.broadcasted_iota(jnp.int32, (rows, LANES), 1)


def beside(halves, width):
    count = len(halves)
    lane = lane_ids(halves[0].shape[0])
    ahead = [pltpu.roll(x, width, 1) for x in halves]
    behind = [pltpu.roll(x, LANES - width, 1) for x in halves]
    if count == 1:
        return ahead, behind
    left = [jnp.where(lane < width, ahead[h - 1], ahead[h]) for h in range(count)]
    right = [
        jnp.where(lane >= LANES - width, behind[(h + 1) % count], behind[h]) for h in range(count)
    ]
    return left, right


def pair_sum(x, width):
    low = (lane_ids(x.shape[0]) & width) == 0
    return x + jnp.where(low, pltpu.roll(x, LANES - width, 1), pltpu.roll(x, width, 1))


def low_of_pair(x, width):
    low = (lane_ids(x.shape[0]) & width) == 0
    return jnp.where(low, x, pltpu.roll(x, width, 1))


def high_of_pair(x, width):
    low = (lane_ids(x.shape[0]) & width) == 0
    return jnp.where(low, pltpu.roll(x, LANES - width, 1), x)


def picked(x, lanes):
    return jnp.take_along_axis(x, lanes, axis=1, mode="promise_in_bounds")


def chunks(low, high, step, body):
    for start in range(low, high, step):
        body(PAD + start, min(step, high - start))


def stencil(mode, target, field, base, maps, low, high, size, width=1, halves=2, first=0, extra=None):
    def body(start, size):
        at = pl.ds(start, size)
        span = range(first, first + halves)
        coef = [[maps[m, h, at, :] for h in span] for m in range(4)]
        for c in range(CHANNELS):
            here = [field[c, h, at, :] for h in span]
            above = [field[c, h, pl.ds(start - 1, size), :] for h in span]
            below = [field[c, h, pl.ds(start + 1, size), :] for h in span]
            left, right = beside(here, width)
            for i, h in enumerate(span[:1] if mode == "final" else span):
                near = (above[i], below[i], left[i], right[i])
                if mode in ("difference", "scaled_difference", "final"):
                    near = [n - here[i] for n in near]
                total = coef[0][i] * near[0] + coef[1][i] * near[1]
                total = total + (coef[2][i] * near[2] + coef[3][i] * near[3])
                if mode == "first":
                    result = (2.0 - RELAX_WEIGHT) * here[i] + total
                elif mode == "relax":
                    result = (1.0 - RELAX_WEIGHT) * here[i] + base[c, h, at, :] + total
                elif mode == "relax_add":
                    result = (1.0 - RELAX_WEIGHT) * here[i] + base[c, h, at, :] + total
                    result = extra[c, h, at, :] + result
                elif mode == "residual":
                    result = base[c, h, at, :] - RELAX_WEIGHT * here[i] + total
                    result = maps[SCALE, h, at, :] * result
                elif mode == "difference":
                    result = base[c, h, at, :] + total
                else:
                    result = maps[SCALE, h, at, :] * (base[c, h, at, :] + total)
                target[c, h, at, :] = result

    chunks(low, high, STEP, body)


def scaled_maps(raw, factor):
    whole = raw[0] + raw[1] + raw[2] + raw[3]
    inside = whole > 0.0
    share = jnp.where(inside, RELAX_WEIGHT / jnp.where(inside, whole, 1.0), 0.0)
    return [r * share for r in raw], whole * (factor / RELAX_WEIGHT), share * (1.0 / factor)


def even_odd(ref, lead, start, count):
    return (
        ref[lead + (pl.ds(start, count, stride=2), slice(None))],
        ref[lead + (pl.ds(start + 1, count, stride=2), slice(None))],
    )


FIELDS = 5
WEIGHT, LABEL = 3, 4
UPDOWN_ROWS = FIELDS * REACH + 8
SIDE_ROWS = FIELDS * 88 + 16


def stack_kernel(guidance_in, weight_in, label_in, down, up, guidance, weight_at, label_at, arrived):
    copies = [
        pltpu.make_async_copy(source, target, arrived.at[i])
        for i, (source, target) in enumerate(
            ((guidance_in, guidance), (weight_in, weight_at), (label_in, label_at))
        )
    ]
    for copy in copies:
        copy.start()
    for copy in copies:
        copy.wait()
    weight, label = weight_at[...].astype(F32), label_at[...].astype(F32)
    row = lax.broadcasted_iota(jnp.int32, (64, LANES), 0)
    lane = lane_ids(64)

    def edge(turn, axis, inside):
        matching = jnp.where(pltpu.roll(label, turn, axis) == label, 1.0 / 64.0, SEAM_FACTOR / 64.0)
        return jnp.where(inside, (weight + pltpu.roll(weight, turn, axis)) * matching, 0.0)

    below, right = edge(63, 0, row < 63), edge(LANES - 1, 1, lane < LANES - 1)

    def put(a, x):
        down[REACH * a : REACH * (a + 1), :] = x[64 - REACH :]
        up[REACH * a : REACH * (a + 1), :] = x[:REACH]

    ends = [guidance[0, c, 63:64, :] for c in range(CHANNELS)]
    for c in range(CHANNELS):
        first, second = below * guidance[0, c], right * guidance[1, c]
        put(c, (pltpu.roll(first, 1, 0) - first) + (pltpu.roll(second, 1, 1) - second))
        last = jnp.broadcast_to(guidance[1, c, :, LANES - 1 :], (64, LANES))
        ends.append(jnp.sum(jnp.where(row == lane, last, 0.0), axis=0, keepdims=True))
    put(WEIGHT, weight)
    put(LABEL, label)
    ends = jnp.concatenate(ends + [jnp.zeros((2, LANES), F32)], axis=0)
    down[FIELDS * REACH :, :] = ends
    up[FIELDS * REACH :, :] = ends


def own_kernel(down, up, own, ends):
    for a in range(FIELDS):
        own[a, :REACH, :] = up[REACH * a : REACH * (a + 1), :]
        own[a, REACH:, :] = down[REACH * (a + 1) - (64 - REACH) : REACH * (a + 1), :]
    ends[...] = up[FIELDS * REACH :, :]


def upright(row, first, count):
    place = first + lax.broadcasted_iota(jnp.int32, (count, LANES), 0)
    return picked(jnp.broadcast_to(row, (count, LANES)), place)


def whereabouts():
    core = lax.axis_index("core")
    chip = lax.axis_index("y") * 4 + lax.axis_index("x")
    return lax.axis_index("z"), 2 * chip + core, core


def pack_kernel(own, ends, above, below, swap, side, edge):
    first_core = whereabouts()[2] == 0
    low = lane_ids(88) < 64
    base = FIELDS * REACH

    def halves(x):
        return x[:88], pltpu.roll(x[88:], 64, 1)

    for a in range(FIELDS):
        at = slice(REACH * a, REACH * (a + 1))
        whole = jnp.concatenate([above[at, :], own[a], below[at, :]], axis=0)
        top, bottom = halves(whole)
        to_left = jnp.where(low, top, bottom)
        if a < CHANNELS:
            column = jnp.concatenate(
                [
                    upright(above[base + 3 + a : base + 4 + a, :], 64 - REACH, REACH),
                    upright(ends[3 + a : 4 + a, :], 0, 64),
                    upright(below[base + 3 + a : base + 4 + a, :], 0, REACH),
                ],
                axis=0,
            )
            edge[a] = column
            top, bottom = halves(jnp.where(lane_ids(176) == 64, column, whole))
        to_right = jnp.where(low, bottom, top)
        at = slice(88 * a, 88 * (a + 1))
        swap[at, :] = jnp.where(first_core, to_right, to_left)
        side[at, :] = jnp.where(first_core, to_left, to_right)
    for ref in (swap, side):
        ref[88 * FIELDS : 88 * FIELDS + 8, :] = above[base:, :]
        ref[88 * FIELDS + 8 :, :] = ends[...]


def local_down(level, field, base, work, maps, next_base, next_maps, first_rows, rest_rows, next_rows):
    width = 2**level
    low, high, size = first_rows
    stencil("first", field, base, base, maps, low, high, size, width)
    low, high, size = rest_rows
    stencil("scaled_difference", work, field, base, maps, low, high, size, width)
    if next_base is None:
        return

    low, high, size = next_rows

    def body(start, size):
        at = pl.ds(start, size)
        for h in range(2):
            inverse = 0.25 * next_maps[INVERSE, h, at, :]
            for c in range(CHANNELS):
                even, odd = even_odd(work, (c, h), 2 * start - PAD, size)
                next_base[c, h, at, :] = pair_sum(even + odd, width) * inverse

    chunks(low, high, STEP_R, body)


def own_row(x):
    count = x.shape[0] // 8
    spread = picked(x, 8 * (lane_ids(x.shape[0]) & 15))
    rows = []
    keep = (lane_ids(8) >> 4) == lax.broadcasted_iota(jnp.int32, (8, LANES), 0)
    for i in range(count):
        part = jnp.where(keep, spread[8 * i : 8 * i + 8], 0.0)
        rows.append(jnp.sum(part, axis=0, keepdims=True))
    return rows


def repeat(rows, message):
    block = jnp.concatenate(rows * (24 // len(rows)), axis=0)
    for i in range(message.shape[0] // 24):
        message[24 * i : 24 * i + 24, :] = block


def down_levels(fields, bases, work, maps, ranges):
    for level in range(3):
        local_down(
            level,
            fields[level],
            bases[level],
            work[level],
            maps[level],
            bases[level + 1] if level < 2 else None,
            maps[level + 1] if level < 2 else None,
            *ranges[level],
        )
    tiles = []
    for c in range(CHANNELS):
        even, odd = even_odd(work[2], (c, 0), PAD + 16, 8)
        tiles.append(0.25 * pair_sum(even + odd, 4))
    return tiles


FIRST_DOWN = (
    ((8, 184, 176), (8, 184, 176), (0, 96, 96)),
    ((0, 96, 96), (8, 88, 80), (0, 48, 48)),
    ((0, 48, 48), (16, 32, 16), None),
)
LATER_DOWN = (
    ((32, 160, 128), (40, 152, 112), (16, 80, 64)),
    ((16, 80, 64), (16, 80, 64), (8, 40, 32)),
    ((8, 40, 32), (16, 32, 16), None),
)
FIRST_UP = ((32, 160, 128), (16, 80, 64), (0, 48, 48))
LATER_UP = ((56, 136, 80), (24, 72, 48), (8, 40, 32))
FIRST_SPANS = ((16, 80, 64), (0, 48, 48))
LATER_SPANS = ((24, 72, 48), (8, 40, 32))


def clear(ref, *bounds):
    for index in range(ref.shape[0]):
        for h in range(ref.shape[1]):
            for low, high in bounds:
                ref[index, h, low:high, :] = jnp.zeros((high - low, LANES), F32)


def setup_kernel(
    own, ends, above, below, swapped, sided, border,
    m0, m1, m2, source, f0, g1, f1, g2, f2, message,
    cells, raw0, raw1, raw2, w0, w1, w2,
):
    row_at, col_at, core = whereabouts()
    first_core = core == 0
    rows_of = lambda n, low: low + lax.broadcasted_iota(jnp.int32, (n, LANES), 0)
    edge = jnp.zeros((16, LANES), F32)
    not_top, not_bottom = row_at > 0, row_at < 7
    low = lane_ids(88) < 64
    inside = (low & (col_at < 31)) | (~low & (col_at > 0))

    def sides(start, size):
        one, two = swapped[start : start + size, :], sided[start : start + size, :]
        return jnp.where(first_core, one, two), jnp.where(first_core, two, one)

    for a in range(FIELDS):
        at = slice(REACH * a, REACH * (a + 1))
        for h in range(2):
            cells[a, h, 0:16, :] = edge
            cells[a, h, 192:208, :] = edge
        cells[a, 0, 16:72, :] = jnp.where(not_top, above[at, :], 0.0)
        cells[a, 0, 72:136, :] = own[a]
        cells[a, 0, 136:192, :] = jnp.where(not_bottom, below[at, :], 0.0)
        from_right, from_left = sides(88 * a, 88)
        top = jnp.where(low, from_right, from_left)
        bottom = pltpu.roll(jnp.where(low, from_left, from_right), 64, 1)
        cells[a, 1, 16:104, :] = jnp.where(inside & (not_top | (rows_of(88, 8) >= 64)), top, 0.0)
        cells[a, 1, 104:192, :] = jnp.where(
            inside & (not_bottom | (rows_of(88, 96) < 128)), bottom, 0.0
        )
    def fine(start, size):
        at = pl.ds(start, size)
        up_at, down_at = pl.ds(start - 1, size), pl.ds(start + 1, size)
        weights = [cells[WEIGHT, h, at, :] for h in range(2)]
        labels = [cells[LABEL, h, at, :] for h in range(2)]
        weight_sides = beside(weights, 1)
        label_sides = beside(labels, 1)
        coef, shares = [], []
        for h in range(2):
            near_weights = (
                cells[WEIGHT, h, up_at, :], cells[WEIGHT, h, down_at, :], weight_sides[0][h], weight_sides[1][h],
            )
            near_labels = (
                cells[LABEL, h, up_at, :], cells[LABEL, h, down_at, :], label_sides[0][h], label_sides[1][h],
            )
            raw = []
            for m in range(4):
                matching = jnp.where(near_labels[m] == labels[h], 1.0 / 64.0, SEAM_FACTOR / 64.0)
                value = (weights[h] + near_weights[m]) * matching
                value = jnp.where(weights[h] > 0.0, value, 0.0)
                raw.append(value)
                raw0[m, h, at, :] = value
            scaled, scale, share = scaled_maps(raw, 1.0)
            shares.append(share)
            for m in range(4):
                m0[m, h, at, :] = scaled[m]
            m0[SCALE, h, at, :] = scale
            coef.append(scaled)
        for c in range(CHANNELS):
            part = [cells[c, h, at, :] for h in range(2)]
            own_end = border[c, start - PAD - 8 : start - PAD - 8 + size, :]
            left_end = pltpu.roll(part[1], 64, 1), pltpu.roll(part[1], 63, 1)
            first, last = lane_ids(size) == 0, lane_ids(size) == LANES - 1
            flux = jnp.where(first, coef[0][LEFT] * left_end[0], 0.0)
            flux = flux - jnp.where(last, coef[0][RIGHT] * own_end, 0.0)
            source[c, 0, at, :] = shares[0] * part[0] + flux
            flux = jnp.where(first, coef[1][LEFT] * own_end, 0.0)
            flux = flux - jnp.where(last, coef[1][RIGHT] * left_end[1], 0.0)
            source[c, 1, at, :] = shares[1] * part[1] + flux

    chunks(8, 184, STEP_F, fine)
    from_right, from_left = sides(88 * FIELDS, 16)
    beside_own = jnp.where(lane_ids(16) < 64, from_right, from_left)
    for first, upper in ((0, 71), (8, 135)):
        for c in range(CHANNELS):
            if first == 0:
                straight = above[FIELDS * REACH + c : FIELDS * REACH + c + 1, :]
            else:
                straight = ends[c : c + 1, :]
            for h, flow in ((0, straight), (1, beside_own[first + c : first + c + 1])):
                if first == 0:
                    flow = jnp.where(not_top, flow, 0.0)
                one, two = pl.ds(upper, 1), pl.ds(upper + 1, 1)
                source[c, h, one, :] = source[c, h, one, :] - m0[DOWN, h, one, :] * flow
                source[c, h, two, :] = source[c, h, two, :] + m0[UP, h, two, :] * flow

    def coarser(raw, width, start, size, h):
        parts = []
        for m in range(4):
            even, odd = even_odd(raw, (m, h), start, size)
            if m == UP:
                parts.append(0.5 * pair_sum(even, width))
            elif m == DOWN:
                parts.append(0.5 * pair_sum(odd, width))
            elif m == LEFT:
                parts.append(0.5 * low_of_pair(even + odd, width))
            else:
                parts.append(0.5 * high_of_pair(even + odd, width))
        return parts

    for level, fine_raw, raw, maps, rows in ((1, raw0, raw1, m1, 96), (2, raw1, raw2, m2, 48)):

        def coarse(start, size, level=level, fine_raw=fine_raw, raw=raw, maps=maps):
            at = pl.ds(start, size)
            for h in range(2):
                parts = coarser(fine_raw, 2 ** (level - 1), 2 * start - PAD, size, h)
                scaled, scale, inverse = scaled_maps(parts, 0.5**level)
                for m in range(4):
                    raw[m, h, at, :] = parts[m]
                    maps[m, h, at, :] = scaled[m]
                maps[SCALE, h, at, :] = scale
                maps[INVERSE, h, at, :] = inverse

        chunks(0, rows, STEP_C, coarse)
    tiles = down_levels((f0, f1, f2), (source, g1, g2), (w0, w1, w2), (m0, m1, m2), FIRST_DOWN)
    upward, downward, leftward, rightward = coarser(raw2, 4, PAD + 16, 8, 0)
    row = lax.broadcasted_iota(jnp.int32, (8, LANES), 0)
    cell = lane_ids(8) >> 3
    turned = pltpu.roll(pltpu.roll(rightward, LANES - 8, 1), 7, 0)
    ends = jnp.where(row == 7, downward, jnp.where(cell == 15, rightward, turned))
    repeat(own_row(jnp.concatenate(tiles + [upward, leftward, ends], axis=0)), message)


def unpack(place, mine, other, count, stride, ordered, put):
    core = place[2]
    for f in range(count):
        for z in range(8):
            at = pl.ds(f + stride * z, 16, stride=8 * stride)
            own, theirs = mine[at, :], other[at, :]
            ordered[f, pl.ds(32 * z, 16, stride=2), :] = jnp.where(core == 0, own, theirs)
            ordered[f, pl.ds(32 * z + 1, 16, stride=2), :] = jnp.where(core == 0, theirs, own)
    sub = lax.broadcasted_iota(jnp.int32, (8, LANES), 0)
    part, cell = lane_ids(8) >> 4, lane_ids(8) & 15
    first = (((sub - part) & 7) << 4) + cell
    last = (((part - sub) & 7) << 4) + cell
    for z in range(8):
        for f in range(count):
            for group in range(4):
                x = picked(ordered[f, pl.ds(z * 32 + 8 * group, 8), :], first)
                for k in (1, 2, 4):
                    x = jnp.where((part & k) != 0, pltpu.roll(x, 8 - k, 0), x)
                put(f, PAD + 8 * z, group, picked(x, last))


def folded(halves, kind):
    lane = lane_ids(halves[0].shape[0])
    even = (2 * lane) & (LANES - 1)

    def one(x):
        if kind == "low":
            return picked(x, even)
        if kind == "high":
            return picked(x, even + 1)
        return picked(x, even) + picked(x, even + 1)

    parts = [one(x) for x in halves]
    if len(parts) == 1:
        parts.append(jnp.zeros_like(parts[0]))
    return [jnp.where(lane < 64, parts[i], parts[i + 1]) for i in range(0, len(parts), 2)]


def doubled(x):
    lane = lane_ids(x.shape[0])
    return [picked(x, lane >> 1), picked(x, 64 + (lane >> 1))]


WHOLE = {3: (4, 64, 1), 4: (2, 32, 0), 5: (1, 16, 0), 6: (1, 8, 0)}


def whole_maps(level, raw, maps):
    halves, rows, first = WHOLE[level]

    def body(start, size):
        at = pl.ds(start, size)
        lane = lane_ids(size)
        for i in range(halves):
            scaled, scale, inverse = scaled_maps(
                [raw[m, first + i, at, :] for m in range(4)], 0.5**level
            )
            breadth = 64 if level == 6 else LANES
            if i == 0:
                scaled[LEFT] = jnp.where((lane & (breadth - 1)) == 0, 0.0, scaled[LEFT])
            if i == halves - 1:
                at_last = (lane & (breadth - 1)) == breadth - 1
                scaled[RIGHT] = jnp.where(at_last, 0.0, scaled[RIGHT])
            for m in range(4):
                maps[m, first + i, at, :] = scaled[m]
            maps[SCALE, first + i, at, :] = scale
            maps[INVERSE, first + i, at, :] = inverse

    chunks(0, rows, STEP_W, body)


def coarsen_whole(level, raw, next_raw):
    halves, rows, first = WHOLE[level]
    next_halves, next_rows, next_first = WHOLE[level + 1]
    for m in range(4):
        parts = []
        for h in range(halves):
            even, odd = even_odd(raw, (m, first + h), PAD, next_rows)
            parts.append(even if m == UP else odd if m == DOWN else even + odd)
        kind = "sum" if m in (UP, DOWN) else "low" if m == LEFT else "high"
        if level == 5:
            parts = parts * 2
        for h, x in enumerate(folded(parts, kind)):
            next_raw[m, next_first + h, PAD : PAD + next_rows, :] = 0.5 * x


def one_sweep(maps):
    coef = [maps[m, 0, PAD : PAD + 8, :] for m in range(4)]
    row = lax.broadcasted_iota(jnp.int32, (8, LANES), 0)
    coef[UP] = jnp.where(row == 0, 0.0, coef[UP])
    coef[DOWN] = jnp.where(row == 7, 0.0, coef[DOWN])
    steps = ((-1, 0), (1, 0), (0, -1), (0, 1))
    return dict(zip(steps, coef))


def moved(x, rows, columns):
    if rows:
        x = pltpu.roll(x, (-rows) % 8, 0)
    if columns:
        x = pltpu.roll(x, (-columns) % LANES, 1)
    return x


DIAMOND = [(a, b) for a in range(-4, 5) for b in range(-4, 5) if abs(a) + abs(b) <= 4]


def four_sweeps(maps, product):
    sweep = one_sweep(maps)
    whole = dict(sweep)
    whole[0, 0] = jnp.full((8, LANES), 1.0 - RELAX_WEIGHT, F32)
    for _ in range(3):
        grown = {at: (1.0 - RELAX_WEIGHT) * x for at, x in whole.items()}
        for step, coef in sweep.items():
            for at, x in whole.items():
                place = (at[0] + step[0], at[1] + step[1])
                term = coef * moved(x, *step)
                grown[place] = grown[place] + term if place in grown else term
        whole = grown
    for i, at in enumerate(DIAMOND):
        product[i] = moved(whole[at], -at[0], 0)


def coarse_solve(base, maps, product):
    sweep = one_sweep(maps)
    right_side = [base[i, 0, PAD : PAD + 8, :] for i in range(2)]
    first = right_side
    for _ in range(3):
        first = [
            (1.0 - RELAX_WEIGHT) * v + g + sum(coef * moved(v, *at) for at, coef in sweep.items())
            for v, g in zip(first, right_side)
        ]
    values = first
    for _ in range(COARSE_SWEEPS // 4 - 1):
        lanes = [[moved(v, 0, b) for b in range(-4, 5)] for v in values]
        totals = [list() for _ in values]
        for a in range(-4, 5):
            sums = [None] * len(values)
            for i, at in enumerate(DIAMOND):
                if at[0] == a:
                    coef = product[i]
                    for c in range(len(values)):
                        term = coef * lanes[c][at[1] + 4]
                        sums[c] = term if sums[c] is None else sums[c] + term
            for c in range(len(values)):
                totals[c].append(moved(sums[c], a, 0))
        values = []
        for c in range(len(first)):
            t = totals[c]
            even = (t[0] + t[1]) + (t[2] + t[3])
            odd = (t[5] + t[6]) + (t[7] + t[8])
            values.append((first[c] + t[4]) + (even + odd))
    return values


def whole_cycle(level, bases, fields, others, maps, product):
    halves, rows, first = WHOLE[level]
    base, field, other, level_maps = bases[level], fields[level], others[level], maps[level]
    size = rows
    stencil("first", field, base, base, level_maps, 0, rows, size, 1, halves, first)
    stencil("residual", other, field, base, level_maps, 0, rows, size, 1, halves, first)
    next_halves, next_rows, next_first = WHOLE[level + 1]
    summed = []
    for h in range(halves):
        parts = []
        for c in range(CHANNELS):
            even, odd = even_odd(other, (c, first + h), PAD, next_rows)
            parts.append(even + odd)
        summed.append(jnp.concatenate(parts, axis=0))
    if level == 5:
        parts = [summed[0][c * next_rows : (c + 1) * next_rows] for c in range(CHANNELS)]
        inverse = 0.25 * maps[6][INVERSE, 0, PAD : PAD + next_rows, :]
        for i, group in enumerate((parts[:2], parts[2:])):
            bases[6][i, 0, PAD : PAD + next_rows, :] = folded(group, "sum")[0] * inverse
        summed = []
    for h, x in enumerate(folded(summed, "sum") if summed else []):
        inverse = 0.25 * maps[level + 1][INVERSE, next_first + h, PAD : PAD + next_rows, :]
        for c in range(CHANNELS):
            part = x[c * next_rows : (c + 1) * next_rows]
            bases[level + 1][c, next_first + h, PAD : PAD + next_rows, :] = part * inverse
    if level == 5:
        both, third = coarse_solve(bases[6], maps[6], product)
        coarse = [None]
    else:
        whole_cycle(level + 1, bases, fields, others, maps, product)
        coarse = [
            jnp.concatenate(
                [
                    fields[level + 1][c, next_first + h, PAD : PAD + next_rows, :]
                    for c in range(CHANNELS)
                ],
                axis=0,
            )
            for h in range(next_halves)
        ]
    for m, x in enumerate(coarse):
        if x is None:
            wide = [jnp.concatenate(doubled(both) + doubled(third)[:1], axis=0)]
        else:
            wide = doubled(x)
        for i in range(min(halves, 2)):
            h = first + 2 * m + i
            for c in range(CHANNELS):
                part = wide[i][c * next_rows : (c + 1) * next_rows]
                for offset in range(2):
                    at = pl.ds(PAD + offset, next_rows, stride=2)
                    field[c, h, at, :] = field[c, h, at, :] + part
    if level > 3:
        stencil("relax", other, field, base, level_maps, 0, rows, size, 1, halves, first)
        stencil("relax", field, other, base, level_maps, 0, rows, size, 1, halves, first)


def window(ref, index, place):
    group = lax.shift_right_logical(place[1], 3)
    offset = 16 * (place[1] & 7)
    at = pl.ds(pl.multiple_of(8 * place[0], 8), 24)
    lane = lane_ids(24)
    turn = lax.rem(LANES - offset, LANES)
    before, here, after = [pltpu.roll(ref[index, group + i, at, :], turn, 1) for i in range(3)]
    low = lane < 64
    fits = lane + offset < LANES
    return jnp.where(low, jnp.where(fits, here, after), jnp.where(fits, before, here))


def correct_level_two(
    place, bases, fields, maps, f2, target, near_maps, near_base, near_a, near_b
):
    if maps is not None:
        for m in range(4):
            near_maps[m, 0, PAD : PAD + 24, :] = window(maps[3], m, place)
    edge = jnp.zeros((PAD, LANES), F32)
    for c in range(CHANNELS):
        near_base[c, 0, PAD : PAD + 24, :] = window(bases[3], c, place)
        near_a[c, 0, PAD : PAD + 24, :] = window(fields[3], c, place)
        for ref in (near_a, near_b):
            ref[c, 0, 0:PAD, :] = edge
            ref[c, 0, PAD + 24 : PAD + 32, :] = edge
    stencil("relax", near_b, near_a, near_base, near_maps, 0, 24, 24, 1, 1)
    stencil("relax", near_a, near_b, near_base, near_maps, 0, 24, 24, 1, 1)
    flat = jnp.concatenate([near_a[c, 0, PAD : PAD + 24, :] for c in range(CHANNELS)], axis=0)
    lane = lane_ids(flat.shape[0])
    wide = [picked(flat, lane >> 3), picked(flat, jnp.where(lane < 64, 16, 112) + (lane >> 3))]
    for c in range(CHANNELS):
        for h in range(2):
            part = wide[h][24 * c : 24 * c + 24]
            for offset in range(2):
                at = pl.ds(PAD + offset, 24, stride=2)
                target[c, h, at, :] = f2[c, h, at, :] + part


def add_rows(target, field, coarse, low, high, size):
    def body(start, size):
        for c in range(CHANNELS):
            for h in range(2):
                part = coarse[c, h, pl.ds(start, size), :]
                for offset in range(2):
                    at = pl.ds(2 * start - PAD + offset, size, stride=2)
                    target[c, h, at, :] = field[c, h, at, :] + part

    chunks(low, high, STEP_A, body)


def up_levels(ranges, spans, before, fields, bases, works, maps, extra):
    low, high, size = ranges[2]
    stencil("relax", works[2], fields[2], bases[2], maps[2], low, high, size, 4)
    stencil("relax", fields[2], works[2], bases[2], maps[2], low, high, size, 4)
    add_rows(fields[1], before[1], fields[2], *spans[1])
    low, high, size = ranges[1]
    stencil("relax", works[1], fields[1], bases[1], maps[1], low, high, size, 2)
    stencil("relax", fields[1], works[1], bases[1], maps[1], low, high, size, 2)
    add_rows(fields[0], before[0], fields[1], *spans[0])
    low, high, size = ranges[0]
    stencil("relax", works[0], fields[0], bases[0], maps[0], low, high, size, 1)
    if extra is None:
        stencil("relax", fields[0], works[0], bases[0], maps[0], low, high, size, 1)
    else:
        stencil(
            "relax_add", fields[0], works[0], bases[0], maps[0], low, high, size, 1, extra=extra
        )


def complete_maps(raw):
    size = 64
    at = pl.ds(PAD, size)
    lane = lane_ids(size)
    row = lax.broadcasted_iota(jnp.int32, (size, LANES), 0)
    ends = [raw[RIGHT, h, at, :] for h in range(1, 5)]
    shifted = beside([raw[LEFT, h, at, :] for h in range(1, 5)], 1)[1]
    last = ends[3]
    last = jnp.where((row & 7) == 7, pltpu.roll(pltpu.roll(last, 1, 1), 1, 0), last)
    shifted[3] = jnp.where(lane == LANES - 1, last, shifted[3])
    for i in range(4):
        below = raw[UP, 1 + i, pl.ds(PAD + 1, size), :]
        raw[DOWN, 1 + i, at, :] = jnp.where(row == size - 1, ends[i], below)
        raw[RIGHT, 1 + i, at, :] = shifted[i]


def middle_kernel(
    mine, other, m0, m1, m2, source, f0, g1, f1, g2, f2,
    m3, m4, m5, m6, product, near_maps, solution, n0, h0, k1, h1, k2, h2, message,
    ordered, raw3, raw4, raw5, raw6, b3, v3, o3, b4, v4, o4, b5, v5, o5, b6,
    w0, w1, w2, near_base, near_a, near_b,
):
    place = whereabouts()
    for ref in (m3, b3, v3):
        rows = ref.shape[2]
        clear(ref, (0, PAD), (rows - PAD, rows))
        for index in range(ref.shape[0]):
            for h in (0, 5):
                ref[index, h] = jnp.zeros((rows, LANES), F32)
    for ref in (b4, v4, o4, b5, v5, o5):
        rows = ref.shape[2]
        clear(ref, (0, PAD), (rows - PAD, rows))

    def put(f, start, group, tile):
        if f < CHANNELS:
            b3[f, 1 + group, pl.ds(start, 8), :] = tile
        else:
            slot = (UP, LEFT, RIGHT)[f - CHANNELS]
            raw3[slot, 1 + group, pl.ds(start, 8), :] = tile

    unpack(place, mine, other, 6, 6, ordered, put)
    complete_maps(raw3)
    raws = {3: raw3, 4: raw4, 5: raw5, 6: raw6}
    maps = {3: m3, 4: m4, 5: m5, 6: m6}
    whole_maps(3, raw3, m3)
    for level in (3, 4, 5):
        coarsen_whole(level, raws[level], raws[level + 1])
        whole_maps(level + 1, raws[level + 1], maps[level + 1])
    four_sweeps(m6, product)
    scale_base(b3, m3)
    whole_cycle(
        3, {3: b3, 4: b4, 5: b5, 6: b6}, {3: v3, 4: v4, 5: v5}, {3: o3, 4: o4, 5: o5}, maps,
        product,
    )
    correct_level_two(
        place, {3: b3}, {3: v3}, maps, f2, h2, near_maps, near_base, near_a, near_b
    )
    local_maps = (m0, m1, m2)
    up_levels(
        FIRST_UP, FIRST_SPANS, (f0, f1), (solution, h1, h2), (source, g1, g2), (w0, w1, w2), local_maps, None,
    )
    stencil("difference", n0, solution, source, m0, 32, 160, 128, 1)
    tiles = down_levels((h0, h1, h2), (n0, k1, k2), (w0, w1, w2), local_maps, LATER_DOWN)
    repeat(own_row(jnp.concatenate(tiles, axis=0)), message)


def scale_base(base, maps):
    halves, rows, first = WHOLE[3]

    def body(start, size):
        at = pl.ds(start, size)
        for i in range(halves):
            inverse = maps[INVERSE, first + i, at, :]
            for c in range(CHANNELS):
                base[c, first + i, at, :] = base[c, first + i, at, :] * inverse

    chunks(0, rows, STEP_W, body)


def last_kernel(
    mine, other, m0, m1, m2, source, m3, m4, m5, m6, product, near_maps, before, n0, f0, k1, f1, k2, f2,
    solution, residual,
    ordered, b3, v3, o3, b4, v4, o4, b5, v5, o5, b6,
    h0, h1, h2, w0, w1, w2, near_base, near_a, near_b, left,
):
    place = whereabouts()
    for ref in (b3, v3):
        rows = ref.shape[2]
        clear(ref, (0, PAD), (rows - PAD, rows))
        for index in range(ref.shape[0]):
            for h in (0, 5):
                ref[index, h] = jnp.zeros((rows, LANES), F32)
    for ref in (b4, v4, o4, b5, v5, o5):
        rows = ref.shape[2]
        clear(ref, (0, PAD), (rows - PAD, rows))

    def put(f, start, group, tile):
        b3[f, 1 + group, pl.ds(start, 8), :] = tile

    unpack(place, mine, other, CHANNELS, CHANNELS, ordered, put)
    maps = {3: m3, 4: m4, 5: m5, 6: m6}
    scale_base(b3, m3)
    whole_cycle(
        3, {3: b3, 4: b4, 5: b5, 6: b6}, {3: v3, 4: v4, 5: v5}, {3: o3, 4: o4, 5: o5}, maps,
        product,
    )
    correct_level_two(
        place, {3: b3}, {3: v3}, None, f2, h2, near_maps, near_base, near_a, near_b
    )
    local_maps = (m0, m1, m2)
    up_levels(
        LATER_UP, LATER_SPANS, (f0, f1), (h0, h1, h2), (n0, k1, k2), (w0, w1, w2), local_maps, before,
    )
    own = pl.ds(PAD + 64, 64)
    copies = [
        pltpu.make_async_copy(field.at[:, 0, own, :], target, left.at[i])
        for i, (field, target) in enumerate(((h0, solution), (w0, residual)))
    ]
    copies[0].start()
    stencil("final", w0, h0, source, m0, 64, 128, 64, 1)
    copies[1].start()
    for copy in copies:
        copy.wait()


def shape(*dims):
    return jax.ShapeDtypeStruct(dims, F32)


def field_shape(level, count):
    return (count, 2, LOCAL_ROWS[level] + 2 * PAD, LANES)


def whole_shape(level, count):
    halves, rows, first = WHOLE[level]
    return (count, halves + 2 * first, rows + 2 * PAD, LANES)


def call(kernel, outs, scratch, *args, out_space=pltpu.VMEM, semaphores=()):
    in_specs = [pl.BlockSpec(memory_space=pltpu.VMEM) for _ in args]
    return pl.pallas_call(
        kernel,
        out_shape=[shape(*o) for o in outs],
        in_specs=in_specs,
        out_specs=[pl.BlockSpec(memory_space=out_space) for _ in outs],
        scratch_shapes=[pltpu.VMEM(s, F32) for s in scratch] + list(semaphores),
        compiler_params=pltpu.CompilerParams(vmem_limit_bytes=14 * 1024 * 1024),
        cost_estimate=pl.CostEstimate(flops=0, bytes_accessed=8_000_000, transcendentals=0),
    )(*args)


def ring(count, step):
    return [(i, (i + step) % count) for i in range(count)]


def gathered(message):
    mine = lax.all_to_all(message.reshape(128, 1, -1), CHIPS, 0, 0, tiled=True)
    mine = mine.reshape(message.shape)
    return mine, lax.ppermute(mine, "core", ring(2, 1))


def local(guidance, seam_weight, source_label):
    down, up = pl.pallas_call(
        stack_kernel,
        out_shape=[pltpu.VMEM((UPDOWN_ROWS, LANES), F32)] * 2,
        in_specs=[pl.BlockSpec(memory_space=pltpu.HBM)] * 3,
        out_specs=[pl.BlockSpec(memory_space=pltpu.VMEM)] * 2,
        scratch_shapes=[
            pltpu.VMEM((2, CHANNELS, 64, LANES), F32),
            pltpu.VMEM((64, LANES), jnp.int32),
            pltpu.VMEM((64, LANES), jnp.int32),
            pltpu.SemaphoreType.DMA((3,)),
        ],
        compiler_params=pltpu.CompilerParams(vmem_limit_bytes=58 * 1024 * 1024),
    )(guidance, seam_weight, source_label)
    above = lax.ppermute(down, "z", ring(8, 1))
    below = lax.ppermute(up, "z", ring(8, -1))
    own, ends = call(own_kernel, [(FIELDS, 64, LANES), (8, LANES)], [], down, up)
    swap, side, border = call(
        pack_kernel,
        [(SIDE_ROWS, LANES)] * 2 + [(CHANNELS, 176, LANES)],
        [],
        own, ends, above, below,
    )
    swapped = lax.ppermute(swap, "core", ring(2, 1))
    pairs = [(i, min(max(i + 2 * (i % 2) - 1, 0), 31)) for i in range(32)]
    sided = lax.ppermute(side, SIDES, pairs)
    fields = [field_shape(level, CHANNELS) for level in range(3)]
    maps = [field_shape(0, 5), field_shape(1, 6), field_shape(2, 6)]
    raws = [field_shape(level, 4) for level in range(3)]
    m0, m1, m2, source, f0, g1, f1, g2, f2, message = call(
        setup_kernel,
        maps + [fields[0], fields[0], fields[1], fields[1], fields[2], fields[2], (6 * 128, LANES)],
        [field_shape(0, FIELDS)] + raws + fields,
        own, ends, above, below, swapped, sided, border,
    )
    mine, other = gathered(message)
    wholes = [whole_shape(level, CHANNELS) for level in (3, 4, 5) for _ in range(3)]
    wholes = wholes + [whole_shape(6, CHANNELS)]
    near = [(CHANNELS, 1, 40, LANES)] * 3
    m3, m4, m5, m6, product, near_maps, solution, n0, h0, k1, h1, k2, h2, message = call(
        middle_kernel,
        [whole_shape(level, 6) for level in (3, 4, 5, 6)]
        + [(len(DIAMOND), 8, LANES), (4, 1, 40, LANES)] + [fields[0]] * 3 + [fields[1]] * 2 + [fields[2]] * 2 + [(CHANNELS * 128, LANES)],
        [(6, 256, LANES)] + [whole_shape(level, 4) for level in (3, 4, 5, 6)]
        + wholes + fields + near,
        mine, other, m0, m1, m2, source, f0, g1, f1, g2, f2,
    )
    mine, other = gathered(message)
    outs = call(
        last_kernel,
        [(CHANNELS, 64, LANES)] * 2,
        [(CHANNELS, 256, LANES)] + wholes + fields + fields + near,
        mine, other, m0, m1, m2, source, m3, m4, m5, m6, product, near_maps,
        solution, n0, h0, k1, h1, k2, h2,
        out_space=pltpu.HBM, semaphores=[pltpu.SemaphoreType.DMA((2,))],
    )
    return tuple(outs)


def solution(mesh):
    fine = Mesh(mesh.devices.reshape(8, 4, 4, 2), ("z", "y", "x", "core"))
    return jax.shard_map(
        local,
        mesh=fine,
        in_specs=(P(None, None, "z", SIDES), P("z", SIDES), P("z", SIDES)),
        out_specs=(P(None, "z", SIDES), P(None, "z", SIDES)),
        check_vma=False,
    )
```
